512 devices in a mesh: seq: 32 (over x, y, core), exp: 16 (over z).
Axes of the slice: x: 4, y: 4, z: 16, core: 2. Of those that a mesh axis runs over, the one named last changes fastest.
Arguments:
- encoded: bfloat16 [16, 512, 5120], P('exp', 'seq'), may hold values from -6 to 6
- key_weight: bfloat16 [2, 5120, 4096], P(None, 'exp', 'seq'), may hold values from -0.078125 to 0.078125
- value_weight: bfloat16 [2, 5120, 4096], P(None, 'exp', 'seq'), may hold values from -0.078125 to 0.078125
- queries: bfloat16 [16, 8, 4096], P('exp', None, 'seq'), may hold values from -8 to 8
- state: bfloat16 [16, 8, 5120], P('exp'), may hold values from -4 to 4
- out_weight: bfloat16 [4096, 5120], P('seq'), may hold values from -0.25 to 0.25
- norm_gain: float32 [5120], replicated, may hold values from 0.25 to 1.75
- router: bfloat16 [5120, 4], replicated, may hold values from -0.15625 to 0.15625
- expert_ids: int32 [16, 8, 2], P('exp'), may hold values from 0 to 3, all different within a row; in each aligned block of 8 rows (0 to 7, 8 to 15, ..., all dimensions but the last counted through in order) at most 6 rows name the same one
- gate_weight: bfloat16 [16, 1280, 10240], P('exp', None, 'seq'), may hold values from -0.078125 to 0.078125
- up_weight: bfloat16 [16, 1280, 10240], P('exp', None, 'seq'), may hold values from -0.078125 to 0.078125
- down_weight: bfloat16 [16, 10240, 1280], P('exp', 'seq'), may hold values from -0.125 to 0.125
Outputs:
- key_cache: bfloat16 [2, 16, 512, 4096], P(None, 'exp', None, 'seq')
- value_cache: bfloat16 [2, 16, 512, 4096], P(None, 'exp', None, 'seq')
- mixed_rows: bfloat16 [16, 8, 5120], P('exp')
The draws below stay inside these ranges and needn't reach their ends.
Inputs may be any that keep to these rules, and one draw needn't show every extreme that they name: `expert_ids`: among the rows of one document no expert is named more than 6 times, and some expert reaches 6.
All inputs are finite; a program needn't handle non-finite values.
Results may differ from the reference program's by a relative error of at most 0.02.
Values may be sent and summed in bfloat16 or wider, within the bound.
No kernel may reach another device: no remote copies, remote signals or barrier semaphores. Data moves between devices by JAX's collectives and lax.ppermute only.
A program may use at most 64 MiB of HBM per device.

```python
import math
import jax
import jax.numpy as jnp
import numpy as np
from jax import lax

D = 5120
DH = 128
FF = 10240
EXPERTS = 4
TOP = 2
NL = 2
DEC_DEV = 8
CAP = 6
HEADS = 32
GROUP = 4
ENC_LEN = 512
DOCS = 16


def block_scale(rng, shape, split, smallest, top_value):
    gain, own = 1.0, jax.random.fold_in(rng, 6)
    for dim, blocks in split:
        draws = jnp.exp(jax.random.uniform(jax.random.fold_in(own, dim), (blocks,), jnp.float32, smallest / len(split), top_value / len(split)))
        gain = gain * jnp.repeat(draws, shape[dim] // blocks).reshape([-1 if axis == dim else 1 for axis in range(len(shape))])
    return gain


def deal_out(key, own, number, rows, count, top, bound, skew):
    order = jax.random.permutation(key, count)
    heavy_load, usual = portions_of(count, rows * top, bound, skew, True), portions_of(count, rows * top, bound, skew, False)
    places = jnp.arange(count)

    def named(lengths, offset_by):
        used = int((lengths > 0).sum())
        fixed = max(1, used // 4)
        passed = fixed + (places - fixed + offset_by * (used - fixed)) % max(1, count - fixed)
        return jnp.zeros((count,), jnp.int32).at[order[jnp.where(places < fixed, places, passed)]].set(jnp.asarray(lengths, jnp.int32))

    lengths = jnp.where(number % 4 == 0, named(heavy_load, number // 4), named(usual, number - number // 4 - 1))
    mixed = jax.random.permutation(jax.random.fold_in(own, 3), count)
    giver, taker = mixed[0:count // 2 * 2:2], mixed[1:count // 2 * 2:2]
    slack = jnp.minimum(lengths[giver] - 1, bound - lengths[taker]) // 2
    slack = jnp.where((giver == order[0]) | (taker == order[0]) | (lengths[taker] == 0), 0, jnp.maximum(slack, 0))
    passed = jax.random.randint(jax.random.fold_in(own, 4), (count // 2,), 0, 1 << 20) % (slack + 1)
    lengths = lengths.at[giver].add(-passed).at[taker].add(passed)
    items = jnp.searchsorted(jnp.cumsum(lengths), jnp.arange(rows * top), side="right").astype(jnp.int32)
    table = items.reshape(top, rows).T
    table = table[jax.random.permutation(jax.random.fold_in(own, 1), rows)]
    offset_by = jax.random.randint(jax.random.fold_in(own, 2), (rows, 1), 0, top)
    return jnp.take_along_axis(table, (jnp.arange(top)[None, :] + offset_by) % top, axis=1)


def portions_of(number_of, total, reach, lean, full):
    weights = [(1 << 20) // math.isqrt(grade ** lean) + 1 for grade in range(1, number_of + 1)]
    largest = reach if full else min(reach, max(-(-total // number_of), total * weights[0] // sum(weights)))
    least = 1 if total - largest >= number_of - 1 else 0
    given, rest = [largest] + [least] * (number_of - 1), total - largest - least * (number_of - 1)
    while rest > 0:
        free = [i for i in range(1, number_of) if given[i] < largest] or [i for i in range(1, number_of) if given[i] < reach]
        mass, budget = sum([weights[i] for i in free]), rest
        for i in free:
            more = min(reach - given[i], max(1, budget * weights[i] // mass), rest)
            given[i] = given[i] + more
            rest = rest - more
    return np.array(given)


def noise(rng, extent, spread, reach, cuts=(), held_as=jnp.bfloat16):
    values = jax.random.normal(rng, extent, jnp.float32) * spread
    if len(cuts) > 0:
        values = block_scale(rng, extent, cuts, -0.22, 0.18) * values
    return jnp.clip(values, min=-reach, max=reach).astype(held_as)


def setup_inputs(seed: int = 0) -> dict:
    streams_of = jax.random.split(jax.random.key(seed), 13)
    encoded = noise(streams_of[0], (DOCS, ENC_LEN, D), 1.0, 6.0, ((0, 16), (1, 32)))
    key_weight = noise(streams_of[1], (NL, D, HEADS * DH), D ** -0.5, 0.078125, ((1, 16), (2, 32)))
    value_weight = noise(streams_of[2], (NL, D, HEADS * DH), D ** -0.5, 0.078125, ((1, 16), (2, 32)))
    queries = noise(streams_of[3], (DOCS, DEC_DEV, HEADS * DH), 2.0, 8.0, ((0, 16), (2, 32)))
    state = noise(streams_of[4], (DOCS, DEC_DEV, D), 0.5, 4.0, ((0, 16),))
    out_weight = noise(streams_of[5], (HEADS * DH, D), (DH * 4) ** -0.5, 0.25, ((0, 32),))
    norm_gain = jnp.clip(1.0 + 0.15 * jax.random.normal(streams_of[6], (D,), jnp.float32), 0.25, 1.75)
    router = noise(streams_of[7], (D, EXPERTS), (D // 4) ** -0.5, 0.15625)
    expert_ids_keys = jax.random.split(jax.random.fold_in(streams_of[8], 1), DOCS * DEC_DEV // DEC_DEV)
    expert_ids_turns = jax.random.permutation(jax.random.fold_in(streams_of[8], 3), DOCS * DEC_DEV // DEC_DEV)
    expert_ids = jax.vmap(lambda own, number: deal_out(jax.random.fold_in(streams_of[8], 2), own, number, DEC_DEV, EXPERTS, TOP, CAP, 2))(expert_ids_keys, expert_ids_turns).reshape((DOCS, DEC_DEV, TOP))
    gate_weight = noise(streams_of[9], (EXPERTS * GROUP, D // GROUP, FF), D ** -0.5, 0.078125, ((0, 16), (2, 32)))
    up_weight = noise(streams_of[10], (EXPERTS * GROUP, D // GROUP, FF), D ** -0.5, 0.078125, ((0, 16), (2, 32)))
    down_weight = noise(streams_of[11], (EXPERTS * GROUP, FF, D // GROUP), (FF // 4) ** -0.5, 0.125, ((0, 16), (1, 32)))
    return {"encoded": encoded, "key_weight": key_weight, "value_weight": value_weight, "queries": queries, "state": state, "out_weight": out_weight, "norm_gain": norm_gain, "router": router, "expert_ids": expert_ids, "gate_weight": gate_weight, "up_weight": up_weight, "down_weight": down_weight}


epsilon = 1e-06

def reference(encoded, key_weight, value_weight, queries, state, out_weight, norm_gain, router, expert_ids, gate_weight, up_weight, down_weight):
    flat_tokens = encoded.reshape(DOCS * ENC_LEN, D)

    def project_layer(weight_pair):
        key_part = jnp.dot(flat_tokens, weight_pair[0], preferred_element_type=jnp.float32).astype(jnp.bfloat16)
        value_part = jnp.dot(flat_tokens, weight_pair[1], preferred_element_type=jnp.float32).astype(jnp.bfloat16)
        return (key_part, value_part)
    key_flat, value_flat = lax.map(project_layer, (key_weight, value_weight))
    key_cache = key_flat.reshape(NL, DOCS, ENC_LEN, HEADS * DH)
    value_cache = value_flat.reshape(NL, DOCS, ENC_LEN, HEADS * DH)
    query_heads = queries.astype(jnp.float32).reshape(DOCS, DEC_DEV, HEADS, DH)
    keys_first = key_cache[0].astype(jnp.float32).reshape(DOCS, ENC_LEN, HEADS, DH)
    values_first = value_cache[0].astype(jnp.float32).reshape(DOCS, ENC_LEN, HEADS, DH)
    scores = jnp.einsum('brhd,bkhd->bhrk', query_heads, keys_first) / jnp.sqrt(jnp.float32(DH))
    attn = jax.nn.softmax(scores, axis=-1).astype(jnp.bfloat16)
    context = jnp.einsum('bhrk,bkhd->brhd', attn.astype(jnp.float32), values_first).astype(jnp.bfloat16)
    context = context.reshape(DOCS * DEC_DEV, HEADS * DH)
    attended = state.reshape(DOCS * DEC_DEV, D).astype(jnp.float32) + jnp.dot(context, out_weight, preferred_element_type=jnp.float32)
    mean_square = lax.optimization_barrier(jnp.mean(attended * attended, axis=1, keepdims=True))
    normed = (attended * lax.rsqrt(mean_square + epsilon) * norm_gain).astype(jnp.bfloat16)
    probs = jax.nn.softmax(jnp.dot(normed, router, preferred_element_type=jnp.float32), axis=-1)
    chosen = expert_ids.reshape(DOCS * DEC_DEV, TOP)
    onehot = (chosen[:, :, None] == jnp.arange(EXPERTS, dtype=jnp.int32)[None, None, :]).astype(jnp.float32)
    share_weight = lax.optimization_barrier(jnp.sum(onehot * probs[:, None, :], axis=2))
    expert_weight = lax.optimization_barrier(jnp.sum(onehot * share_weight[:, :, None], axis=1))
    gate_all = gate_weight.reshape(EXPERTS, D, FF)
    up_all = up_weight.reshape(EXPERTS, D, FF)
    down_all = down_weight.reshape(EXPERTS, GROUP, FF, D // GROUP).transpose(0, 2, 1, 3).reshape(EXPERTS, FF, D)

    def one_expert(total, items):
        gate_one, up_one, down_one, column = items
        gate_val = jnp.dot(normed, gate_one, preferred_element_type=jnp.float32)
        up_val = jnp.dot(normed, up_one, preferred_element_type=jnp.float32)
        hidden = (jax.nn.gelu(gate_val, approximate=True) * up_val).astype(jnp.bfloat16)
        output = jnp.dot(hidden, down_one, preferred_element_type=jnp.float32).astype(jnp.bfloat16)
        return (total + column[:, None] * output.astype(jnp.float32), None)
    combined, unused = lax.scan(one_expert, jnp.zeros((DOCS * DEC_DEV, D), jnp.float32), (gate_all, up_all, down_all, expert_weight.T))
    mixed_rows = (attended + combined).astype(jnp.bfloat16).reshape(DOCS, DEC_DEV, D)
    return (key_cache, value_cache, mixed_rows)
```

```python
import functools
import math

import jax
import jax.numpy as jnp
from jax import lax
from jax.experimental import pallas as pl
from jax.experimental.pallas import tpu as pltpu
from jax.sharding import Mesh
from jax.sharding import PartitionSpec as P

EPS = 1e-06
SEQ = ("x", "y", "c")
EXP = ("e", "g")
LANES = 128
BF = jnp.bfloat16
F32 = jnp.float32


def shifted(x, count, by):
    return lax.ppermute(x, EXP, [(i, (i + by) % count) for i in range(count)])


def exchanged(x, axes):
    return lax.all_to_all(x, axes, split_axis=0, concat_axis=0, tiled=True)


def spread(x, axes):
    count = lax.axis_size(axes)
    return exchanged(jnp.broadcast_to(x[None], (count,) + x.shape), axes)


def project(enc_ref, weight_ref, acc_ref, key_ref, value_ref):
    width = key_ref.shape[-1]
    depth = weight_ref.shape[0]
    step = 512
    acc_ref[...] = jnp.zeros_like(acc_ref)

    @pl.loop(0, depth // step)
    def _(k):
        at = pl.multiple_of(k * step, step)
        acc_ref[...] += jnp.dot(
            enc_ref[:, pl.ds(at, step)],
            weight_ref[pl.ds(at, step), :],
            preferred_element_type=F32,
        )

    key_ref[0] = acc_ref[:, :width].astype(BF)
    value_ref[0] = acc_ref[:, width:].astype(BF)


def attention_kernel(offsets, count, tiles, groups, z_ref, *refs):
    blocks = refs[:count]
    enc_ref, query_ref, out_ref, key_ref, value_ref, term_ref, weight_ref, acc_ref = refs[count:]
    rows = blocks[0].shape[0]
    for block, offset in zip(blocks, offsets):
        place = lax.rem(z_ref[0] + (count + offset), count)
        weight_ref[pl.ds(pl.multiple_of(place * rows, 64), rows), :] = block[...]
    project(enc_ref, weight_ref, acc_ref, key_ref, value_ref)
    head = key_ref.shape[-1]
    scores = lax.dot_general(
        query_ref[...], key_ref[0], (((1,), (1,)), ((), ())), preferred_element_type=F32
    ) / math.sqrt(head)
    raised = jnp.exp(scores - jnp.max(scores, axis=-1, keepdims=True))
    attn = (raised / jnp.sum(raised, axis=-1, keepdims=True)).astype(BF)
    context = jnp.dot(attn, value_ref[0], preferred_element_type=F32).astype(BF)
    half = query_ref.shape[0] // 2
    for t in range(tiles):
        parts = [
            jnp.dot(
                context,
                out_ref[:, (g * tiles + t) * LANES : (g * tiles + t + 1) * LANES],
                preferred_element_type=F32,
            )
            for g in range(groups)
        ]
        for h in range(2):
            term_ref[2 * t + h] = jnp.concatenate(
                [p[h * half : (h + 1) * half] for p in parts], axis=0
            ).astype(BF)
    for s in range(2 * tiles, term_ref.shape[0]):
        term_ref[s] = jnp.zeros(term_ref.shape[1:], BF)


def second_kernel(enc_ref, weight_ref, key_in, value_in, key_ref, value_ref, acc_ref):
    project(enc_ref, weight_ref, acc_ref, key_ref, value_ref)


def per_device(
    encoded,
    key_weight,
    value_weight,
    queries,
    state,
    out_weight,
    norm_gain,
    router,
    expert_ids,
    gate_weight,
    up_weight,
    down_weight,
):
    seq_count = lax.axis_size(SEQ)
    exp_count = lax.axis_size(EXP)
    groups = lax.axis_size("g")
    experts = lax.axis_size("e")
    dec_rows = state.shape[1]
    half = dec_rows // 2
    model_width = state.shape[2]
    block_width = model_width // groups
    tiles = block_width // LANES
    tile_slots = seq_count // 2
    head = key_weight.shape[2]
    hidden_here = gate_weight.shape[2]
    tokens = encoded.shape[1] * seq_count
    z = lax.axis_index(EXP)
    my_tile = lax.axis_index(("x", "y"))
    my_half = lax.axis_index("c")
    my_expert = lax.axis_index("e")
    my_group = lax.axis_index("g")

    enc_all = lax.all_gather(encoded[0], SEQ, axis=0, tiled=True)
    first = jnp.concatenate([key_weight[0], value_weight[0]], axis=1)
    second = jnp.concatenate([key_weight[1], value_weight[1]], axis=1)
    blocks, offsets = [first], [0]
    up, down = first, first
    for k in range(1, exp_count // 2 + 1):
        up = shifted(up, exp_count, 1)
        blocks.append(up)
        offsets.append(-k)
        if k < exp_count // 2:
            down = shifted(down, exp_count, -1)
            blocks.append(down)
            offsets.append(k)
    second, enc_all = lax.optimization_barrier((second, enc_all))
    second_all = lax.all_gather(second, EXP, axis=0, tiled=True)

    whole = lambda shape: pl.BlockSpec(shape, lambda i, *_: (0,) * len(shape))
    cache_shape = jax.ShapeDtypeStruct((2, tokens, head), BF)
    key_cache, value_cache, terms = pl.pallas_call(
        functools.partial(attention_kernel, offsets, exp_count, tiles, groups),
        grid_spec=pltpu.PrefetchScalarGridSpec(
            num_scalar_prefetch=1,
            grid=(1,),
            in_specs=[whole(first.shape)] * exp_count
            + [whole(enc_all.shape), whole((dec_rows, head)), whole(out_weight.shape)],
            out_specs=[
                pl.BlockSpec((1, tokens, head), lambda i, *_: (0, 0, 0)),
                pl.BlockSpec((1, tokens, head), lambda i, *_: (0, 0, 0)),
                whole((seq_count, groups * half, LANES)),
            ],
            scratch_shapes=[
                pltpu.VMEM((model_width, 2 * head), BF),
                pltpu.VMEM((tokens, 2 * head), F32),
            ],
        ),
        out_shape=[
            cache_shape,
            cache_shape,
            jax.ShapeDtypeStruct((seq_count, groups * half, LANES), BF),
        ],
        compiler_params=pltpu.CompilerParams(vmem_limit_bytes=48 * 1024 * 1024),
        name="project_attend",
    )(z.reshape(1), *blocks, enc_all, queries[0], out_weight)

    state_parts = state[0].astype(F32).reshape(2, half, groups, tiles, LANES)
    state_parts = jnp.pad(state_parts, ((0, 0), (0, 0), (0, 0), (0, tile_slots - tiles), (0, 0)))
    state_here = lax.dynamic_index_in_dim(state_parts, my_half, 0, keepdims=False)
    state_here = lax.dynamic_index_in_dim(state_here, my_tile, 2, keepdims=False).transpose(1, 0, 2)
    chosen = jnp.any(
        expert_ids[0][:, :, None] == jnp.arange(experts, dtype=jnp.int32), axis=1
    ).astype(F32)
    chosen = lax.dynamic_slice_in_dim(chosen, my_half * half, half, 0).T
    got = exchanged(terms, SEQ)
    attended = jnp.sum(got.astype(F32), axis=0).reshape(groups, half, LANES) + state_here
    routed = (attended[None] * chosen[:, None, :, None]).astype(BF)
    routed = exchanged(routed.reshape(exp_count, half, LANES), EXP)
    rows_all = spread(routed.reshape(exp_count * half, LANES), SEQ)
    row_count = 2 * exp_count * half
    x = rows_all[: 2 * tiles].reshape(tiles, row_count, LANES).transpose(1, 0, 2)
    x = x.reshape(row_count, block_width).astype(F32)
    gain = lax.dynamic_slice_in_dim(norm_gain, my_group * block_width, block_width, 0)
    router_here = lax.dynamic_slice_in_dim(router, my_group * block_width, block_width, 0)
    squares = jnp.sum(x * x, axis=1, keepdims=True)
    scaled = (x * gain).astype(BF)
    pair_weight = jnp.concatenate([gate_weight[0].T, up_weight[0].T], axis=0)
    pair = lax.dot_general(
        scaled, pair_weight, (((1,), (1,)), ((), ())), preferred_element_type=F32
    )
    logits = jnp.dot(scaled, router_here, preferred_element_type=F32)
    extra = jnp.concatenate([squares, logits], axis=1)
    high = lax.reduce_precision(extra, 8, 7)
    extra = jnp.concatenate([high, extra - high], axis=1)
    extra = jnp.pad(extra, ((0, 0), (0, LANES - extra.shape[1])))
    partial = jnp.concatenate([pair, extra], axis=1).astype(BF)
    part_rows = row_count // groups
    summed = jnp.sum(
        exchanged(partial.reshape(groups, part_rows, -1), "g").astype(F32), axis=0
    )
    extra = summed[:, 2 * hidden_here :]
    extra = extra[:, : experts + 1] + extra[:, experts + 1 : 2 * experts + 2]
    scale = lax.rsqrt(extra[:, :1] / model_width + EPS)
    probs = jax.nn.softmax(extra[:, 1:] * scale, axis=-1)
    share = jnp.sum(
        jnp.where(jnp.arange(experts) == my_expert, probs, 0.0), axis=1, keepdims=True
    )
    gate = summed[:, :hidden_here] * scale
    lifted = summed[:, hidden_here : 2 * hidden_here] * scale
    hidden = (jax.nn.gelu(gate, approximate=True) * lifted * share).astype(BF)
    hidden = spread(hidden, "g").reshape(row_count, hidden_here)
    out = jnp.dot(hidden, down_weight[0], preferred_element_type=F32).astype(BF)
    out = out.reshape(2, exp_count * half, tiles, LANES).transpose(2, 0, 1, 3)
    out = jnp.pad(out, ((0, tile_slots - tiles), (0, 0), (0, 0), (0, 0)))
    back = exchanged(out.reshape(seq_count, exp_count * half, LANES), SEQ)
    back = jnp.sum(back.astype(F32), axis=0).astype(BF)
    back = exchanged(back.reshape(exp_count, half, LANES), EXP)
    back = jnp.sum(back.astype(F32).reshape(experts, groups, half, LANES), axis=0)
    mixed = (attended + back).astype(BF).reshape(groups * half, LANES)
    mixed = spread(mixed, SEQ)[: 2 * tiles].reshape(tiles, 2, groups, half, LANES)
    mixed = mixed.transpose(1, 3, 2, 0, 4).reshape(1, dec_rows, model_width)

    key_cache, value_cache = pl.pallas_call(
        second_kernel,
        grid=(1,),
        in_specs=[
            pl.BlockSpec(enc_all.shape, lambda i: (0, 0)),
            pl.BlockSpec(second_all.shape, lambda i: (0, 0)),
            pl.BlockSpec(memory_space=pl.ANY),
            pl.BlockSpec(memory_space=pl.ANY),
        ],
        out_specs=[pl.BlockSpec((1, tokens, head), lambda i: (1, 0, 0))] * 2,
        out_shape=[cache_shape, cache_shape],
        scratch_shapes=[pltpu.VMEM((tokens, 2 * head), F32)],
        input_output_aliases={2: 0, 3: 1},
        compiler_params=pltpu.CompilerParams(vmem_limit_bytes=48 * 1024 * 1024),
        name="project_second",
    )(enc_all, second_all, key_cache, value_cache)
    return key_cache[:, None], value_cache[:, None], mixed


def solution(mesh):
    fine = Mesh(mesh.devices.reshape(4, 4, 2, 4, 4), SEQ + EXP)
    return jax.shard_map(
        per_device,
        mesh=fine,
        in_specs=(
            P(EXP, SEQ, None),
            P(None, EXP, SEQ),
            P(None, EXP, SEQ),
            P(EXP, None, SEQ),
            P(EXP, None, None),
            P(SEQ, None),
            P(),
            P(),
            P(EXP, None, None),
            P(EXP, None, SEQ),
            P(EXP, None, SEQ),
            P(EXP, SEQ, None),
        ),
        out_specs=(P(None, EXP, None, SEQ), P(None, EXP, None, SEQ), P(EXP, None, None)),
        check_vma=False,
    )
```

```python
import functools
import math

import jax
import jax.numpy as jnp
from jax import lax
from jax.experimental import pallas as pl
from jax.experimental.pallas import tpu as pltpu
from jax.sharding import Mesh
from jax.sharding import PartitionSpec as P

EPS = 1e-06
SEQ = ("x", "y", "c")
EXP = ("e", "g")
LANES = 128
BF = jnp.bfloat16
F32 = jnp.float32
CHUNKS = 10
WIDE = 384


def shifted(x, count, by):
    return lax.ppermute(x, EXP, [(i, (i + by) % count) for i in range(count)])


def exchanged(x, axes):
    return lax.all_to_all(x, axes, split_axis=0, concat_axis=0, tiled=True)


def spread(x, axes):
    count = lax.axis_size(axes)
    return exchanged(jnp.broadcast_to(x[None], (count,) + x.shape), axes)


def project(enc_ref, weight_ref, out_enc, copies, acc_ref, key_ref, value_ref):
    width = key_ref.shape[-1]
    step = weight_ref.shape[0] // len(copies)
    for k, copy in enumerate(copies):
        copy.wait()
        term = jnp.dot(
            out_enc[:, k * step : (k + 1) * step],
            weight_ref[k * step : (k + 1) * step, :],
            preferred_element_type=F32,
        )
        if k == 0:
            acc_ref[...] = term
        else:
            acc_ref[...] += term
    key_ref[0] = acc_ref[:, :width].astype(BF)
    value_ref[0] = acc_ref[:, width:].astype(BF)


def chunk_copies(enc_ref, held, sems, count):
    step = held.shape[1] // count
    copies = [
        pltpu.make_async_copy(
            enc_ref.at[:, k * step : (k + 1) * step],
            held.at[:, k * step : (k + 1) * step],
            sems.at[k],
        )
        for k in range(count)
    ]
    for copy in copies:
        copy.start()
    return copies


def attention_kernel(
    pieces,
    tiles,
    groups,
    experts,
    group_ref,
    *refs,
):
    blocks = refs[: len(pieces)]
    (
        query_ref,
        enc_ref,
        out_hbm,
        key_ref,
        value_ref,
        term_ref,
        weight_ref,
        acc_ref,
        held,
        out_ref,
        sems,
    ) = refs[len(pieces) :]
    copies = chunk_copies(enc_ref, held, sems, CHUNKS)
    out_copy = pltpu.make_async_copy(out_hbm, out_ref, sems.at[CHUNKS])
    out_copy.start()
    rows = weight_ref.shape[0] // (groups * experts)
    for block, (offset, first, last) in zip(blocks, pieces):
        group = lax.rem(group_ref[0] + (groups + offset), groups)
        for e in range(first, last):
            at = pl.multiple_of((e * groups + group) * rows, 64)
            weight_ref[pl.ds(at, rows), :] = block[(e - first) * rows : (e - first + 1) * rows, :]
    project(enc_ref, weight_ref, held, copies, acc_ref, key_ref, value_ref)
    head = key_ref.shape[-1]
    scores = lax.dot_general(
        query_ref[...], key_ref[0], (((1,), (1,)), ((), ())), preferred_element_type=F32
    ) / math.sqrt(head)
    raised = jnp.exp(scores - jnp.max(scores, axis=-1, keepdims=True))
    attn = (raised / jnp.sum(raised, axis=-1, keepdims=True)).astype(BF)
    context = jnp.dot(attn, value_ref[0], preferred_element_type=F32).astype(BF)
    out_copy.wait()
    half = query_ref.shape[0] // 2
    for t in range(tiles):
        parts = [
            jnp.dot(
                context,
                out_ref[:, (g * tiles + t) * LANES : (g * tiles + t + 1) * LANES],
                preferred_element_type=F32,
            )
            for g in range(groups)
        ]
        for h in range(2):
            term_ref[2 * t + h] = jnp.concatenate(
                [p[h * half : (h + 1) * half] for p in parts], axis=0
            ).astype(BF)
    for s in range(2 * tiles, term_ref.shape[0]):
        term_ref[s] = jnp.zeros(term_ref.shape[1:], BF)


def second_kernel(
    enc_ref, weight_ref, key_in, value_in, key_ref, value_ref, acc_ref, held, sems
):
    copies = chunk_copies(enc_ref, held, sems, CHUNKS)
    project(enc_ref, weight_ref, held, copies, acc_ref, key_ref, value_ref)


def expert_input_kernel(
    hidden, rows_ref, gain_ref, router_ref, gate_ref, up_ref, part_ref, x_ref, gate_all, up_all
):
    tiles = rows_ref.shape[0]
    wide = gate_all.shape[0]
    squares = None
    for t in range(tiles):
        x = rows_ref[t].astype(F32)
        term = jnp.sum(x * x, axis=1, keepdims=True)
        squares = term if squares is None else squares + term
        gain = gain_ref[:, t * LANES : (t + 1) * LANES]
        x_ref[:, t * LANES : (t + 1) * LANES] = (x * gain).astype(BF)
    gate_all[:hidden] = gate_ref[...]
    gate_all[hidden:] = router_ref[...]
    up_all[:hidden] = up_ref[...]
    up_all[hidden:] = jnp.zeros((wide - hidden, up_all.shape[1]), BF)
    contract = (((1,), (1,)), ((), ()))
    gate = lax.dot_general(x_ref[...], gate_all[...], contract, preferred_element_type=F32)
    lane = lax.broadcasted_iota(jnp.int32, gate.shape, 1)
    gate = jnp.where((lane == hidden + 4) | (lane == hidden + 12), squares, gate)
    high = gate.astype(BF)
    low = (gate - high.astype(F32)).astype(BF)
    part_ref[:, :wide] = jnp.where(lane >= hidden + 8, low.astype(F32), high.astype(F32)).astype(BF)
    up = lax.dot_general(x_ref[...], up_all[...], contract, preferred_element_type=F32)
    part_ref[:, wide:] = up.astype(BF)


def per_device(
    encoded,
    key_weight,
    value_weight,
    queries,
    state,
    out_weight,
    norm_gain,
    router,
    expert_ids,
    gate_weight,
    up_weight,
    down_weight,
):
    seq_count = lax.axis_size(SEQ)
    exp_count = lax.axis_size(EXP)
    groups = lax.axis_size("g")
    experts = lax.axis_size("e")
    dec_rows = state.shape[1]
    half = dec_rows // 2
    model_width = state.shape[2]
    block_width = model_width // groups
    tiles = block_width // LANES
    tile_slots = seq_count // 2
    head = key_weight.shape[2]
    hidden_here = gate_weight.shape[2]
    tokens = encoded.shape[1] * seq_count
    my_tile = lax.axis_index(("x", "y"))
    my_half = lax.axis_index("c")
    my_expert = lax.axis_index("e")
    my_group = lax.axis_index("g")

    enc_all = lax.all_gather(encoded[0], SEQ, axis=0, tiled=True)
    first = jnp.concatenate([key_weight[0], value_weight[0]], axis=1)
    second = jnp.concatenate([key_weight[1], value_weight[1]], axis=1)
    own = lax.all_gather(first, "e", axis=0, tiled=True)
    middle = own.shape[0] // 2
    left = shifted(own, exp_count, 1)
    right = shifted(own, exp_count, -1)
    far_left = shifted(left[:middle], exp_count, 1)
    far_right = shifted(right[middle:], exp_count, -1)
    blocks = [own, left, right, far_left, far_right]
    pieces = [
        (0, 0, experts),
        (-1, 0, experts),
        (1, 0, experts),
        (-2, 0, experts // 2),
        (2, experts // 2, experts),
    ]
    second, enc_all = lax.optimization_barrier((second, enc_all))
    second_all = lax.all_gather(second, EXP, axis=0, tiled=True)

    whole = lambda shape: pl.BlockSpec(shape, lambda i, *_: (0,) * len(shape))
    cache_shape = jax.ShapeDtypeStruct((2, tokens, head), BF)
    key_cache, value_cache, terms = pl.pallas_call(
        functools.partial(attention_kernel, pieces, tiles, groups, experts),
        grid_spec=pltpu.PrefetchScalarGridSpec(
            num_scalar_prefetch=1,
            grid=(1,),
            in_specs=[whole(block.shape) for block in blocks]
            + [
                whole((dec_rows, head)),
                pl.BlockSpec(memory_space=pltpu.HBM),
                pl.BlockSpec(memory_space=pltpu.HBM),
            ],
            out_specs=[
                pl.BlockSpec((1, tokens, head), lambda i, *_: (0, 0, 0)),
                pl.BlockSpec((1, tokens, head), lambda i, *_: (0, 0, 0)),
                whole((seq_count, groups * half, LANES)),
            ],
            scratch_shapes=[
                pltpu.VMEM((model_width, 2 * head), BF),
                pltpu.VMEM((tokens, 2 * head), F32),
                pltpu.VMEM((tokens, model_width), BF),
                pltpu.VMEM(out_weight.shape, BF),
                pltpu.SemaphoreType.DMA((CHUNKS + 1,)),
            ],
        ),
        out_shape=[
            cache_shape,
            cache_shape,
            jax.ShapeDtypeStruct((seq_count, groups * half, LANES), BF),
        ],
        compiler_params=pltpu.CompilerParams(vmem_limit_bytes=48 * 1024 * 1024),
        name="project_attend",
    )(my_group.reshape(1), *blocks, queries[0], enc_all, out_weight)

    state_parts = state[0].astype(F32).reshape(2, half, groups, tiles, LANES)
    state_parts = jnp.pad(state_parts, ((0, 0), (0, 0), (0, 0), (0, tile_slots - tiles), (0, 0)))
    state_here = lax.dynamic_index_in_dim(state_parts, my_half, 0, keepdims=False)
    state_here = lax.dynamic_index_in_dim(state_here, my_tile, 2, keepdims=False).transpose(1, 0, 2)
    chosen = jnp.any(
        expert_ids[0][:, :, None] == jnp.arange(experts, dtype=jnp.int32), axis=1
    ).astype(F32)
    chosen = lax.dynamic_slice_in_dim(chosen, my_half * half, half, 0).T
    got = exchanged(terms, SEQ)
    attended = jnp.sum(got.astype(F32), axis=0).reshape(groups, half, LANES) + state_here
    routed = (attended[None] * chosen[:, None, :, None]).astype(BF)
    routed = exchanged(routed.reshape(exp_count, half, LANES), EXP)
    rows_all = spread(routed.reshape(exp_count * half, LANES), SEQ)
    row_count = 2 * exp_count * half
    gain = lax.dynamic_slice_in_dim(norm_gain, my_group * block_width, block_width, 0)
    routes = lax.dynamic_slice_in_dim(router.T, my_group * block_width, block_width, 1)
    gap = jnp.zeros((8 - experts, block_width), BF)
    routes = jnp.concatenate([routes, gap, routes, gap], axis=0)
    routes = jnp.pad(routes, ((0, WIDE - hidden_here - routes.shape[0]), (0, 0)))
    partial = pl.pallas_call(
        functools.partial(expert_input_kernel, hidden_here),
        grid=(1,),
        in_specs=[
            whole((tiles, row_count, LANES)),
            whole((1, block_width)),
            whole(routes.shape),
            whole((hidden_here, block_width)),
            whole((hidden_here, block_width)),
        ],
        out_specs=whole((row_count, 2 * WIDE)),
        out_shape=jax.ShapeDtypeStruct((row_count, 2 * WIDE), BF),
        scratch_shapes=[
            pltpu.VMEM((row_count, block_width), BF),
            pltpu.VMEM((WIDE, block_width), BF),
            pltpu.VMEM((WIDE, block_width), BF),
        ],
        compiler_params=pltpu.CompilerParams(vmem_limit_bytes=24 * 1024 * 1024),
        name="expert_input",
    )(
        rows_all.reshape(tile_slots, row_count, LANES),
        gain[None],
        routes,
        gate_weight[0].T,
        up_weight[0].T,
    )
    summed = jnp.sum(lax.all_gather(partial, "g", axis=0).astype(F32), axis=0)
    extra = summed[:, hidden_here : hidden_here + 5] + summed[:, hidden_here + 8 : hidden_here + 13]
    scale = lax.rsqrt(extra[:, 4:] / model_width + EPS)
    probs = jax.nn.softmax(extra[:, :4] * scale, axis=-1)
    share = jnp.sum(
        jnp.where(jnp.arange(experts) == my_expert, probs, 0.0), axis=1, keepdims=True
    )
    gate = summed[:, :hidden_here] * scale
    lifted = summed[:, WIDE : WIDE + hidden_here] * scale
    hidden = (jax.nn.gelu(gate, approximate=True) * lifted * share).astype(BF)
    out = jnp.dot(hidden, down_weight[0], preferred_element_type=F32).astype(BF)
    out = out.reshape(2, exp_count * half, tiles, LANES).transpose(2, 0, 1, 3)
    out = jnp.pad(out, ((0, tile_slots - tiles), (0, 0), (0, 0), (0, 0)))
    out, second_all = lax.optimization_barrier(
        (out.reshape(seq_count, exp_count * half, LANES), second_all)
    )
    back = exchanged(out, SEQ)
    key_cache, value_cache = pl.pallas_call(
        second_kernel,
        grid=(1,),
        in_specs=[
            pl.BlockSpec(memory_space=pltpu.HBM),
            pl.BlockSpec(second_all.shape, lambda i: (0, 0)),
            pl.BlockSpec(memory_space=pl.ANY),
            pl.BlockSpec(memory_space=pl.ANY),
        ],
        out_specs=[pl.BlockSpec((1, tokens, head), lambda i: (1, 0, 0))] * 2,
        out_shape=[cache_shape, cache_shape],
        scratch_shapes=[
            pltpu.VMEM((tokens, 2 * head), F32),
            pltpu.VMEM((tokens, model_width), BF),
            pltpu.SemaphoreType.DMA((CHUNKS,)),
        ],
        cost_estimate=pl.CostEstimate(
            flops=4 * tokens * model_width * head,
            bytes_accessed=10 * tokens * model_width,
            transcendentals=0,
        ),
        input_output_aliases={2: 0, 3: 1},
        compiler_params=pltpu.CompilerParams(vmem_limit_bytes=48 * 1024 * 1024),
        name="project_second",
    )(enc_all, second_all, key_cache, value_cache)
    back, key_cache, value_cache = lax.optimization_barrier((back, key_cache, value_cache))
    back = jnp.sum(back.astype(F32), axis=0).astype(BF)
    back = exchanged(back.reshape(exp_count, half, LANES), EXP)
    back = jnp.sum(back.astype(F32).reshape(experts, groups, half, LANES), axis=0)
    mixed = (attended + back).astype(BF).reshape(groups * half, LANES)
    mixed = spread(mixed, SEQ)[: 2 * tiles].reshape(tiles, 2, groups, half, LANES)
    mixed = mixed.transpose(1, 3, 2, 0, 4).reshape(1, dec_rows, model_width)

    return key_cache[:, None], value_cache[:, None], mixed


def solution(mesh):
    fine = Mesh(mesh.devices.reshape(4, 4, 2, 4, 4), SEQ + EXP)
    return jax.shard_map(
        per_device,
        mesh=fine,
        in_specs=(
            P(EXP, SEQ, None),
            P(None, EXP, SEQ),
            P(None, EXP, SEQ),
            P(EXP, None, SEQ),
            P(EXP, None, None),
            P(SEQ, None),
            P(),
            P(),
            P(EXP, None, None),
            P(EXP, None, SEQ),
            P(EXP, None, SEQ),
            P(EXP, SEQ, None),
        ),
        out_specs=(P(None, EXP, None, SEQ), P(None, EXP, None, SEQ), P(EXP, None, None)),
        check_vma=False,
    )
```

```python
import functools
import math

import jax
import jax.numpy as jnp
from jax import lax
from jax.experimental import pallas as pl
from jax.experimental.pallas import tpu as pltpu
from jax.sharding import Mesh
from jax.sharding import PartitionSpec as P

EPS = 1e-06
SEQ = ("x", "y", "c")
CHIPS = ("x", "y")
EXP = ("e", "g")
LANES = 128
BF = jnp.bfloat16
F32 = jnp.float32
CHUNKS = 10
WIDE = 384


def shifted(x, count, by):
    return lax.ppermute(x, EXP, [(i, (i + by) % count) for i in range(count)])


def exchanged(x, axes):
    return lax.all_to_all(x, axes, split_axis=0, concat_axis=0, tiled=True)


def spread(x, axes):
    count = lax.axis_size(axes)
    return exchanged(jnp.broadcast_to(x[None], (count,) + x.shape), axes)


def project(enc_ref, weight_ref, out_enc, copies, acc_ref, key_ref, value_ref):
    width = key_ref.shape[-1]
    step = weight_ref.shape[0] // len(copies)
    for k, copy in enumerate(copies):
        copy.wait()
        term = jnp.dot(
            out_enc[:, k * step : (k + 1) * step],
            weight_ref[k * step : (k + 1) * step, :],
            preferred_element_type=F32,
        )
        if k == 0:
            acc_ref[...] = term
        else:
            acc_ref[...] += term
    key_ref[0] = acc_ref[:, :width].astype(BF)
    value_ref[0] = acc_ref[:, width:].astype(BF)


def chunk_copies(enc_ref, held, sems, count):
    step = held.shape[1] // count
    copies = [
        pltpu.make_async_copy(
            enc_ref.at[:, k * step : (k + 1) * step],
            held.at[:, k * step : (k + 1) * step],
            sems.at[k],
        )
        for k in range(count)
    ]
    for copy in copies:
        copy.start()
    return copies


def attention_kernel(
    pieces,
    tiles,
    groups,
    experts,
    group_ref,
    *refs,
):
    blocks = refs[: len(pieces)]
    (
        query_ref,
        enc_ref,
        out_hbm,
        key_ref,
        value_ref,
        term_ref,
        weight_ref,
        acc_ref,
        held,
        out_ref,
        sems,
    ) = refs[len(pieces) :]
    copies = chunk_copies(enc_ref, held, sems, CHUNKS)
    out_copy = pltpu.make_async_copy(out_hbm, out_ref, sems.at[CHUNKS])
    out_copy.start()
    rows = weight_ref.shape[0] // (groups * experts)
    for block, (offset, first, last) in zip(blocks, pieces):
        group = lax.rem(group_ref[0] + (groups + offset), groups)
        for e in range(first, last):
            at = pl.multiple_of((e * groups + group) * rows, 64)
            weight_ref[pl.ds(at, rows), :] = block[(e - first) * rows : (e - first + 1) * rows, :]
    project(enc_ref, weight_ref, held, copies, acc_ref, key_ref, value_ref)
    head = key_ref.shape[-1]
    scores = lax.dot_general(
        query_ref[...], key_ref[0], (((1,), (1,)), ((), ())), preferred_element_type=F32
    ) / math.sqrt(head)
    raised = jnp.exp(scores - jnp.max(scores, axis=-1, keepdims=True))
    attn = (raised / jnp.sum(raised, axis=-1, keepdims=True)).astype(BF)
    context = jnp.dot(attn, value_ref[0], preferred_element_type=F32).astype(BF)
    out_copy.wait()
    for t in range(tiles):
        term_ref[t] = jnp.concatenate(
            [
                jnp.dot(
                    context,
                    out_ref[:, (g * tiles + t) * LANES : (g * tiles + t + 1) * LANES],
                    preferred_element_type=F32,
                )
                for g in range(groups)
            ],
            axis=0,
        ).astype(BF)
    for t in range(tiles, term_ref.shape[0]):
        term_ref[t] = jnp.zeros(term_ref.shape[1:], BF)


def second_kernel(
    enc_ref, weight_ref, key_in, value_in, key_ref, value_ref, acc_ref, held, sems
):
    copies = chunk_copies(enc_ref, held, sems, CHUNKS)
    project(enc_ref, weight_ref, held, copies, acc_ref, key_ref, value_ref)


def expert_input_kernel(
    hidden, rows_ref, gain_ref, router_ref, gate_ref, up_ref, part_ref, x_ref, gate_all, up_all
):
    tiles = rows_ref.shape[0]
    wide = gate_all.shape[0]
    squares = None
    for t in range(tiles):
        x = rows_ref[t].astype(F32)
        term = jnp.sum(x * x, axis=1, keepdims=True)
        squares = term if squares is None else squares + term
        gain = gain_ref[:, t * LANES : (t + 1) * LANES]
        x_ref[:, t * LANES : (t + 1) * LANES] = (x * gain).astype(BF)
    gate_all[:hidden] = gate_ref[...]
    gate_all[hidden:] = router_ref[...]
    up_all[:hidden] = up_ref[...]
    up_all[hidden:] = jnp.zeros((wide - hidden, up_all.shape[1]), BF)
    contract = (((1,), (1,)), ((), ()))
    gate = lax.dot_general(x_ref[...], gate_all[...], contract, preferred_element_type=F32)
    lane = lax.broadcasted_iota(jnp.int32, gate.shape, 1)
    gate = jnp.where((lane == hidden + 4) | (lane == hidden + 12), squares, gate)
    high = gate.astype(BF)
    low = (gate - high.astype(F32)).astype(BF)
    part_ref[:, :wide] = jnp.where(lane >= hidden + 8, low.astype(F32), high.astype(F32)).astype(BF)
    up = lax.dot_general(x_ref[...], up_all[...], contract, preferred_element_type=F32)
    part_ref[:, wide:] = up.astype(BF)


def expert_output_kernel(hidden, width, expert_ref, part_ref, down_ref, out_ref):
    total = part_ref[0].astype(F32)
    for k in range(1, part_ref.shape[0]):
        total = total + part_ref[k].astype(F32)
    wide = total.shape[1] // 2
    gate, lifted = total[:, :wide], total[:, wide:]

    def column(j):
        return gate[:, hidden + j : hidden + j + 1] + gate[:, hidden + 8 + j : hidden + 9 + j]

    scale = lax.rsqrt(column(4) / width + EPS)
    logits = [column(j) * scale for j in range(4)]
    top = functools.reduce(jnp.maximum, logits)
    raised = [jnp.exp(logit - top) for logit in logits]
    mine = [jnp.where(expert_ref[0] == j, raised[j], 0.0) for j in range(4)]
    share = sum(mine) / sum(raised)
    gate = gate * scale
    active = 0.5 * gate * (1.0 + jnp.tanh(math.sqrt(2 / math.pi) * (gate + 0.044715 * gate**3)))
    units = (active * (lifted * scale) * share)[:, :hidden].astype(BF)
    out = jnp.dot(units, down_ref[...], preferred_element_type=F32)
    tiles = out.shape[1] // LANES
    for t in range(tiles):
        out_ref[t] = out[:, t * LANES : (t + 1) * LANES].astype(BF)
    for t in range(tiles, out_ref.shape[0]):
        out_ref[t] = jnp.zeros(out_ref.shape[1:], BF)


def per_device(
    encoded,
    key_weight,
    value_weight,
    queries,
    state,
    out_weight,
    norm_gain,
    router,
    expert_ids,
    gate_weight,
    up_weight,
    down_weight,
):
    seq_count = lax.axis_size(SEQ)
    exp_count = lax.axis_size(EXP)
    groups = lax.axis_size("g")
    experts = lax.axis_size("e")
    dec_rows = state.shape[1]
    model_width = state.shape[2]
    block_width = model_width // groups
    tiles = block_width // LANES
    tile_slots = seq_count // 2
    head = key_weight.shape[2]
    hidden_here = gate_weight.shape[2]
    tokens = encoded.shape[1] * seq_count
    my_tile = lax.axis_index(CHIPS)
    my_core = lax.axis_index("c")
    my_expert = lax.axis_index("e")
    my_group = lax.axis_index("g")

    enc_all = lax.all_gather(encoded[0], SEQ, axis=0, tiled=True)
    first = jnp.concatenate([key_weight[0], value_weight[0]], axis=1)
    second = jnp.concatenate([key_weight[1], value_weight[1]], axis=1)
    own = lax.all_gather(first, "e", axis=0, tiled=True)
    second, own = lax.optimization_barrier((second, own))
    middle = own.shape[0] // 2
    left = shifted(own, exp_count, 1)
    right = shifted(own, exp_count, -1)
    far_left = shifted(left[:middle], exp_count, 1)
    far_right = shifted(right[middle:], exp_count, -1)
    blocks = [own, left, right, far_left, far_right]
    pieces = [
        (0, 0, experts),
        (-1, 0, experts),
        (1, 0, experts),
        (-2, 0, experts // 2),
        (2, experts // 2, experts),
    ]
    second_all = lax.all_gather(second, EXP, axis=0, tiled=True)

    whole = lambda shape: pl.BlockSpec(shape, lambda i, *_: (0,) * len(shape))
    cache_shape = jax.ShapeDtypeStruct((2, tokens, head), BF)
    key_cache, value_cache, terms = pl.pallas_call(
        functools.partial(attention_kernel, pieces, tiles, groups, experts),
        grid_spec=pltpu.PrefetchScalarGridSpec(
            num_scalar_prefetch=1,
            grid=(1,),
            in_specs=[whole(block.shape) for block in blocks]
            + [
                whole((dec_rows, head)),
                pl.BlockSpec(memory_space=pltpu.HBM),
                pl.BlockSpec(memory_space=pltpu.HBM),
            ],
            out_specs=[
                pl.BlockSpec((1, tokens, head), lambda i, *_: (0, 0, 0)),
                pl.BlockSpec((1, tokens, head), lambda i, *_: (0, 0, 0)),
                whole((tile_slots, groups * dec_rows, LANES)),
            ],
            scratch_shapes=[
                pltpu.VMEM((model_width, 2 * head), BF),
                pltpu.VMEM((tokens, 2 * head), F32),
                pltpu.VMEM((tokens, model_width), BF),
                pltpu.VMEM(out_weight.shape, BF),
                pltpu.SemaphoreType.DMA((CHUNKS + 1,)),
            ],
        ),
        out_shape=[
            cache_shape,
            cache_shape,
            jax.ShapeDtypeStruct((tile_slots, groups * dec_rows, LANES), BF),
        ],
        compiler_params=pltpu.CompilerParams(vmem_limit_bytes=48 * 1024 * 1024),
        name="project_attend",
    )(my_group.reshape(1), *blocks, queries[0], enc_all, out_weight)

    state_parts = state[0].astype(F32).reshape(dec_rows, groups, tiles, LANES)
    state_parts = jnp.pad(state_parts, ((0, 0), (0, 0), (0, tile_slots - tiles), (0, 0)))
    state_here = lax.dynamic_index_in_dim(state_parts, my_tile, 2, keepdims=False).transpose(1, 0, 2)
    state_here = jnp.where(my_core == 0, state_here, 0.0)
    chosen = jnp.any(
        expert_ids[0][:, :, None] == jnp.arange(experts, dtype=jnp.int32), axis=1
    ).astype(F32).T
    got = exchanged(terms, CHIPS)
    attended = jnp.sum(got.astype(F32), axis=0).reshape(groups, dec_rows, LANES) + state_here
    routed = (attended[None] * chosen[:, None, :, None]).astype(BF)
    routed = jnp.broadcast_to(routed[None], (2,) + routed.shape)
    routed = exchanged(routed.reshape(2 * exp_count, dec_rows, LANES), ("c",) + EXP)
    row_count = exp_count * dec_rows
    routed = jnp.sum(routed.astype(F32).reshape(2, row_count, LANES), axis=0).astype(BF)
    rows_all = spread(routed, CHIPS)
    gain = lax.dynamic_slice_in_dim(norm_gain, my_group * block_width, block_width, 0)
    routes = lax.dynamic_slice_in_dim(router.T, my_group * block_width, block_width, 1)
    gap = jnp.zeros((8 - experts, block_width), BF)
    routes = jnp.concatenate([routes, gap, routes, gap], axis=0)
    routes = jnp.pad(routes, ((0, WIDE - hidden_here - routes.shape[0]), (0, 0)))
    partial = pl.pallas_call(
        functools.partial(expert_input_kernel, hidden_here),
        grid=(1,),
        in_specs=[
            whole((tiles, row_count, LANES)),
            whole((1, block_width)),
            whole(routes.shape),
            whole((hidden_here, block_width)),
            whole((hidden_here, block_width)),
        ],
        out_specs=whole((row_count, 2 * WIDE)),
        out_shape=jax.ShapeDtypeStruct((row_count, 2 * WIDE), BF),
        scratch_shapes=[
            pltpu.VMEM((row_count, block_width), BF),
            pltpu.VMEM((WIDE, block_width), BF),
            pltpu.VMEM((WIDE, block_width), BF),
        ],
        compiler_params=pltpu.CompilerParams(vmem_limit_bytes=24 * 1024 * 1024),
        name="expert_input",
    )(
        rows_all,
        gain[None],
        routes,
        gate_weight[0].T,
        up_weight[0].T,
    )
    parts = lax.all_gather(partial, "g", axis=0)
    out = pl.pallas_call(
        functools.partial(expert_output_kernel, hidden_here, model_width),
        grid_spec=pltpu.PrefetchScalarGridSpec(
            num_scalar_prefetch=1,
            grid=(1,),
            in_specs=[whole(parts.shape), whole((hidden_here, block_width))],
            out_specs=whole((tile_slots, row_count, LANES)),
        ),
        out_shape=jax.ShapeDtypeStruct((tile_slots, row_count, LANES), BF),
        compiler_params=pltpu.CompilerParams(vmem_limit_bytes=24 * 1024 * 1024),
        name="expert_output",
    )(my_expert.reshape(1), parts, down_weight[0])
    out, second_all = lax.optimization_barrier((out, second_all))
    back = exchanged(out, CHIPS)
    key_cache, value_cache = pl.pallas_call(
        second_kernel,
        grid=(1,),
        in_specs=[
            pl.BlockSpec(memory_space=pltpu.HBM),
            pl.BlockSpec(second_all.shape, lambda i: (0, 0)),
            pl.BlockSpec(memory_space=pl.ANY),
            pl.BlockSpec(memory_space=pl.ANY),
        ],
        out_specs=[pl.BlockSpec((1, tokens, head), lambda i: (1, 0, 0))] * 2,
        out_shape=[cache_shape, cache_shape],
        scratch_shapes=[
            pltpu.VMEM((tokens, 2 * head), F32),
            pltpu.VMEM((tokens, model_width), BF),
            pltpu.SemaphoreType.DMA((CHUNKS,)),
        ],
        cost_estimate=pl.CostEstimate(
            flops=4 * tokens * model_width * head,
            bytes_accessed=10 * tokens * model_width,
            transcendentals=0,
        ),
        input_output_aliases={2: 0, 3: 1},
        compiler_params=pltpu.CompilerParams(vmem_limit_bytes=48 * 1024 * 1024),
        name="project_second",
    )(enc_all, second_all, key_cache, value_cache)
    back, key_cache, value_cache = lax.optimization_barrier((back, key_cache, value_cache))
    back = jnp.sum(back.astype(F32), axis=0).astype(BF)
    back = exchanged(back.reshape(exp_count, dec_rows, LANES), EXP)
    back = jnp.sum(back.astype(F32).reshape(experts, groups, dec_rows, LANES), axis=0)
    mixed = (attended + back).astype(BF).reshape(groups * dec_rows, LANES)
    mixed = spread(mixed, SEQ)[: 2 * tiles].reshape(tiles, 2, groups, dec_rows, LANES)
    mixed = jnp.sum(mixed.astype(F32), axis=1).astype(BF)
    mixed = mixed.transpose(2, 1, 0, 3).reshape(1, dec_rows, model_width)
    return key_cache[:, None], value_cache[:, None], mixed


def solution(mesh):
    fine = Mesh(mesh.devices.reshape(4, 4, 2, 4, 4), SEQ + EXP)
    return jax.shard_map(
        per_device,
        mesh=fine,
        in_specs=(
            P(EXP, SEQ, None),
            P(None, EXP, SEQ),
            P(None, EXP, SEQ),
            P(EXP, None, SEQ),
            P(EXP, None, None),
            P(SEQ, None),
            P(),
            P(),
            P(EXP, None, None),
            P(EXP, None, SEQ),
            P(EXP, None, SEQ),
            P(EXP, SEQ, None),
        ),
        out_specs=(P(None, EXP, None, SEQ), P(None, EXP, None, SEQ), P(EXP, None, None)),
        check_vma=False,
    )
```

```python
import functools
import math

import jax
import jax.numpy as jnp
from jax import lax
from jax.experimental import pallas as pl
from jax.experimental.pallas import tpu as pltpu
from jax.sharding import Mesh
from jax.sharding import PartitionSpec as P

EPS = 1e-06
SEQ = ("x", "y", "c")
CHIPS = ("x", "y")
EXP = ("e", "g")
LANES = 128
BF = jnp.bfloat16
F32 = jnp.float32
CHUNKS = 10
WIDE = 384


def shifted(x, count, by):
    return lax.ppermute(x, EXP, [(i, (i + by) % count) for i in range(count)])


def exchanged(x, axes):
    return lax.all_to_all(x, axes, split_axis=0, concat_axis=0, tiled=True)


def spread(x, axes):
    count = lax.axis_size(axes)
    return exchanged(jnp.broadcast_to(x[None], (count,) + x.shape), axes)


def project(enc_ref, weight_ref, out_enc, copies, acc_ref, key_ref, value_ref):
    width = key_ref.shape[-1]
    step = weight_ref.shape[0] // len(copies)
    for k, copy in enumerate(copies):
        copy.wait()
        term = jnp.dot(
            out_enc[:, k * step : (k + 1) * step],
            weight_ref[k * step : (k + 1) * step, :],
            preferred_element_type=F32,
        )
        if k == 0:
            acc_ref[...] = term
        else:
            acc_ref[...] += term
    key_ref[0] = acc_ref[:, :width].astype(BF)
    value_ref[0] = acc_ref[:, width:].astype(BF)


def chunk_copies(enc_ref, held, sems, count):
    step = held.shape[1] // count
    copies = [
        pltpu.make_async_copy(
            enc_ref.at[:, k * step : (k + 1) * step],
            held.at[:, k * step : (k + 1) * step],
            sems.at[k],
        )
        for k in range(count)
    ]
    for copy in copies:
        copy.start()
    return copies


def attention_kernel(
    pieces,
    tiles,
    groups,
    experts,
    group_ref,
    *refs,
):
    blocks = refs[: len(pieces)]
    (
        query_ref,
        enc_ref,
        out_hbm,
        key_ref,
        value_ref,
        term_ref,
        weight_ref,
        acc_ref,
        held,
        out_ref,
        sems,
    ) = refs[len(pieces) :]
    copies = chunk_copies(enc_ref, held, sems, CHUNKS)
    out_copy = pltpu.make_async_copy(out_hbm, out_ref, sems.at[CHUNKS])
    out_copy.start()
    rows = weight_ref.shape[0] // (groups * experts)
    for block, (offset, first, last) in zip(blocks, pieces):
        group = lax.rem(group_ref[0] + (groups + offset), groups)
        for e in range(first, last):
            at = pl.multiple_of((e * groups + group) * rows, 64)
            weight_ref[pl.ds(at, rows), :] = block[(e - first) * rows : (e - first + 1) * rows, :]
    project(enc_ref, weight_ref, held, copies, acc_ref, key_ref, value_ref)
    head = key_ref.shape[-1]
    scores = lax.dot_general(
        query_ref[...], key_ref[0], (((1,), (1,)), ((), ())), preferred_element_type=F32
    ) / math.sqrt(head)
    raised = jnp.exp(scores - jnp.max(scores, axis=-1, keepdims=True))
    attn = (raised / jnp.sum(raised, axis=-1, keepdims=True)).astype(BF)
    context = jnp.dot(attn, value_ref[0], preferred_element_type=F32).astype(BF)
    out_copy.wait()
    half = query_ref.shape[0] // 2
    for t in range(tiles):
        parts = [
            jnp.dot(
                context,
                out_ref[:, (g * tiles + t) * LANES : (g * tiles + t + 1) * LANES],
                preferred_element_type=F32,
            )
            for g in range(groups)
        ]
        for h in range(2):
            term_ref[2 * t + h] = jnp.concatenate(
                [p[h * half : (h + 1) * half] for p in parts], axis=0
            ).astype(BF)
    for s in range(2 * tiles, term_ref.shape[0]):
        term_ref[s] = jnp.zeros(term_ref.shape[1:], BF)


def second_kernel(
    enc_ref, weight_ref, key_in, value_in, key_ref, value_ref, acc_ref, held, sems
):
    copies = chunk_copies(enc_ref, held, sems, CHUNKS)
    project(enc_ref, weight_ref, held, copies, acc_ref, key_ref, value_ref)


def expert_input_kernel(
    hidden, rows_ref, gain_ref, router_ref, gate_ref, up_ref, part_ref, x_ref, gate_all, up_all
):
    tiles = rows_ref.shape[0]
    wide = gate_all.shape[0]
    squares = None
    for t in range(tiles):
        x = rows_ref[t].astype(F32)
        term = jnp.sum(x * x, axis=1, keepdims=True)
        squares = term if squares is None else squares + term
        gain = gain_ref[:, t * LANES : (t + 1) * LANES]
        x_ref[:, t * LANES : (t + 1) * LANES] = (x * gain).astype(BF)
    gate_all[:hidden] = gate_ref[...]
    gate_all[hidden:] = router_ref[...]
    up_all[:hidden] = up_ref[...]
    up_all[hidden:] = jnp.zeros((wide - hidden, up_all.shape[1]), BF)
    contract = (((1,), (1,)), ((), ()))
    gate = lax.dot_general(x_ref[...], gate_all[...], contract, preferred_element_type=F32)
    lane = lax.broadcasted_iota(jnp.int32, gate.shape, 1)
    gate = jnp.where((lane == hidden + 4) | (lane == hidden + 12), squares, gate)
    high = gate.astype(BF)
    low = (gate - high.astype(F32)).astype(BF)
    part_ref[:, :wide] = jnp.where(lane >= hidden + 8, low.astype(F32), high.astype(F32)).astype(BF)
    up = lax.dot_general(x_ref[...], up_all[...], contract, preferred_element_type=F32)
    part_ref[:, wide:] = up.astype(BF)


def expert_output_kernel(hidden, width, expert_ref, part_ref, down_ref, out_ref):
    total = part_ref[0].astype(F32)
    for k in range(1, part_ref.shape[0]):
        total = total + part_ref[k].astype(F32)
    wide = total.shape[1] // 2
    gate, lifted = total[:, :wide], total[:, wide:]

    def column(j):
        return gate[:, hidden + j : hidden + j + 1] + gate[:, hidden + 8 + j : hidden + 9 + j]

    scale = lax.rsqrt(column(4) / width + EPS)
    logits = [column(j) * scale for j in range(4)]
    top = functools.reduce(jnp.maximum, logits)
    raised = [jnp.exp(logit - top) for logit in logits]
    mine = [jnp.where(expert_ref[0] == j, raised[j], 0.0) for j in range(4)]
    share = sum(mine) / sum(raised)
    gate = gate * scale
    active = 0.5 * gate * (1.0 + jnp.tanh(math.sqrt(2 / math.pi) * (gate + 0.044715 * gate**3)))
    units = (active * (lifted * scale) * share)[:, :hidden].astype(BF)
    out = jnp.dot(units, down_ref[...], preferred_element_type=F32)
    tiles = out.shape[1] // LANES
    for t in range(tiles):
        out_ref[t] = out[:, t * LANES : (t + 1) * LANES].astype(BF)
    for t in range(tiles, out_ref.shape[0]):
        out_ref[t] = jnp.zeros(out_ref.shape[1:], BF)


def per_device(
    encoded,
    key_weight,
    value_weight,
    queries,
    state,
    out_weight,
    norm_gain,
    router,
    expert_ids,
    gate_weight,
    up_weight,
    down_weight,
):
    seq_count = lax.axis_size(SEQ)
    exp_count = lax.axis_size(EXP)
    groups = lax.axis_size("g")
    experts = lax.axis_size("e")
    dec_rows = state.shape[1]
    half = dec_rows // 2
    model_width = state.shape[2]
    block_width = model_width // groups
    tiles = block_width // LANES
    tile_slots = seq_count // 2
    head = key_weight.shape[2]
    hidden_here = gate_weight.shape[2]
    tokens = encoded.shape[1] * seq_count
    my_tile = lax.axis_index(CHIPS)
    my_core = lax.axis_index("c")
    my_expert = lax.axis_index("e")
    my_group = lax.axis_index("g")

    enc_all = lax.all_gather(encoded[0], SEQ, axis=0, tiled=True)
    first = jnp.concatenate([key_weight[0], value_weight[0]], axis=1)
    second = jnp.concatenate([key_weight[1], value_weight[1]], axis=1)
    own = lax.all_gather(first, "e", axis=0, tiled=True)
    second, own = lax.optimization_barrier((second, own))
    middle = own.shape[0] // 2
    left = shifted(own, exp_count, 1)
    right = shifted(own, exp_count, -1)
    far_left = shifted(left[:middle], exp_count, 1)
    far_right = shifted(right[middle:], exp_count, -1)
    blocks = [own, left, right, far_left, far_right]
    pieces = [
        (0, 0, experts),
        (-1, 0, experts),
        (1, 0, experts),
        (-2, 0, experts // 2),
        (2, experts // 2, experts),
    ]
    second_all = lax.all_gather(second, EXP, axis=0, tiled=True)

    whole = lambda shape: pl.BlockSpec(shape, lambda i, *_: (0,) * len(shape))
    cache_shape = jax.ShapeDtypeStruct((2, tokens, head), BF)
    key_cache, value_cache, terms = pl.pallas_call(
        functools.partial(attention_kernel, pieces, tiles, groups, experts),
        grid_spec=pltpu.PrefetchScalarGridSpec(
            num_scalar_prefetch=1,
            grid=(1,),
            in_specs=[whole(block.shape) for block in blocks]
            + [
                whole((dec_rows, head)),
                pl.BlockSpec(memory_space=pltpu.HBM),
                pl.BlockSpec(memory_space=pltpu.HBM),
            ],
            out_specs=[
                pl.BlockSpec((1, tokens, head), lambda i, *_: (0, 0, 0)),
                pl.BlockSpec((1, tokens, head), lambda i, *_: (0, 0, 0)),
                whole((seq_count, groups * half, LANES)),
            ],
            scratch_shapes=[
                pltpu.VMEM((model_width, 2 * head), BF),
                pltpu.VMEM((tokens, 2 * head), F32),
                pltpu.VMEM((tokens, model_width), BF),
                pltpu.VMEM(out_weight.shape, BF),
                pltpu.SemaphoreType.DMA((CHUNKS + 1,)),
            ],
        ),
        out_shape=[
            cache_shape,
            cache_shape,
            jax.ShapeDtypeStruct((seq_count, groups * half, LANES), BF),
        ],
        compiler_params=pltpu.CompilerParams(vmem_limit_bytes=48 * 1024 * 1024),
        name="project_attend",
    )(my_group.reshape(1), *blocks, queries[0], enc_all, out_weight)

    state_parts = state[0].astype(F32).reshape(2, half, groups, tiles, LANES)
    state_parts = jnp.pad(state_parts, ((0, 0), (0, 0), (0, 0), (0, tile_slots - tiles), (0, 0)))
    state_here = lax.dynamic_index_in_dim(state_parts, my_core, 0, keepdims=False)
    state_here = lax.dynamic_index_in_dim(state_here, my_tile, 2, keepdims=False).transpose(1, 0, 2)
    chosen = jnp.any(
        expert_ids[0][:, :, None] == jnp.arange(experts, dtype=jnp.int32), axis=1
    ).astype(F32)
    chosen = lax.dynamic_slice_in_dim(chosen, my_core * half, half, 0).T
    got = exchanged(terms, SEQ)
    attended = jnp.sum(got.astype(F32), axis=0).reshape(groups, half, LANES) + state_here
    routed = (attended[None] * chosen[:, None, :, None]).astype(BF)
    routed = exchanged(routed.reshape(exp_count, half, LANES), EXP)
    row_count = exp_count * dec_rows
    rows_all = spread(routed.reshape(exp_count * half, LANES), SEQ)
    rows_all = rows_all.reshape(tile_slots, row_count, LANES)
    gain = lax.dynamic_slice_in_dim(norm_gain, my_group * block_width, block_width, 0)
    routes = lax.dynamic_slice_in_dim(router.T, my_group * block_width, block_width, 1)
    gap = jnp.zeros((8 - experts, block_width), BF)
    routes = jnp.concatenate([routes, gap, routes, gap], axis=0)
    routes = jnp.pad(routes, ((0, WIDE - hidden_here - routes.shape[0]), (0, 0)))
    partial = pl.pallas_call(
        functools.partial(expert_input_kernel, hidden_here),
        grid=(1,),
        in_specs=[
            whole((tiles, row_count, LANES)),
            whole((1, block_width)),
            whole(routes.shape),
            whole((hidden_here, block_width)),
            whole((hidden_here, block_width)),
        ],
        out_specs=whole((row_count, 2 * WIDE)),
        out_shape=jax.ShapeDtypeStruct((row_count, 2 * WIDE), BF),
        scratch_shapes=[
            pltpu.VMEM((row_count, block_width), BF),
            pltpu.VMEM((WIDE, block_width), BF),
            pltpu.VMEM((WIDE, block_width), BF),
        ],
        compiler_params=pltpu.CompilerParams(vmem_limit_bytes=24 * 1024 * 1024),
        name="expert_input",
    )(
        rows_all,
        gain[None],
        routes,
        gate_weight[0].T,
        up_weight[0].T,
    )
    parts = lax.all_gather(partial, "g", axis=0)
    out = pl.pallas_call(
        functools.partial(expert_output_kernel, hidden_here, model_width),
        grid_spec=pltpu.PrefetchScalarGridSpec(
            num_scalar_prefetch=1,
            grid=(1,),
            in_specs=[whole(parts.shape), whole((hidden_here, block_width))],
            out_specs=whole((tile_slots, row_count, LANES)),
        ),
        out_shape=jax.ShapeDtypeStruct((tile_slots, row_count, LANES), BF),
        compiler_params=pltpu.CompilerParams(vmem_limit_bytes=24 * 1024 * 1024),
        name="expert_output",
    )(my_expert.reshape(1), parts, down_weight[0])
    out, second_all = lax.optimization_barrier((out, second_all))
    back = exchanged(out.reshape(seq_count, exp_count * half, LANES), SEQ)
    key_cache, value_cache = pl.pallas_call(
        second_kernel,
        grid=(1,),
        in_specs=[
            pl.BlockSpec(memory_space=pltpu.HBM),
            pl.BlockSpec(second_all.shape, lambda i: (0, 0)),
            pl.BlockSpec(memory_space=pl.ANY),
            pl.BlockSpec(memory_space=pl.ANY),
        ],
        out_specs=[pl.BlockSpec((1, tokens, head), lambda i: (1, 0, 0))] * 2,
        out_shape=[cache_shape, cache_shape],
        scratch_shapes=[
            pltpu.VMEM((tokens, 2 * head), F32),
            pltpu.VMEM((tokens, model_width), BF),
            pltpu.SemaphoreType.DMA((CHUNKS,)),
        ],
        cost_estimate=pl.CostEstimate(
            flops=4 * tokens * model_width * head,
            bytes_accessed=10 * tokens * model_width,
            transcendentals=0,
        ),
        input_output_aliases={2: 0, 3: 1},
        compiler_params=pltpu.CompilerParams(vmem_limit_bytes=48 * 1024 * 1024),
        name="project_second",
    )(enc_all, second_all, key_cache, value_cache)
    back, key_cache, value_cache = lax.optimization_barrier((back, key_cache, value_cache))
    back = jnp.sum(back.astype(F32), axis=0).astype(BF)
    back = exchanged(back.reshape(exp_count, half, LANES), EXP)
    back = jnp.sum(back.astype(F32).reshape(experts, groups, half, LANES), axis=0)
    mixed = (attended + back).astype(BF).reshape(groups * half, LANES)
    mixed = spread(mixed, SEQ)[: 2 * tiles].reshape(tiles, 2, groups, half, LANES)
    mixed = mixed.transpose(1, 3, 2, 0, 4).reshape(1, dec_rows, model_width)
    return key_cache[:, None], value_cache[:, None], mixed


def solution(mesh):
    fine = Mesh(mesh.devices.reshape(4, 4, 2, 4, 4), SEQ + EXP)
    return jax.shard_map(
        per_device,
        mesh=fine,
        in_specs=(
            P(EXP, SEQ, None),
            P(None, EXP, SEQ),
            P(None, EXP, SEQ),
            P(EXP, None, SEQ),
            P(EXP, None, None),
            P(SEQ, None),
            P(),
            P(),
            P(EXP, None, None),
            P(EXP, None, SEQ),
            P(EXP, None, SEQ),
            P(EXP, SEQ, None),
        ),
        out_specs=(P(None, EXP, None, SEQ), P(None, EXP, None, SEQ), P(EXP, None, None)),
        check_vma=False,
    )
```

```python
import functools
import math

import jax
import jax.numpy as jnp
from jax import lax
from jax.experimental import pallas as pl
from jax.experimental.pallas import tpu as pltpu
from jax.sharding import Mesh
from jax.sharding import PartitionSpec as P

EPS = 1e-06
SEQ = ("x", "y", "c")
CHIPS = ("x", "y")
EXP = ("e", "g")
LANES = 128
BF = jnp.bfloat16
F32 = jnp.float32
WIDE = 384


def shifted(x, count, by):
    return lax.ppermute(x, EXP, [(i, (i + by) % count) for i in range(count)])


def exchanged(x, axes):
    return lax.all_to_all(x, axes, split_axis=0, concat_axis=0, tiled=True)


def spread(x, axes):
    count = lax.axis_size(axes)
    return exchanged(jnp.broadcast_to(x[None], (count,) + x.shape), axes)


def order_kernel(pieces, groups, experts, group_ref, *refs):
    blocks, weight_ref = refs[:-1], refs[-1]
    rows = weight_ref.shape[0] // (groups * experts)
    for block, (offset, first, last) in zip(blocks, pieces):
        group = lax.rem(group_ref[0] + (groups + offset), groups)
        for e in range(first, last):
            at = pl.multiple_of((e * groups + group) * rows, 64)
            weight_ref[pl.ds(at, rows), :] = block[(e - first) * rows : (e - first + 1) * rows, :]


def attention_kernel(tiles, groups, query_ref, pair_ref, out_ref, key_ref, value_ref, term_ref):
    head = key_ref.shape[-1]
    key_ref[0] = pair_ref[:, :head]
    value_ref[0] = pair_ref[:, head:]
    scores = lax.dot_general(
        query_ref[...], key_ref[0], (((1,), (1,)), ((), ())), preferred_element_type=F32
    ) / math.sqrt(head)
    raised = jnp.exp(scores - jnp.max(scores, axis=-1, keepdims=True))
    attn = (raised / jnp.sum(raised, axis=-1, keepdims=True)).astype(BF)
    context = jnp.dot(attn, value_ref[0], preferred_element_type=F32).astype(BF)
    half = query_ref.shape[0] // 2
    for t in range(tiles):
        parts = [
            jnp.dot(
                context,
                out_ref[:, (g * tiles + t) * LANES : (g * tiles + t + 1) * LANES],
                preferred_element_type=F32,
            )
            for g in range(groups)
        ]
        for h in range(2):
            term_ref[2 * t + h] = jnp.concatenate(
                [p[h * half : (h + 1) * half] for p in parts], axis=0
            ).astype(BF)
    for s in range(2 * tiles, term_ref.shape[0]):
        term_ref[s] = jnp.zeros(term_ref.shape[1:], BF)


def second_kernel(pair_ref, key_in, value_in, key_ref, value_ref):
    head = key_ref.shape[-1]
    key_ref[0] = pair_ref[:, :head]
    value_ref[0] = pair_ref[:, head:]


def expert_input_kernel(
    hidden, rows_ref, gain_ref, router_ref, gate_ref, up_ref, part_ref, x_ref, gate_all, up_all
):
    tiles = rows_ref.shape[0]
    wide = gate_all.shape[0]
    squares = None
    for t in range(tiles):
        x = rows_ref[t].astype(F32)
        term = jnp.sum(x * x, axis=1, keepdims=True)
        squares = term if squares is None else squares + term
        gain = gain_ref[:, t * LANES : (t + 1) * LANES]
        x_ref[:, t * LANES : (t + 1) * LANES] = (x * gain).astype(BF)
    gate_all[:hidden] = gate_ref[...]
    gate_all[hidden:] = router_ref[...]
    up_all[:hidden] = up_ref[...]
    up_all[hidden:] = jnp.zeros((wide - hidden, up_all.shape[1]), BF)
    contract = (((1,), (1,)), ((), ()))
    gate = lax.dot_general(x_ref[...], gate_all[...], contract, preferred_element_type=F32)
    lane = lax.broadcasted_iota(jnp.int32, gate.shape, 1)
    gate = jnp.where((lane == hidden + 4) | (lane == hidden + 12), squares, gate)
    high = gate.astype(BF)
    low = (gate - high.astype(F32)).astype(BF)
    part_ref[:, :wide] = jnp.where(lane >= hidden + 8, low.astype(F32), high.astype(F32)).astype(BF)
    up = lax.dot_general(x_ref[...], up_all[...], contract, preferred_element_type=F32)
    part_ref[:, wide:] = up.astype(BF)


def expert_output_kernel(hidden, width, expert_ref, part_ref, down_ref, out_ref):
    total = part_ref[0].astype(F32)
    for k in range(1, part_ref.shape[0]):
        total = total + part_ref[k].astype(F32)
    wide = total.shape[1] // 2
    gate, lifted = total[:, :wide], total[:, wide:]

    def column(j):
        return gate[:, hidden + j : hidden + j + 1] + gate[:, hidden + 8 + j : hidden + 9 + j]

    scale = lax.rsqrt(column(4) / width + EPS)
    logits = [column(j) * scale for j in range(4)]
    top = functools.reduce(jnp.maximum, logits)
    raised = [jnp.exp(logit - top) for logit in logits]
    mine = [jnp.where(expert_ref[0] == j, raised[j], 0.0) for j in range(4)]
    share = sum(mine) / sum(raised)
    gate = gate * scale
    active = 0.5 * gate * (1.0 + jnp.tanh(math.sqrt(2 / math.pi) * (gate + 0.044715 * gate**3)))
    units = (active * (lifted * scale) * share)[:, :hidden].astype(BF)
    out = jnp.dot(units, down_ref[...], preferred_element_type=F32)
    tiles = out.shape[1] // LANES
    for t in range(tiles):
        out_ref[t] = out[:, t * LANES : (t + 1) * LANES].astype(BF)
    for t in range(tiles, out_ref.shape[0]):
        out_ref[t] = jnp.zeros(out_ref.shape[1:], BF)


def per_device(
    encoded,
    key_weight,
    value_weight,
    queries,
    state,
    out_weight,
    norm_gain,
    router,
    expert_ids,
    gate_weight,
    up_weight,
    down_weight,
):
    seq_count = lax.axis_size(SEQ)
    exp_count = lax.axis_size(EXP)
    groups = lax.axis_size("g")
    experts = lax.axis_size("e")
    dec_rows = state.shape[1]
    half = dec_rows // 2
    model_width = state.shape[2]
    block_width = model_width // groups
    tiles = block_width // LANES
    tile_slots = seq_count // 2
    head = key_weight.shape[2]
    hidden_here = gate_weight.shape[2]
    tokens = encoded.shape[1] * seq_count
    my_tile = lax.axis_index(CHIPS)
    my_core = lax.axis_index("c")
    my_expert = lax.axis_index("e")
    my_group = lax.axis_index("g")

    enc_all = lax.all_gather(encoded[0], SEQ, axis=0, tiled=True)
    first = jnp.concatenate([key_weight[0], value_weight[0]], axis=1)
    second = jnp.concatenate([key_weight[1], value_weight[1]], axis=1)
    own = lax.all_gather(first, "e", axis=0, tiled=True)
    second, own = lax.optimization_barrier((second, own))
    middle = own.shape[0] // 2
    left = shifted(own, exp_count, 1)
    right = shifted(own, exp_count, -1)
    far_left = shifted(left[:middle], exp_count, 1)
    far_right = shifted(right[middle:], exp_count, -1)
    blocks = [own, left, right, far_left, far_right]
    pieces = [
        (0, 0, experts),
        (-1, 0, experts),
        (1, 0, experts),
        (-2, 0, experts // 2),
        (2, experts // 2, experts),
    ]
    second_all = lax.all_gather(second, EXP, axis=0, tiled=True)

    whole = lambda shape: pl.BlockSpec(shape, lambda i, *_: (0,) * len(shape))
    cache_shape = jax.ShapeDtypeStruct((2, tokens, head), BF)
    ordered = pl.pallas_call(
        functools.partial(order_kernel, pieces, groups, experts),
        grid_spec=pltpu.PrefetchScalarGridSpec(
            num_scalar_prefetch=1,
            grid=(1,),
            in_specs=[whole(block.shape) for block in blocks],
            out_specs=whole((model_width, 2 * head)),
        ),
        out_shape=jax.ShapeDtypeStruct((model_width, 2 * head), BF),
        compiler_params=pltpu.CompilerParams(vmem_limit_bytes=24 * 1024 * 1024),
        name="order_weights",
    )(my_group.reshape(1), *blocks)
    pair = jnp.dot(enc_all, ordered, preferred_element_type=F32).astype(BF)
    key_cache, value_cache, terms = pl.pallas_call(
        functools.partial(attention_kernel, tiles, groups),
        grid=(1,),
        in_specs=[whole((dec_rows, head)), whole(pair.shape), whole(out_weight.shape)],
        out_specs=[
            pl.BlockSpec((1, tokens, head), lambda i: (0, 0, 0)),
            pl.BlockSpec((1, tokens, head), lambda i: (0, 0, 0)),
            whole((seq_count, groups * half, LANES)),
        ],
        out_shape=[
            cache_shape,
            cache_shape,
            jax.ShapeDtypeStruct((seq_count, groups * half, LANES), BF),
        ],
        compiler_params=pltpu.CompilerParams(vmem_limit_bytes=16 * 1024 * 1024),
        name="attend",
    )(queries[0], pair, out_weight)

    state_parts = state[0].astype(F32).reshape(2, half, groups, tiles, LANES)
    state_parts = jnp.pad(state_parts, ((0, 0), (0, 0), (0, 0), (0, tile_slots - tiles), (0, 0)))
    state_here = lax.dynamic_index_in_dim(state_parts, my_core, 0, keepdims=False)
    state_here = lax.dynamic_index_in_dim(state_here, my_tile, 2, keepdims=False).transpose(1, 0, 2)
    chosen = jnp.any(
        expert_ids[0][:, :, None] == jnp.arange(experts, dtype=jnp.int32), axis=1
    ).astype(F32)
    chosen = lax.dynamic_slice_in_dim(chosen, my_core * half, half, 0).T
    got = exchanged(terms, SEQ)
    attended = jnp.sum(got.astype(F32), axis=0).reshape(groups, half, LANES) + state_here
    routed = (attended[None] * chosen[:, None, :, None]).astype(BF)
    routed = exchanged(routed.reshape(exp_count, half, LANES), EXP)
    row_count = exp_count * dec_rows
    rows_all = spread(routed.reshape(exp_count * half, LANES), SEQ)
    rows_all = rows_all.reshape(tile_slots, row_count, LANES)
    gain = lax.dynamic_slice_in_dim(norm_gain, my_group * block_width, block_width, 0)
    routes = lax.dynamic_slice_in_dim(router.T, my_group * block_width, block_width, 1)
    gap = jnp.zeros((8 - experts, block_width), BF)
    routes = jnp.concatenate([routes, gap, routes, gap], axis=0)
    routes = jnp.pad(routes, ((0, WIDE - hidden_here - routes.shape[0]), (0, 0)))
    partial = pl.pallas_call(
        functools.partial(expert_input_kernel, hidden_here),
        grid=(1,),
        in_specs=[
            whole((tiles, row_count, LANES)),
            whole((1, block_width)),
            whole(routes.shape),
            whole((hidden_here, block_width)),
            whole((hidden_here, block_width)),
        ],
        out_specs=whole((row_count, 2 * WIDE)),
        out_shape=jax.ShapeDtypeStruct((row_count, 2 * WIDE), BF),
        scratch_shapes=[
            pltpu.VMEM((row_count, block_width), BF),
            pltpu.VMEM((WIDE, block_width), BF),
            pltpu.VMEM((WIDE, block_width), BF),
        ],
        compiler_params=pltpu.CompilerParams(vmem_limit_bytes=24 * 1024 * 1024),
        name="expert_input",
    )(
        rows_all,
        gain[None],
        routes,
        gate_weight[0].T,
        up_weight[0].T,
    )
    parts = lax.all_gather(partial, "g", axis=0)
    out = pl.pallas_call(
        functools.partial(expert_output_kernel, hidden_here, model_width),
        grid_spec=pltpu.PrefetchScalarGridSpec(
            num_scalar_prefetch=1,
            grid=(1,),
            in_specs=[whole(parts.shape), whole((hidden_here, block_width))],
            out_specs=whole((tile_slots, row_count, LANES)),
        ),
        out_shape=jax.ShapeDtypeStruct((tile_slots, row_count, LANES), BF),
        compiler_params=pltpu.CompilerParams(vmem_limit_bytes=24 * 1024 * 1024),
        name="expert_output",
    )(my_expert.reshape(1), parts, down_weight[0])
    out, second_all = lax.optimization_barrier((out, second_all))
    back = exchanged(out.reshape(seq_count, exp_count * half, LANES), SEQ)
    second_pair = jnp.dot(enc_all, second_all, preferred_element_type=F32).astype(BF)
    key_cache, value_cache = pl.pallas_call(
        second_kernel,
        grid=(1,),
        in_specs=[
            pl.BlockSpec(second_pair.shape, lambda i: (0, 0)),
            pl.BlockSpec(memory_space=pl.ANY),
            pl.BlockSpec(memory_space=pl.ANY),
        ],
        out_specs=[pl.BlockSpec((1, tokens, head), lambda i: (1, 0, 0))] * 2,
        out_shape=[cache_shape, cache_shape],
        input_output_aliases={1: 0, 2: 1},
        compiler_params=pltpu.CompilerParams(vmem_limit_bytes=8 * 1024 * 1024),
        name="store_second",
    )(second_pair, key_cache, value_cache)
    back, key_cache, value_cache = lax.optimization_barrier((back, key_cache, value_cache))
    back = jnp.sum(back.astype(F32), axis=0).astype(BF)
    back = exchanged(back.reshape(exp_count, half, LANES), EXP)
    back = jnp.sum(back.astype(F32).reshape(experts, groups, half, LANES), axis=0)
    mixed = (attended + back).astype(BF).reshape(groups * half, LANES)
    mixed = spread(mixed, SEQ)[: 2 * tiles].reshape(tiles, 2, groups, half, LANES)
    mixed = mixed.transpose(1, 3, 2, 0, 4).reshape(1, dec_rows, model_width)
    return key_cache[:, None], value_cache[:, None], mixed


def solution(mesh):
    fine = Mesh(mesh.devices.reshape(4, 4, 2, 4, 4), SEQ + EXP)
    return jax.shard_map(
        per_device,
        mesh=fine,
        in_specs=(
            P(EXP, SEQ, None),
            P(None, EXP, SEQ),
            P(None, EXP, SEQ),
            P(EXP, None, SEQ),
            P(EXP, None, None),
            P(SEQ, None),
            P(),
            P(),
            P(EXP, None, None),
            P(EXP, None, SEQ),
            P(EXP, None, SEQ),
            P(EXP, SEQ, None),
        ),
        out_specs=(P(None, EXP, None, SEQ), P(None, EXP, None, SEQ), P(EXP, None, None)),
        check_vma=False,
    )
```

```python
import functools
import math

import jax
import jax.numpy as jnp
from jax import lax
from jax.experimental import pallas as pl
from jax.experimental.pallas import tpu as pltpu
from jax.sharding import Mesh
from jax.sharding import PartitionSpec as P

EPS = 1e-06
SEQ = ("x", "y", "c")
CHIPS = ("x", "y")
EXP = ("e", "g")
LANES = 128
BF = jnp.bfloat16
F32 = jnp.float32
WIDE = 384
CAP = 6


def shifted(x, count, by):
    return lax.ppermute(x, EXP, [(i, (i + by) % count) for i in range(count)])


def exchanged(x, axes):
    return lax.all_to_all(x, axes, split_axis=0, concat_axis=0, tiled=True)


def spread(x, axes):
    count = lax.axis_size(axes)
    return exchanged(jnp.broadcast_to(x[None], (count,) + x.shape), axes)


def order_kernel(pieces, groups, experts, group_ref, *refs):
    blocks, weight_ref = refs[:-1], refs[-1]
    rows = weight_ref.shape[0] // (groups * experts)
    for block, (offset, first, last) in zip(blocks, pieces):
        group = lax.rem(group_ref[0] + (groups + offset), groups)
        for e in range(first, last):
            at = pl.multiple_of((e * groups + group) * rows, 64)
            weight_ref[pl.ds(at, rows), :] = block[(e - first) * rows : (e - first + 1) * rows, :]


def attention_kernel(tiles, groups, query_ref, pair_ref, out_ref, key_ref, value_ref, term_ref):
    head = key_ref.shape[-1]
    key_ref[0] = pair_ref[:, :head]
    value_ref[0] = pair_ref[:, head:]
    scores = lax.dot_general(
        query_ref[...], key_ref[0], (((1,), (1,)), ((), ())), preferred_element_type=F32
    ) / math.sqrt(head)
    raised = jnp.exp(scores - jnp.max(scores, axis=-1, keepdims=True))
    attn = (raised / jnp.sum(raised, axis=-1, keepdims=True)).astype(BF)
    context = jnp.dot(attn, value_ref[0], preferred_element_type=F32).astype(BF)
    half = query_ref.shape[0] // 2
    for t in range(tiles):
        parts = [
            jnp.dot(
                context,
                out_ref[:, (g * tiles + t) * LANES : (g * tiles + t + 1) * LANES],
                preferred_element_type=F32,
            )
            for g in range(groups)
        ]
        for h in range(2):
            term_ref[2 * t + h] = jnp.concatenate(
                [p[h * half : (h + 1) * half] for p in parts], axis=0
            ).astype(BF)
    for s in range(2 * tiles, term_ref.shape[0]):
        term_ref[s] = jnp.zeros(term_ref.shape[1:], BF)


def second_kernel(pair_ref, key_in, value_in, key_ref, value_ref):
    head = key_ref.shape[-1]
    key_ref[0] = pair_ref[:, :head]
    value_ref[0] = pair_ref[:, head:]


def selection(slots, target_ref):
    place = lax.broadcasted_iota(jnp.int32, (slots, target_ref.shape[1]), 0).astype(F32)
    return jnp.where(place == target_ref[...], 1.0, 0.0).astype(BF)


def expert_input_kernel(
    hidden,
    rows_ref,
    target_ref,
    gain_ref,
    router_ref,
    gate_ref,
    up_ref,
    part_ref,
    x_ref,
    gate_all,
    up_all,
):
    tiles = rows_ref.shape[0]
    wide = gate_all.shape[0]
    select = selection(x_ref.shape[0], target_ref)
    squares = None
    for t in range(tiles):
        x = jnp.dot(select, rows_ref[t], preferred_element_type=F32)
        term = jnp.sum(x * x, axis=1, keepdims=True)
        squares = term if squares is None else squares + term
        gain = gain_ref[:, t * LANES : (t + 1) * LANES]
        x_ref[:, t * LANES : (t + 1) * LANES] = (x * gain).astype(BF)
    gate_all[:hidden] = gate_ref[...]
    gate_all[hidden:] = router_ref[...]
    up_all[:hidden] = up_ref[...]
    up_all[hidden:] = jnp.zeros((wide - hidden, up_all.shape[1]), BF)
    contract = (((1,), (1,)), ((), ()))
    gate = lax.dot_general(x_ref[...], gate_all[...], contract, preferred_element_type=F32)
    lane = lax.broadcasted_iota(jnp.int32, gate.shape, 1)
    gate = jnp.where((lane == hidden + 4) | (lane == hidden + 12), squares, gate)
    high = gate.astype(BF)
    low = (gate - high.astype(F32)).astype(BF)
    part_ref[:, :wide] = jnp.where(lane >= hidden + 8, low.astype(F32), high.astype(F32)).astype(BF)
    up = lax.dot_general(x_ref[...], up_all[...], contract, preferred_element_type=F32)
    part_ref[:, wide:] = up.astype(BF)


def expert_output_kernel(hidden, width, expert_ref, part_ref, target_ref, down_ref, out_ref):
    total = part_ref[0].astype(F32)
    for k in range(1, part_ref.shape[0]):
        total = total + part_ref[k].astype(F32)
    wide = total.shape[1] // 2
    gate, lifted = total[:, :wide], total[:, wide:]

    def column(j):
        return gate[:, hidden + j : hidden + j + 1] + gate[:, hidden + 8 + j : hidden + 9 + j]

    scale = lax.rsqrt(column(4) / width + EPS)
    logits = [column(j) * scale for j in range(4)]
    top = functools.reduce(jnp.maximum, logits)
    raised = [jnp.exp(logit - top) for logit in logits]
    mine = [jnp.where(expert_ref[0] == j, raised[j], 0.0) for j in range(4)]
    share = sum(mine) / sum(raised)
    gate = gate * scale
    active = 0.5 * gate * (1.0 + jnp.tanh(math.sqrt(2 / math.pi) * (gate + 0.044715 * gate**3)))
    units = (active * (lifted * scale) * share)[:, :hidden].astype(BF)
    select = selection(units.shape[0], target_ref)
    units = lax.dot_general(select, units, (((0,), (0,)), ((), ())), preferred_element_type=F32)
    out = jnp.dot(units.astype(BF), down_ref[...], preferred_element_type=F32)
    tiles = out.shape[1] // LANES
    for t in range(tiles):
        out_ref[t] = out[:, t * LANES : (t + 1) * LANES].astype(BF)
    for t in range(tiles, out_ref.shape[0]):
        out_ref[t] = jnp.zeros(out_ref.shape[1:], BF)


def per_device(
    encoded,
    key_weight,
    value_weight,
    queries,
    state,
    out_weight,
    norm_gain,
    router,
    expert_ids,
    gate_weight,
    up_weight,
    down_weight,
):
    seq_count = lax.axis_size(SEQ)
    exp_count = lax.axis_size(EXP)
    groups = lax.axis_size("g")
    experts = lax.axis_size("e")
    dec_rows = state.shape[1]
    half = dec_rows // 2
    model_width = state.shape[2]
    block_width = model_width // groups
    tiles = block_width // LANES
    tile_slots = seq_count // 2
    head = key_weight.shape[2]
    hidden_here = gate_weight.shape[2]
    tokens = encoded.shape[1] * seq_count
    my_tile = lax.axis_index(CHIPS)
    my_core = lax.axis_index("c")
    my_expert = lax.axis_index("e")
    my_group = lax.axis_index("g")

    enc_all = lax.all_gather(encoded[0], SEQ, axis=0, tiled=True)
    first = jnp.concatenate([key_weight[0], value_weight[0]], axis=1)
    second = jnp.concatenate([key_weight[1], value_weight[1]], axis=1)
    own = lax.all_gather(first, "e", axis=0, tiled=True)
    second, own = lax.optimization_barrier((second, own))
    middle = own.shape[0] // 2
    left = shifted(own, exp_count, 1)
    right = shifted(own, exp_count, -1)
    far_left = shifted(left[:middle], exp_count, 1)
    far_right = shifted(right[middle:], exp_count, -1)
    blocks = [own, left, right, far_left, far_right]
    pieces = [
        (0, 0, experts),
        (-1, 0, experts),
        (1, 0, experts),
        (-2, 0, experts // 2),
        (2, experts // 2, experts),
    ]
    second_all = lax.all_gather(second, EXP, axis=0, tiled=True)

    whole = lambda shape: pl.BlockSpec(shape, lambda i, *_: (0,) * len(shape))
    cache_shape = jax.ShapeDtypeStruct((2, tokens, head), BF)
    ordered = pl.pallas_call(
        functools.partial(order_kernel, pieces, groups, experts),
        grid_spec=pltpu.PrefetchScalarGridSpec(
            num_scalar_prefetch=1,
            grid=(1,),
            in_specs=[whole(block.shape) for block in blocks],
            out_specs=whole((model_width, 2 * head)),
        ),
        out_shape=jax.ShapeDtypeStruct((model_width, 2 * head), BF),
        compiler_params=pltpu.CompilerParams(vmem_limit_bytes=24 * 1024 * 1024),
        name="order_weights",
    )(my_group.reshape(1), *blocks)
    pair = jnp.dot(enc_all, ordered, preferred_element_type=F32).astype(BF)
    key_cache, value_cache, terms = pl.pallas_call(
        functools.partial(attention_kernel, tiles, groups),
        grid=(1,),
        in_specs=[whole((dec_rows, head)), whole(pair.shape), whole(out_weight.shape)],
        out_specs=[
            pl.BlockSpec((1, tokens, head), lambda i: (0, 0, 0)),
            pl.BlockSpec((1, tokens, head), lambda i: (0, 0, 0)),
            whole((seq_count, groups * half, LANES)),
        ],
        out_shape=[
            cache_shape,
            cache_shape,
            jax.ShapeDtypeStruct((seq_count, groups * half, LANES), BF),
        ],
        compiler_params=pltpu.CompilerParams(vmem_limit_bytes=16 * 1024 * 1024),
        name="attend",
    )(queries[0], pair, out_weight)

    state_parts = state[0].astype(F32).reshape(2, half, groups, tiles, LANES)
    state_parts = jnp.pad(state_parts, ((0, 0), (0, 0), (0, 0), (0, tile_slots - tiles), (0, 0)))
    state_here = lax.dynamic_index_in_dim(state_parts, my_core, 0, keepdims=False)
    state_here = lax.dynamic_index_in_dim(state_here, my_tile, 2, keepdims=False).transpose(1, 0, 2)
    chosen = jnp.any(
        expert_ids[0][:, :, None] == jnp.arange(experts, dtype=jnp.int32), axis=1
    ).astype(F32)
    flags = jnp.pad(chosen.T, ((0, 0), (0, LANES - dec_rows)))
    flags = jnp.broadcast_to(flags[:, None, None], (experts, groups, 1, LANES))
    flags = jnp.pad(flags, ((0, 0), (0, 0), (0, half - 1), (0, 0)))
    chosen = lax.dynamic_slice_in_dim(chosen, my_core * half, half, 0).T
    got = exchanged(terms, SEQ)
    attended = jnp.sum(got.astype(F32), axis=0).reshape(groups, half, LANES) + state_here
    routed = jnp.concatenate([attended[None] * chosen[:, None, :, None], flags], axis=2)
    routed = exchanged(routed.astype(BF).reshape(exp_count, 2 * half, LANES), EXP)
    row_count = exp_count * dec_rows
    rows_all = spread(routed[:, :half].reshape(exp_count * half, LANES), SEQ)
    rows_all = rows_all.reshape(tile_slots, row_count, LANES)
    flags = routed[:, half, :dec_rows].astype(F32)
    before = jnp.triu(jnp.ones((dec_rows, dec_rows), F32), 1)
    target = jnp.dot(flags, before) + CAP * jnp.arange(exp_count, dtype=F32)[:, None]
    target = jnp.where(flags > 0.5, target, -1.0)
    target = target.reshape(exp_count, 2, half).transpose(1, 0, 2).reshape(1, row_count)
    slot_count = exp_count * CAP
    gain = lax.dynamic_slice_in_dim(norm_gain, my_group * block_width, block_width, 0)
    routes = lax.dynamic_slice_in_dim(router.T, my_group * block_width, block_width, 1)
    gap = jnp.zeros((8 - experts, block_width), BF)
    routes = jnp.concatenate([routes, gap, routes, gap], axis=0)
    routes = jnp.pad(routes, ((0, WIDE - hidden_here - routes.shape[0]), (0, 0)))
    partial = pl.pallas_call(
        functools.partial(expert_input_kernel, hidden_here),
        grid=(1,),
        in_specs=[
            whole((tiles, row_count, LANES)),
            whole(target.shape),
            whole((1, block_width)),
            whole(routes.shape),
            whole((hidden_here, block_width)),
            whole((hidden_here, block_width)),
        ],
        out_specs=whole((slot_count, 2 * WIDE)),
        out_shape=jax.ShapeDtypeStruct((slot_count, 2 * WIDE), BF),
        scratch_shapes=[
            pltpu.VMEM((slot_count, block_width), BF),
            pltpu.VMEM((WIDE, block_width), BF),
            pltpu.VMEM((WIDE, block_width), BF),
        ],
        compiler_params=pltpu.CompilerParams(vmem_limit_bytes=24 * 1024 * 1024),
        name="expert_input",
    )(
        rows_all,
        target,
        gain[None],
        routes,
        gate_weight[0].T,
        up_weight[0].T,
    )
    parts = lax.all_gather(partial, "g", axis=0)
    out = pl.pallas_call(
        functools.partial(expert_output_kernel, hidden_here, model_width),
        grid_spec=pltpu.PrefetchScalarGridSpec(
            num_scalar_prefetch=1,
            grid=(1,),
            in_specs=[
                whole(parts.shape),
                whole(target.shape),
                whole((hidden_here, block_width)),
            ],
            out_specs=whole((tile_slots, row_count, LANES)),
        ),
        out_shape=jax.ShapeDtypeStruct((tile_slots, row_count, LANES), BF),
        compiler_params=pltpu.CompilerParams(vmem_limit_bytes=24 * 1024 * 1024),
        name="expert_output",
    )(my_expert.reshape(1), parts, target, down_weight[0])
    out, second_all = lax.optimization_barrier((out, second_all))
    back = exchanged(out.reshape(seq_count, exp_count * half, LANES), SEQ)
    second_pair = jnp.dot(enc_all, second_all, preferred_element_type=F32).astype(BF)
    key_cache, value_cache = pl.pallas_call(
        second_kernel,
        grid=(1,),
        in_specs=[
            pl.BlockSpec(second_pair.shape, lambda i: (0, 0)),
            pl.BlockSpec(memory_space=pl.ANY),
            pl.BlockSpec(memory_space=pl.ANY),
        ],
        out_specs=[pl.BlockSpec((1, tokens, head), lambda i: (1, 0, 0))] * 2,
        out_shape=[cache_shape, cache_shape],
        input_output_aliases={1: 0, 2: 1},
        compiler_params=pltpu.CompilerParams(vmem_limit_bytes=8 * 1024 * 1024),
        name="store_second",
    )(second_pair, key_cache, value_cache)
    back, key_cache, value_cache = lax.optimization_barrier((back, key_cache, value_cache))
    back = jnp.sum(back.astype(F32), axis=0).astype(BF)
    back = exchanged(back.reshape(exp_count, half, LANES), EXP)
    back = jnp.sum(back.astype(F32).reshape(experts, groups, half, LANES), axis=0)
    mixed = (attended + back).astype(BF).reshape(groups * half, LANES)
    mixed = spread(mixed, SEQ)[: 2 * tiles].reshape(tiles, 2, groups, half, LANES)
    mixed = mixed.transpose(1, 3, 2, 0, 4).reshape(1, dec_rows, model_width)
    return key_cache[:, None], value_cache[:, None], mixed


def solution(mesh):
    fine = Mesh(mesh.devices.reshape(4, 4, 2, 4, 4), SEQ + EXP)
    return jax.shard_map(
        per_device,
        mesh=fine,
        in_specs=(
            P(EXP, SEQ, None),
            P(None, EXP, SEQ),
            P(None, EXP, SEQ),
            P(EXP, None, SEQ),
            P(EXP, None, None),
            P(SEQ, None),
            P(),
            P(),
            P(EXP, None, None),
            P(EXP, None, SEQ),
            P(EXP, None, SEQ),
            P(EXP, SEQ, None),
        ),
        out_specs=(P(None, EXP, None, SEQ), P(None, EXP, None, SEQ), P(EXP, None, None)),
        check_vma=False,
    )
```

```python
import functools
import math

import jax
import jax.numpy as jnp
from jax import lax
from jax.experimental import pallas as pl
from jax.experimental.pallas import tpu as pltpu
from jax.sharding import Mesh
from jax.sharding import PartitionSpec as P

EPS = 1e-06
SEQ = ("x", "y", "c")
CHIPS = ("x", "y")
EXP = ("e", "g")
LANES = 128
BF = jnp.bfloat16
F32 = jnp.float32
WIDE = 384
CAP = 6
TOP = 2
PAIRS = 3
EACH = CAP // PAIRS


def shifted(x, count, by):
    return lax.ppermute(x, EXP, [(i, (i + by) % count) for i in range(count)])


def exchanged(x, axes):
    return lax.all_to_all(x, axes, split_axis=0, concat_axis=0, tiled=True)


def spread(x, axes):
    count = lax.axis_size(axes)
    return exchanged(jnp.broadcast_to(x[None], (count,) + x.shape), axes)


def order_kernel(pieces, groups, experts, group_ref, *refs):
    blocks, weight_ref = refs[:-1], refs[-1]
    rows = weight_ref.shape[0] // (groups * experts)
    for block, (offset, first, last) in zip(blocks, pieces):
        group = lax.rem(group_ref[0] + (groups + offset), groups)
        for e in range(first, last):
            at = pl.multiple_of((e * groups + group) * rows, 64)
            weight_ref[pl.ds(at, rows), :] = block[(e - first) * rows : (e - first + 1) * rows, :]


def attention_kernel(
    tiles, groups, query_ref, pair_ref, pick_ref, out_ref, key_ref, value_ref, term_ref
):
    head = key_ref.shape[-1]
    key_ref[0] = pair_ref[:, :head]
    value_ref[0] = pair_ref[:, head:]
    scores = lax.dot_general(
        query_ref[...], key_ref[0], (((1,), (1,)), ((), ())), preferred_element_type=F32
    ) / math.sqrt(head)
    raised = jnp.exp(scores - jnp.max(scores, axis=-1, keepdims=True))
    attn = (raised / jnp.sum(raised, axis=-1, keepdims=True)).astype(BF)
    context = jnp.dot(attn, value_ref[0], preferred_element_type=F32).astype(BF)
    context = jnp.dot(pick_ref[...], context, preferred_element_type=F32).astype(BF)
    rows = context.shape[0] // PAIRS
    for t in range(tiles):
        parts = [
            jnp.dot(
                context,
                out_ref[:, (g * tiles + t) * LANES : (g * tiles + t + 1) * LANES],
                preferred_element_type=F32,
            )
            for g in range(groups)
        ]
        for k in range(PAIRS):
            term_ref[PAIRS * t + k] = jnp.concatenate(
                [p[k * rows : (k + 1) * rows] for p in parts], axis=0
            ).astype(BF)
    for s in range(PAIRS * tiles, term_ref.shape[0]):
        term_ref[s] = jnp.zeros(term_ref.shape[1:], BF)


def second_kernel(pair_ref, key_in, value_in, key_ref, value_ref):
    head = key_ref.shape[-1]
    key_ref[0] = pair_ref[:, :head]
    value_ref[0] = pair_ref[:, head:]


def expert_input_kernel(
    hidden, rows_ref, gain_ref, router_ref, gate_ref, up_ref, part_ref, x_ref, gate_all, up_all
):
    tiles = x_ref.shape[1] // LANES
    wide = gate_all.shape[0]
    squares = None
    for t in range(tiles):
        x = jnp.concatenate([rows_ref[PAIRS * t + k] for k in range(PAIRS)], axis=0).astype(F32)
        term = jnp.sum(x * x, axis=1, keepdims=True)
        squares = term if squares is None else squares + term
        gain = gain_ref[:, t * LANES : (t + 1) * LANES]
        x_ref[:, t * LANES : (t + 1) * LANES] = (x * gain).astype(BF)
    gate_all[:hidden] = gate_ref[...]
    gate_all[hidden:] = router_ref[...]
    up_all[:hidden] = up_ref[...]
    up_all[hidden:] = jnp.zeros((wide - hidden, up_all.shape[1]), BF)
    contract = (((1,), (1,)), ((), ()))
    gate = lax.dot_general(x_ref[...], gate_all[...], contract, preferred_element_type=F32)
    lane = lax.broadcasted_iota(jnp.int32, gate.shape, 1)
    gate = jnp.where((lane == hidden + 4) | (lane == hidden + 12), squares, gate)
    high = gate.astype(BF)
    low = (gate - high.astype(F32)).astype(BF)
    part_ref[:, :wide] = jnp.where(lane >= hidden + 8, low.astype(F32), high.astype(F32)).astype(BF)
    up = lax.dot_general(x_ref[...], up_all[...], contract, preferred_element_type=F32)
    part_ref[:, wide:] = up.astype(BF)


def expert_output_kernel(hidden, width, expert_ref, part_ref, down_ref, out_ref):
    total = part_ref[0].astype(F32)
    for k in range(1, part_ref.shape[0]):
        total = total + part_ref[k].astype(F32)
    wide = total.shape[1] // 2
    gate, lifted = total[:, :wide], total[:, wide:]

    def column(j):
        return gate[:, hidden + j : hidden + j + 1] + gate[:, hidden + 8 + j : hidden + 9 + j]

    scale = lax.rsqrt(column(4) / width + EPS)
    logits = [column(j) * scale for j in range(4)]
    top = functools.reduce(jnp.maximum, logits)
    raised = [jnp.exp(logit - top) for logit in logits]
    mine = [jnp.where(expert_ref[0] == j, raised[j], 0.0) for j in range(4)]
    share = sum(mine) / sum(raised)
    gate = gate * scale
    active = 0.5 * gate * (1.0 + jnp.tanh(math.sqrt(2 / math.pi) * (gate + 0.044715 * gate**3)))
    units = (active * (lifted * scale) * share)[:, :hidden].astype(BF)
    out = jnp.dot(units, down_ref[...], preferred_element_type=F32).astype(BF)
    tiles = out.shape[1] // LANES
    rows = out_ref.shape[1]
    for t in range(tiles):
        for k in range(PAIRS):
            out_ref[PAIRS * t + k] = out[k * rows : (k + 1) * rows, t * LANES : (t + 1) * LANES]
    for s in range(PAIRS * tiles, out_ref.shape[0]):
        out_ref[s] = jnp.zeros(out_ref.shape[1:], BF)


def rows_kernel(tiles, groups, parts_ref, place_ref, out_ref):
    rows = out_ref.shape[0]
    for t in range(tiles):
        parts = jnp.concatenate([parts_ref[PAIRS * t + k] for k in range(PAIRS)], axis=0)
        placed = jnp.dot(place_ref[...], parts, preferred_element_type=F32)
        for g in range(groups):
            at = (g * tiles + t) * LANES
            out_ref[:, at : at + LANES] = placed[g * rows : (g + 1) * rows].astype(BF)


def per_device(
    encoded,
    key_weight,
    value_weight,
    queries,
    state,
    out_weight,
    norm_gain,
    router,
    expert_ids,
    gate_weight,
    up_weight,
    down_weight,
):
    seq_count = lax.axis_size(SEQ)
    exp_count = lax.axis_size(EXP)
    groups = lax.axis_size("g")
    experts = lax.axis_size("e")
    dec_rows = state.shape[1]
    model_width = state.shape[2]
    block_width = model_width // groups
    tiles = block_width // LANES
    head = key_weight.shape[2]
    hidden_here = gate_weight.shape[2]
    tokens = encoded.shape[1] * seq_count
    my_seq = lax.axis_index(SEQ)
    my_expert = lax.axis_index("e")
    my_group = lax.axis_index("g")

    enc_all = lax.all_gather(encoded[0], SEQ, axis=0, tiled=True)
    first = jnp.concatenate([key_weight[0], value_weight[0]], axis=1)
    second = jnp.concatenate([key_weight[1], value_weight[1]], axis=1)
    own = lax.all_gather(first, "e", axis=0, tiled=True)
    second, own = lax.optimization_barrier((second, own))
    middle = own.shape[0] // 2
    left = shifted(own, exp_count, 1)
    right = shifted(own, exp_count, -1)
    far_left = shifted(left[:middle], exp_count, 1)
    far_right = shifted(right[middle:], exp_count, -1)
    blocks = [own, left, right, far_left, far_right]
    pieces = [
        (0, 0, experts),
        (-1, 0, experts),
        (1, 0, experts),
        (-2, 0, experts // 2),
        (2, experts // 2, experts),
    ]
    second_all = lax.all_gather(second, EXP, axis=0, tiled=True)

    whole = lambda shape: pl.BlockSpec(shape, lambda i, *_: (0,) * len(shape))
    cache_shape = jax.ShapeDtypeStruct((2, tokens, head), BF)
    ordered = pl.pallas_call(
        functools.partial(order_kernel, pieces, groups, experts),
        grid_spec=pltpu.PrefetchScalarGridSpec(
            num_scalar_prefetch=1,
            grid=(1,),
            in_specs=[whole(block.shape) for block in blocks],
            out_specs=whole((model_width, 2 * head)),
        ),
        out_shape=jax.ShapeDtypeStruct((model_width, 2 * head), BF),
        compiler_params=pltpu.CompilerParams(vmem_limit_bytes=24 * 1024 * 1024),
        name="order_weights",
    )(my_group.reshape(1), *blocks)
    pair = jnp.dot(enc_all, ordered, preferred_element_type=F32).astype(BF)
    flags = jnp.any(
        expert_ids[0][:, :, None] == jnp.arange(experts, dtype=jnp.int32), axis=1
    ).astype(F32).T
    before = jnp.triu(jnp.ones((dec_rows, dec_rows), F32), 1)
    slot = jnp.where(flags > 0.5, jnp.dot(flags, before), -1.0)
    slots = jnp.arange(CAP, dtype=F32).reshape(PAIRS, 1, EACH, 1)
    pick = jnp.where(slot[None, :, None, :] == slots, 1.0, 0.0).astype(BF)
    piece_rows = experts * EACH
    same = jnp.eye(groups, dtype=BF)
    place = pick.reshape(PAIRS, piece_rows, dec_rows).transpose(2, 0, 1)
    place = (same[:, None, None, :, None] * place[None, :, :, None, :]).reshape(
        groups * dec_rows, PAIRS * groups * piece_rows
    )
    pick = pick.reshape(PAIRS * piece_rows, dec_rows)
    key_cache, value_cache, terms = pl.pallas_call(
        functools.partial(attention_kernel, tiles, groups),
        grid=(1,),
        in_specs=[
            whole((dec_rows, head)),
            whole(pair.shape),
            whole(pick.shape),
            whole(out_weight.shape),
        ],
        out_specs=[
            pl.BlockSpec((1, tokens, head), lambda i: (0, 0, 0)),
            pl.BlockSpec((1, tokens, head), lambda i: (0, 0, 0)),
            whole((seq_count, groups * piece_rows, LANES)),
        ],
        out_shape=[
            cache_shape,
            cache_shape,
            jax.ShapeDtypeStruct((seq_count, groups * piece_rows, LANES), BF),
        ],
        compiler_params=pltpu.CompilerParams(vmem_limit_bytes=16 * 1024 * 1024),
        name="attend",
    )(queries[0], pair, pick, out_weight)

    state_parts = jnp.dot(pick, state[0], preferred_element_type=F32)
    state_parts = state_parts.reshape(PAIRS, piece_rows, groups, tiles, LANES)
    state_here = lax.dynamic_index_in_dim(state_parts, my_seq % PAIRS, 0, keepdims=False)
    my_tile = jnp.minimum(my_seq // PAIRS, tiles - 1)
    state_here = lax.dynamic_index_in_dim(state_here, my_tile, 2, keepdims=False).transpose(1, 0, 2)
    got = exchanged(terms, SEQ)
    attended = jnp.sum(got.astype(F32), axis=0).reshape(groups, piece_rows, LANES) + state_here
    routed = attended.astype(BF).reshape(groups, experts, EACH, LANES).transpose(1, 0, 2, 3)
    routed = exchanged(routed.reshape(exp_count, EACH, LANES), EXP)
    rows_all = spread(routed.reshape(exp_count * EACH, LANES), SEQ)
    slot_count = exp_count * CAP
    gain = lax.dynamic_slice_in_dim(norm_gain, my_group * block_width, block_width, 0)
    routes = lax.dynamic_slice_in_dim(router.T, my_group * block_width, block_width, 1)
    gap = jnp.zeros((8 - experts, block_width), BF)
    routes = jnp.concatenate([routes, gap, routes, gap], axis=0)
    routes = jnp.pad(routes, ((0, WIDE - hidden_here - routes.shape[0]), (0, 0)))
    partial = pl.pallas_call(
        functools.partial(expert_input_kernel, hidden_here),
        grid=(1,),
        in_specs=[
            whole(rows_all.shape),
            whole((1, block_width)),
            whole(routes.shape),
            whole((hidden_here, block_width)),
            whole((hidden_here, block_width)),
        ],
        out_specs=whole((slot_count, 2 * WIDE)),
        out_shape=jax.ShapeDtypeStruct((slot_count, 2 * WIDE), BF),
        scratch_shapes=[
            pltpu.VMEM((slot_count, block_width), BF),
            pltpu.VMEM((WIDE, block_width), BF),
            pltpu.VMEM((WIDE, block_width), BF),
        ],
        compiler_params=pltpu.CompilerParams(vmem_limit_bytes=24 * 1024 * 1024),
        name="expert_input",
    )(
        rows_all,
        gain[None],
        routes,
        gate_weight[0].T,
        up_weight[0].T,
    )
    parts = lax.all_gather(partial, "g", axis=0)
    out = pl.pallas_call(
        functools.partial(expert_output_kernel, hidden_here, model_width),
        grid_spec=pltpu.PrefetchScalarGridSpec(
            num_scalar_prefetch=1,
            grid=(1,),
            in_specs=[
                whole(parts.shape),
                whole((hidden_here, block_width)),
            ],
            out_specs=whole(rows_all.shape),
        ),
        out_shape=jax.ShapeDtypeStruct(rows_all.shape, BF),
        compiler_params=pltpu.CompilerParams(vmem_limit_bytes=24 * 1024 * 1024),
        name="expert_output",
    )(my_expert.reshape(1), parts, down_weight[0])
    out, second_all = lax.optimization_barrier((out, second_all))
    back = exchanged(out, SEQ)
    second_pair = jnp.dot(enc_all, second_all, preferred_element_type=F32).astype(BF)
    key_cache, value_cache = pl.pallas_call(
        second_kernel,
        grid=(1,),
        in_specs=[
            pl.BlockSpec(second_pair.shape, lambda i: (0, 0)),
            pl.BlockSpec(memory_space=pl.ANY),
            pl.BlockSpec(memory_space=pl.ANY),
        ],
        out_specs=[pl.BlockSpec((1, tokens, head), lambda i: (1, 0, 0))] * 2,
        out_shape=[cache_shape, cache_shape],
        input_output_aliases={1: 0, 2: 1},
        compiler_params=pltpu.CompilerParams(vmem_limit_bytes=8 * 1024 * 1024),
        name="store_second",
    )(second_pair, key_cache, value_cache)
    back, key_cache, value_cache = lax.optimization_barrier((back, key_cache, value_cache))
    back = jnp.sum(back.astype(F32), axis=0).astype(BF)
    back = exchanged(back.reshape(exp_count, EACH, LANES), EXP)
    back = back.reshape(experts, groups, EACH, LANES).transpose(1, 0, 2, 3).astype(F32)
    mixed = attended / TOP + back.reshape(groups, piece_rows, LANES)
    mixed = spread(mixed.astype(BF).reshape(groups * piece_rows, LANES), SEQ)
    mixed = pl.pallas_call(
        functools.partial(rows_kernel, tiles, groups),
        grid=(1,),
        in_specs=[whole(mixed.shape), whole(place.shape)],
        out_specs=whole((dec_rows, model_width)),
        out_shape=jax.ShapeDtypeStruct((dec_rows, model_width), BF),
        compiler_params=pltpu.CompilerParams(vmem_limit_bytes=8 * 1024 * 1024),
        name="place_rows",
    )(mixed, place)[None]
    return key_cache[:, None], value_cache[:, None], mixed


def solution(mesh):
    fine = Mesh(mesh.devices.reshape(4, 4, 2, 4, 4), SEQ + EXP)
    return jax.shard_map(
        per_device,
        mesh=fine,
        in_specs=(
            P(EXP, SEQ, None),
            P(None, EXP, SEQ),
            P(None, EXP, SEQ),
            P(EXP, None, SEQ),
            P(EXP, None, None),
            P(SEQ, None),
            P(),
            P(),
            P(EXP, None, None),
            P(EXP, None, SEQ),
            P(EXP, None, SEQ),
            P(EXP, SEQ, None),
        ),
        out_specs=(P(None, EXP, None, SEQ), P(None, EXP, None, SEQ), P(EXP, None, None)),
        check_vma=False,
    )
```

```python
import functools
import math

import jax
import jax.numpy as jnp
from jax import lax
from jax.experimental import pallas as pl
from jax.experimental.pallas import tpu as pltpu
from jax.sharding import Mesh
from jax.sharding import PartitionSpec as P

EPS = 1e-06
SEQ = ("x", "y", "c")
EXP = ("e", "g")
LANES = 128
BF = jnp.bfloat16
F32 = jnp.float32
WIDE = 384
CAP = 6
TOP = 2
PAIRS = 3
EACH = CAP // PAIRS


def shifted(x, count, by):
    return lax.ppermute(x, EXP, [(i, (i + by) % count) for i in range(count)])


def exchanged(x, axes):
    return lax.all_to_all(x, axes, split_axis=0, concat_axis=0, tiled=True)


def spread(x, axes):
    count = lax.axis_size(axes)
    return exchanged(jnp.broadcast_to(x[None], (count,) + x.shape), axes)


def order_kernel(pieces, groups, experts, group_ref, *refs):
    blocks, weight_ref = refs[:-1], refs[-1]
    rows = weight_ref.shape[0] // (groups * experts)
    for block, (offset, first, last) in zip(blocks, pieces):
        group = lax.rem(group_ref[0] + (groups + offset), groups)
        for e in range(first, last):
            at = pl.multiple_of((e * groups + group) * rows, 64)
            weight_ref[pl.ds(at, rows), :] = block[(e - first) * rows : (e - first + 1) * rows, :]


def attention_kernel(
    tiles, groups, query_ref, pair_ref, pick_ref, out_ref, key_ref, value_ref, term_ref
):
    head = key_ref.shape[-1]
    key_ref[0] = pair_ref[:, :head]
    value_ref[0] = pair_ref[:, head:]
    scores = lax.dot_general(
        query_ref[...], key_ref[0], (((1,), (1,)), ((), ())), preferred_element_type=F32
    ) / math.sqrt(head)
    raised = jnp.exp(scores - jnp.max(scores, axis=-1, keepdims=True))
    attn = (raised / jnp.sum(raised, axis=-1, keepdims=True)).astype(BF)
    context = jnp.dot(attn, value_ref[0], preferred_element_type=F32).astype(BF)
    context = jnp.dot(pick_ref[...], context, preferred_element_type=F32).astype(BF)
    rows = context.shape[0] // PAIRS
    for t in range(tiles):
        parts = [
            jnp.dot(
                context,
                out_ref[:, (g * tiles + t) * LANES : (g * tiles + t + 1) * LANES],
                preferred_element_type=F32,
            )
            for g in range(groups)
        ]
        for k in range(PAIRS):
            term_ref[PAIRS * t + k] = jnp.concatenate(
                [p[k * rows : (k + 1) * rows] for p in parts], axis=0
            ).astype(BF)
    for s in range(PAIRS * tiles, term_ref.shape[0]):
        term_ref[s] = jnp.zeros(term_ref.shape[1:], BF)


def second_kernel(pair_ref, key_in, value_in, key_ref, value_ref):
    head = key_ref.shape[-1]
    key_ref[0] = pair_ref[:, :head]
    value_ref[0] = pair_ref[:, head:]


def expert_input_kernel(
    hidden, rows_ref, gain_ref, router_ref, gate_ref, up_ref, part_ref, x_ref, gate_all, up_all
):
    tiles = x_ref.shape[1] // LANES
    wide = gate_all.shape[0]
    squares = None
    for t in range(tiles):
        x = jnp.concatenate([rows_ref[PAIRS * t + k] for k in range(PAIRS)], axis=0).astype(F32)
        term = jnp.sum(x * x, axis=1, keepdims=True)
        squares = term if squares is None else squares + term
        gain = gain_ref[:, t * LANES : (t + 1) * LANES]
        x_ref[:, t * LANES : (t + 1) * LANES] = (x * gain).astype(BF)
    gate_all[:hidden] = gate_ref[...]
    gate_all[hidden:] = router_ref[...]
    up_all[:hidden] = up_ref[...]
    up_all[hidden:] = jnp.zeros((wide - hidden, up_all.shape[1]), BF)
    contract = (((1,), (1,)), ((), ()))
    gate = lax.dot_general(x_ref[...], gate_all[...], contract, preferred_element_type=F32)
    lane = lax.broadcasted_iota(jnp.int32, gate.shape, 1)
    gate = jnp.where((lane == hidden + 4) | (lane == hidden + 12), squares, gate)
    high = gate.astype(BF)
    low = (gate - high.astype(F32)).astype(BF)
    part_ref[:, :wide] = jnp.where(lane >= hidden + 8, low.astype(F32), high.astype(F32)).astype(BF)
    up = lax.dot_general(x_ref[...], up_all[...], contract, preferred_element_type=F32)
    part_ref[:, wide:] = up.astype(BF)


def expert_output_kernel(hidden, width, expert_ref, part_ref, down_ref, out_ref):
    total = part_ref[0].astype(F32)
    for k in range(1, part_ref.shape[0]):
        total = total + part_ref[k].astype(F32)
    wide = total.shape[1] // 2
    gate, lifted = total[:, :wide], total[:, wide:]

    def column(j):
        return gate[:, hidden + j : hidden + j + 1] + gate[:, hidden + 8 + j : hidden + 9 + j]

    scale = lax.rsqrt(column(4) / width + EPS)
    logits = [column(j) * scale for j in range(4)]
    top = functools.reduce(jnp.maximum, logits)
    raised = [jnp.exp(logit - top) for logit in logits]
    mine = [jnp.where(expert_ref[0] == j, raised[j], 0.0) for j in range(4)]
    share = sum(mine) / sum(raised)
    gate = gate * scale
    active = 0.5 * gate * (1.0 + jnp.tanh(math.sqrt(2 / math.pi) * (gate + 0.044715 * gate**3)))
    units = (active * (lifted * scale) * share)[:, :hidden].astype(BF)
    out = jnp.dot(units, down_ref[...], preferred_element_type=F32).astype(BF)
    tiles = out.shape[1] // LANES
    rows = out_ref.shape[1]
    for t in range(tiles):
        for k in range(PAIRS):
            out_ref[PAIRS * t + k] = out[k * rows : (k + 1) * rows, t * LANES : (t + 1) * LANES]
    for s in range(PAIRS * tiles, out_ref.shape[0]):
        out_ref[s] = jnp.zeros(out_ref.shape[1:], BF)


def rows_kernel(tiles, groups, parts_ref, place_ref, out_ref):
    rows = out_ref.shape[0]
    for t in range(tiles):
        parts = jnp.concatenate([parts_ref[PAIRS * t + k] for k in range(PAIRS)], axis=0)
        placed = jnp.dot(place_ref[...], parts, preferred_element_type=F32)
        for g in range(groups):
            at = (g * tiles + t) * LANES
            out_ref[:, at : at + LANES] = placed[g * rows : (g + 1) * rows].astype(BF)


def per_device(
    encoded,
    key_weight,
    value_weight,
    queries,
    state,
    out_weight,
    norm_gain,
    router,
    expert_ids,
    gate_weight,
    up_weight,
    down_weight,
):
    seq_count = lax.axis_size(SEQ)
    exp_count = lax.axis_size(EXP)
    groups = lax.axis_size("g")
    experts = lax.axis_size("e")
    dec_rows = state.shape[1]
    model_width = state.shape[2]
    block_width = model_width // groups
    tiles = block_width // LANES
    head = key_weight.shape[2]
    hidden_here = gate_weight.shape[2]
    tokens = encoded.shape[1] * seq_count
    my_seq = lax.axis_index(SEQ)
    my_expert = lax.axis_index("e")
    my_group = lax.axis_index("g")

    enc_all = lax.all_gather(encoded[0], SEQ, axis=0, tiled=True)
    first = jnp.concatenate([key_weight[0], value_weight[0]], axis=1)
    second = jnp.concatenate([key_weight[1], value_weight[1]], axis=1)
    own = lax.all_gather(first, "e", axis=0, tiled=True)
    second, own = lax.optimization_barrier((second, own))
    middle = own.shape[0] // 2
    left = shifted(own, exp_count, 1)
    right = shifted(own, exp_count, -1)
    far_left = shifted(left[:middle], exp_count, 1)
    far_right = shifted(right[middle:], exp_count, -1)
    blocks = [own, left, right, far_left, far_right]
    pieces = [
        (0, 0, experts),
        (-1, 0, experts),
        (1, 0, experts),
        (-2, 0, experts // 2),
        (2, experts // 2, experts),
    ]
    second_all = lax.all_gather(second, EXP, axis=0, tiled=True)

    whole = lambda shape: pl.BlockSpec(shape, lambda i, *_: (0,) * len(shape))
    cache_shape = jax.ShapeDtypeStruct((2, tokens, head), BF)
    ordered = pl.pallas_call(
        functools.partial(order_kernel, pieces, groups, experts),
        grid_spec=pltpu.PrefetchScalarGridSpec(
            num_scalar_prefetch=1,
            grid=(1,),
            in_specs=[whole(block.shape) for block in blocks],
            out_specs=whole((model_width, 2 * head)),
        ),
        out_shape=jax.ShapeDtypeStruct((model_width, 2 * head), BF),
        compiler_params=pltpu.CompilerParams(vmem_limit_bytes=24 * 1024 * 1024),
        name="order_weights",
    )(my_group.reshape(1), *blocks)
    pair = jnp.dot(enc_all, ordered, preferred_element_type=F32).astype(BF)
    flags = jnp.any(
        expert_ids[0][:, :, None] == jnp.arange(experts, dtype=jnp.int32), axis=1
    ).astype(F32).T
    before = jnp.triu(jnp.ones((dec_rows, dec_rows), F32), 1)
    slot = jnp.where(flags > 0.5, jnp.dot(flags, before), -1.0)
    slots = jnp.arange(CAP, dtype=F32).reshape(PAIRS, 1, EACH, 1)
    pick = jnp.where(slot[None, :, None, :] == slots, 1.0, 0.0).astype(BF)
    piece_rows = experts * EACH
    same = jnp.eye(groups, dtype=BF)
    place = pick.reshape(PAIRS, piece_rows, dec_rows).transpose(2, 0, 1)
    place = (same[:, None, None, :, None] * place[None, :, :, None, :]).reshape(
        groups * dec_rows, PAIRS * groups * piece_rows
    )
    pick = pick.reshape(PAIRS * piece_rows, dec_rows)
    key_cache, value_cache, terms = pl.pallas_call(
        functools.partial(attention_kernel, tiles, groups),
        grid=(1,),
        in_specs=[
            whole((dec_rows, head)),
            whole(pair.shape),
            whole(pick.shape),
            whole(out_weight.shape),
        ],
        out_specs=[
            pl.BlockSpec((1, tokens, head), lambda i: (0, 0, 0)),
            pl.BlockSpec((1, tokens, head), lambda i: (0, 0, 0)),
            whole((seq_count, groups * piece_rows, LANES)),
        ],
        out_shape=[
            cache_shape,
            cache_shape,
            jax.ShapeDtypeStruct((seq_count, groups * piece_rows, LANES), BF),
        ],
        compiler_params=pltpu.CompilerParams(vmem_limit_bytes=16 * 1024 * 1024),
        name="attend",
    )(queries[0], pair, pick, out_weight)

    state_parts = jnp.dot(pick, state[0], preferred_element_type=F32)
    state_parts = state_parts.reshape(PAIRS, piece_rows, groups, tiles, LANES)
    state_here = lax.dynamic_index_in_dim(state_parts, my_seq % PAIRS, 0, keepdims=False)
    my_tile = jnp.minimum(my_seq // PAIRS, tiles - 1)
    state_here = lax.dynamic_index_in_dim(state_here, my_tile, 2, keepdims=False).transpose(1, 0, 2)
    got = exchanged(terms, SEQ)
    attended = jnp.sum(got.astype(F32), axis=0).reshape(groups, piece_rows, LANES) + state_here
    routed = attended.astype(BF).reshape(groups, experts, EACH, LANES).transpose(1, 0, 2, 3)
    routed = exchanged(routed.reshape(exp_count, EACH, LANES), EXP)
    rows_all = spread(routed.reshape(exp_count * EACH, LANES), SEQ)
    slot_count = exp_count * CAP
    gain = lax.dynamic_slice_in_dim(norm_gain, my_group * block_width, block_width, 0)
    routes = lax.dynamic_slice_in_dim(router.T, my_group * block_width, block_width, 1)
    gap = jnp.zeros((8 - experts, block_width), BF)
    routes = jnp.concatenate([routes, gap, routes, gap], axis=0)
    routes = jnp.pad(routes, ((0, WIDE - hidden_here - routes.shape[0]), (0, 0)))
    partial = pl.pallas_call(
        functools.partial(expert_input_kernel, hidden_here),
        grid=(1,),
        in_specs=[
            whole(rows_all.shape),
            whole((1, block_width)),
            whole(routes.shape),
            whole((hidden_here, block_width)),
            whole((hidden_here, block_width)),
        ],
        out_specs=whole((slot_count, 2 * WIDE)),
        out_shape=jax.ShapeDtypeStruct((slot_count, 2 * WIDE), BF),
        scratch_shapes=[
            pltpu.VMEM((slot_count, block_width), BF),
            pltpu.VMEM((WIDE, block_width), BF),
            pltpu.VMEM((WIDE, block_width), BF),
        ],
        compiler_params=pltpu.CompilerParams(vmem_limit_bytes=24 * 1024 * 1024),
        name="expert_input",
    )(
        rows_all,
        gain[None],
        routes,
        gate_weight[0].T,
        up_weight[0].T,
    )
    parts = lax.all_gather(partial, "g", axis=0)
    out = pl.pallas_call(
        functools.partial(expert_output_kernel, hidden_here, model_width),
        grid_spec=pltpu.PrefetchScalarGridSpec(
            num_scalar_prefetch=1,
            grid=(1,),
            in_specs=[
                whole(parts.shape),
                whole((hidden_here, block_width)),
            ],
            out_specs=whole(rows_all.shape),
        ),
        out_shape=jax.ShapeDtypeStruct(rows_all.shape, BF),
        compiler_params=pltpu.CompilerParams(vmem_limit_bytes=24 * 1024 * 1024),
        name="expert_output",
    )(my_expert.reshape(1), parts, down_weight[0])
    back = exchanged(out, SEQ)
    back = jnp.sum(back.astype(F32), axis=0).astype(BF)
    back = exchanged(back.reshape(exp_count, EACH, LANES), EXP)
    back = back.reshape(experts, groups, EACH, LANES).transpose(1, 0, 2, 3).astype(F32)
    mixed = attended / TOP + back.reshape(groups, piece_rows, LANES)
    mixed = mixed.astype(BF).reshape(groups * piece_rows, LANES)
    mixed, second_all = lax.optimization_barrier((mixed, second_all))
    mixed = spread(mixed, SEQ)
    second_pair = jnp.dot(enc_all, second_all, preferred_element_type=F32).astype(BF)
    key_cache, value_cache = pl.pallas_call(
        second_kernel,
        grid=(1,),
        in_specs=[
            pl.BlockSpec(second_pair.shape, lambda i: (0, 0)),
            pl.BlockSpec(memory_space=pl.ANY),
            pl.BlockSpec(memory_space=pl.ANY),
        ],
        out_specs=[pl.BlockSpec((1, tokens, head), lambda i: (1, 0, 0))] * 2,
        out_shape=[cache_shape, cache_shape],
        input_output_aliases={1: 0, 2: 1},
        compiler_params=pltpu.CompilerParams(vmem_limit_bytes=8 * 1024 * 1024),
        name="store_second",
    )(second_pair, key_cache, value_cache)
    mixed, key_cache, value_cache = lax.optimization_barrier((mixed, key_cache, value_cache))
    mixed = pl.pallas_call(
        functools.partial(rows_kernel, tiles, groups),
        grid=(1,),
        in_specs=[whole(mixed.shape), whole(place.shape)],
        out_specs=whole((dec_rows, model_width)),
        out_shape=jax.ShapeDtypeStruct((dec_rows, model_width), BF),
        compiler_params=pltpu.CompilerParams(vmem_limit_bytes=8 * 1024 * 1024),
        name="place_rows",
    )(mixed, place)[None]
    return key_cache[:, None], value_cache[:, None], mixed


def solution(mesh):
    fine = Mesh(mesh.devices.reshape(4, 4, 2, 4, 4), SEQ + EXP)
    return jax.shard_map(
        per_device,
        mesh=fine,
        in_specs=(
            P(EXP, SEQ, None),
            P(None, EXP, SEQ),
            P(None, EXP, SEQ),
            P(EXP, None, SEQ),
            P(EXP, None, None),
            P(SEQ, None),
            P(),
            P(),
            P(EXP, None, None),
            P(EXP, None, SEQ),
            P(EXP, None, SEQ),
            P(EXP, SEQ, None),
        ),
        out_specs=(P(None, EXP, None, SEQ), P(None, EXP, None, SEQ), P(EXP, None, None)),
        check_vma=False,
    )
```

```python
import functools
import math

import jax
import jax.numpy as jnp
from jax import lax
from jax.experimental import pallas as pl
from jax.experimental.pallas import tpu as pltpu
from jax.sharding import Mesh
from jax.sharding import PartitionSpec as P

EPS = 1e-06
SEQ = ("x", "y", "c")
EXP = ("e", "g")
OWNERS = ("g", "e")
LANES = 128
BF = jnp.bfloat16
F32 = jnp.float32
WIDE = 384
CAP = 6
TOP = 2
PAIRS = 3
EACH = CAP // PAIRS


def shifted(x, count, by):
    return lax.ppermute(x, EXP, [(i, (i + by) % count) for i in range(count)])


def exchanged(x, axes):
    return lax.all_to_all(x, axes, split_axis=0, concat_axis=0, tiled=True)


def spread(x, axes):
    count = lax.axis_size(axes)
    return exchanged(jnp.broadcast_to(x[None], (count,) + x.shape), axes)


def order_kernel(pieces, groups, experts, group_ref, *refs):
    blocks, weight_ref = refs[:-1], refs[-1]
    rows = weight_ref.shape[0] // (groups * experts)
    for block, (offset, first, last) in zip(blocks, pieces):
        group = lax.rem(group_ref[0] + (groups + offset), groups)
        for e in range(first, last):
            at = pl.multiple_of((e * groups + group) * rows, 64)
            weight_ref[pl.ds(at, rows), :] = block[(e - first) * rows : (e - first + 1) * rows, :]


def attention_kernel(
    tiles, groups, query_ref, pair_ref, pick_ref, out_ref, key_ref, value_ref, term_ref
):
    head = key_ref.shape[-1]
    key_ref[0] = pair_ref[:, :head]
    value_ref[0] = pair_ref[:, head:]
    scores = lax.dot_general(
        query_ref[...], key_ref[0], (((1,), (1,)), ((), ())), preferred_element_type=F32
    ) / math.sqrt(head)
    raised = jnp.exp(scores - jnp.max(scores, axis=-1, keepdims=True))
    attn = (raised / jnp.sum(raised, axis=-1, keepdims=True)).astype(BF)
    context = jnp.dot(attn, value_ref[0], preferred_element_type=F32).astype(BF)
    context = jnp.dot(pick_ref[...], context, preferred_element_type=F32).astype(BF)
    rows = context.shape[0] // PAIRS
    for t in range(tiles):
        parts = [
            jnp.dot(
                context,
                out_ref[:, (g * tiles + t) * LANES : (g * tiles + t + 1) * LANES],
                preferred_element_type=F32,
            )
            for g in range(groups)
        ]
        for k in range(PAIRS):
            term_ref[PAIRS * t + k] = jnp.concatenate(
                [p[k * rows : (k + 1) * rows] for p in parts], axis=0
            ).astype(BF)
    for s in range(PAIRS * tiles, term_ref.shape[0]):
        term_ref[s] = jnp.zeros(term_ref.shape[1:], BF)


def second_kernel(pair_ref, key_in, value_in, key_ref, value_ref):
    head = key_ref.shape[-1]
    key_ref[0] = pair_ref[:, :head]
    value_ref[0] = pair_ref[:, head:]


def expert_input_kernel(
    hidden, rows_ref, gain_ref, router_ref, gate_ref, up_ref, part_ref, x_ref, gate_all, up_all
):
    tiles = x_ref.shape[1] // LANES
    wide = gate_all.shape[0]
    squares = None
    for t in range(tiles):
        x = jnp.concatenate([rows_ref[PAIRS * t + k] for k in range(PAIRS)], axis=0).astype(F32)
        term = jnp.sum(x * x, axis=1, keepdims=True)
        squares = term if squares is None else squares + term
        gain = gain_ref[:, t * LANES : (t + 1) * LANES]
        x_ref[:, t * LANES : (t + 1) * LANES] = (x * gain).astype(BF)
    gate_all[:hidden] = gate_ref[...]
    gate_all[hidden:] = router_ref[...]
    up_all[:hidden] = up_ref[...]
    up_all[hidden:] = jnp.zeros((wide - hidden, up_all.shape[1]), BF)
    contract = (((1,), (1,)), ((), ()))
    gate = lax.dot_general(x_ref[...], gate_all[...], contract, preferred_element_type=F32)
    lane = lax.broadcasted_iota(jnp.int32, gate.shape, 1)
    gate = jnp.where((lane == hidden + 4) | (lane == hidden + 12), squares, gate)
    high = gate.astype(BF)
    low = (gate - high.astype(F32)).astype(BF)
    part_ref[:, :wide] = jnp.where(lane >= hidden + 8, low.astype(F32), high.astype(F32)).astype(BF)
    up = lax.dot_general(x_ref[...], up_all[...], contract, preferred_element_type=F32)
    part_ref[:, wide:] = up.astype(BF)


def expert_output_kernel(hidden, width, expert_ref, part_ref, down_ref, out_ref):
    total = part_ref[0].astype(F32)
    for k in range(1, part_ref.shape[0]):
        total = total + part_ref[k].astype(F32)
    wide = total.shape[1] // 2
    gate, lifted = total[:, :wide], total[:, wide:]

    def column(j):
        return gate[:, hidden + j : hidden + j + 1] + gate[:, hidden + 8 + j : hidden + 9 + j]

    scale = lax.rsqrt(column(4) / width + EPS)
    logits = [column(j) * scale for j in range(4)]
    top = functools.reduce(jnp.maximum, logits)
    raised = [jnp.exp(logit - top) for logit in logits]
    mine = [jnp.where(expert_ref[0] == j, raised[j], 0.0) for j in range(4)]
    share = sum(mine) / sum(raised)
    gate = gate * scale
    active = 0.5 * gate * (1.0 + jnp.tanh(math.sqrt(2 / math.pi) * (gate + 0.044715 * gate**3)))
    units = (active * (lifted * scale) * share)[:, :hidden].astype(BF)
    out = jnp.dot(units, down_ref[...], preferred_element_type=F32).astype(BF)
    tiles = out.shape[1] // LANES
    rows = out_ref.shape[1]
    for t in range(tiles):
        for k in range(PAIRS):
            out_ref[PAIRS * t + k] = out[k * rows : (k + 1) * rows, t * LANES : (t + 1) * LANES]
    for s in range(PAIRS * tiles, out_ref.shape[0]):
        out_ref[s] = jnp.zeros(out_ref.shape[1:], BF)


def rows_kernel(tiles, groups, parts_ref, place_ref, out_ref):
    rows = out_ref.shape[0]
    for t in range(tiles):
        parts = jnp.concatenate([parts_ref[PAIRS * t + k] for k in range(PAIRS)], axis=0)
        placed = jnp.dot(place_ref[...], parts, preferred_element_type=F32)
        for g in range(groups):
            at = (g * tiles + t) * LANES
            out_ref[:, at : at + LANES] = placed[g * rows : (g + 1) * rows].astype(BF)


def per_device(
    encoded,
    key_weight,
    value_weight,
    queries,
    state,
    out_weight,
    norm_gain,
    router,
    expert_ids,
    gate_weight,
    up_weight,
    down_weight,
):
    seq_count = lax.axis_size(SEQ)
    exp_count = lax.axis_size(EXP)
    groups = lax.axis_size("g")
    experts = lax.axis_size("e")
    dec_rows = state.shape[1]
    model_width = state.shape[2]
    block_width = model_width // groups
    tiles = block_width // LANES
    head = key_weight.shape[2]
    hidden_here = gate_weight.shape[2]
    tokens = encoded.shape[1] * seq_count
    my_seq = lax.axis_index(SEQ)
    my_expert = lax.axis_index("e")
    my_group = lax.axis_index("g")

    enc_all = lax.all_gather(encoded[0], SEQ, axis=0, tiled=True)
    first = jnp.concatenate([key_weight[0], value_weight[0]], axis=1)
    second = jnp.concatenate([key_weight[1], value_weight[1]], axis=1)
    own = lax.all_gather(first, "e", axis=0, tiled=True)
    second, own = lax.optimization_barrier((second, own))
    middle = own.shape[0] // 2
    left = shifted(own, exp_count, 1)
    right = shifted(own, exp_count, -1)
    far_left = shifted(left[:middle], exp_count, 1)
    far_right = shifted(right[middle:], exp_count, -1)
    blocks = [own, left, right, far_left, far_right]
    pieces = [
        (0, 0, experts),
        (-1, 0, experts),
        (1, 0, experts),
        (-2, 0, experts // 2),
        (2, experts // 2, experts),
    ]
    second_all = lax.all_gather(second, EXP, axis=0, tiled=True)

    whole = lambda shape: pl.BlockSpec(shape, lambda i, *_: (0,) * len(shape))
    cache_shape = jax.ShapeDtypeStruct((2, tokens, head), BF)
    ordered = pl.pallas_call(
        functools.partial(order_kernel, pieces, groups, experts),
        grid_spec=pltpu.PrefetchScalarGridSpec(
            num_scalar_prefetch=1,
            grid=(1,),
            in_specs=[whole(block.shape) for block in blocks],
            out_specs=whole((model_width, 2 * head)),
        ),
        out_shape=jax.ShapeDtypeStruct((model_width, 2 * head), BF),
        compiler_params=pltpu.CompilerParams(vmem_limit_bytes=24 * 1024 * 1024),
        name="order_weights",
    )(my_group.reshape(1), *blocks)
    pair = jnp.dot(enc_all, ordered, preferred_element_type=F32).astype(BF)
    flags = jnp.any(
        expert_ids[0][:, :, None] == jnp.arange(experts, dtype=jnp.int32), axis=1
    ).astype(F32).T
    before = jnp.triu(jnp.ones((dec_rows, dec_rows), F32), 1)
    slot = jnp.where(flags > 0.5, jnp.dot(flags, before), -1.0)
    slots = jnp.arange(CAP, dtype=F32).reshape(PAIRS, 1, EACH, 1)
    pick = jnp.where(slot[None, :, None, :] == slots, 1.0, 0.0).astype(BF)
    piece_rows = experts * EACH
    same = jnp.eye(groups, dtype=BF)
    place = pick.reshape(PAIRS, piece_rows, dec_rows).transpose(2, 0, 1)
    place = (same[:, None, None, :, None] * place[None, :, :, None, :]).reshape(
        groups * dec_rows, PAIRS * groups * piece_rows
    )
    pick = pick.reshape(PAIRS * piece_rows, dec_rows)
    key_cache, value_cache, terms = pl.pallas_call(
        functools.partial(attention_kernel, tiles, groups),
        grid=(1,),
        in_specs=[
            whole((dec_rows, head)),
            whole(pair.shape),
            whole(pick.shape),
            whole(out_weight.shape),
        ],
        out_specs=[
            pl.BlockSpec((1, tokens, head), lambda i: (0, 0, 0)),
            pl.BlockSpec((1, tokens, head), lambda i: (0, 0, 0)),
            whole((seq_count, groups * piece_rows, LANES)),
        ],
        out_shape=[
            cache_shape,
            cache_shape,
            jax.ShapeDtypeStruct((seq_count, groups * piece_rows, LANES), BF),
        ],
        compiler_params=pltpu.CompilerParams(vmem_limit_bytes=16 * 1024 * 1024),
        name="attend",
    )(queries[0], pair, pick, out_weight)

    state_parts = jnp.dot(pick, state[0], preferred_element_type=F32)
    state_parts = state_parts.reshape(PAIRS, piece_rows, groups, tiles, LANES)
    state_here = lax.dynamic_index_in_dim(state_parts, my_seq % PAIRS, 0, keepdims=False)
    my_tile = jnp.minimum(my_seq // PAIRS, tiles - 1)
    state_here = lax.dynamic_index_in_dim(state_here, my_tile, 2, keepdims=False).transpose(1, 0, 2)
    got = exchanged(terms, SEQ)
    attended = jnp.sum(got.astype(F32), axis=0).reshape(groups, piece_rows, LANES) + state_here
    routed = exchanged(attended.astype(BF).reshape(exp_count, EACH, LANES), OWNERS)
    rows_all = spread(routed.reshape(exp_count * EACH, LANES), SEQ)
    slot_count = exp_count * CAP
    gain = lax.dynamic_slice_in_dim(norm_gain, my_group * block_width, block_width, 0)
    routes = lax.dynamic_slice_in_dim(router.T, my_group * block_width, block_width, 1)
    gap = jnp.zeros((8 - experts, block_width), BF)
    routes = jnp.concatenate([routes, gap, routes, gap], axis=0)
    routes = jnp.pad(routes, ((0, WIDE - hidden_here - routes.shape[0]), (0, 0)))
    partial = pl.pallas_call(
        functools.partial(expert_input_kernel, hidden_here),
        grid=(1,),
        in_specs=[
            whole(rows_all.shape),
            whole((1, block_width)),
            whole(routes.shape),
            whole((hidden_here, block_width)),
            whole((hidden_here, block_width)),
        ],
        out_specs=whole((slot_count, 2 * WIDE)),
        out_shape=jax.ShapeDtypeStruct((slot_count, 2 * WIDE), BF),
        scratch_shapes=[
            pltpu.VMEM((slot_count, block_width), BF),
            pltpu.VMEM((WIDE, block_width), BF),
            pltpu.VMEM((WIDE, block_width), BF),
        ],
        compiler_params=pltpu.CompilerParams(vmem_limit_bytes=24 * 1024 * 1024),
        name="expert_input",
    )(
        rows_all,
        gain[None],
        routes,
        gate_weight[0].T,
        up_weight[0].T,
    )
    parts = lax.all_gather(partial, "g", axis=0)
    out = pl.pallas_call(
        functools.partial(expert_output_kernel, hidden_here, model_width),
        grid_spec=pltpu.PrefetchScalarGridSpec(
            num_scalar_prefetch=1,
            grid=(1,),
            in_specs=[
                whole(parts.shape),
                whole((hidden_here, block_width)),
            ],
            out_specs=whole(rows_all.shape),
        ),
        out_shape=jax.ShapeDtypeStruct(rows_all.shape, BF),
        compiler_params=pltpu.CompilerParams(vmem_limit_bytes=24 * 1024 * 1024),
        name="expert_output",
    )(my_expert.reshape(1), parts, down_weight[0])
    back = exchanged(out, SEQ)
    back = jnp.sum(back.astype(F32), axis=0).astype(BF)
    back = exchanged(back.reshape(exp_count, EACH, LANES), OWNERS)
    mixed = attended / TOP + back.reshape(groups, piece_rows, LANES).astype(F32)
    mixed = mixed.astype(BF).reshape(groups * piece_rows, LANES)
    mixed, second_all = lax.optimization_barrier((mixed, second_all))
    mixed = spread(mixed, SEQ)
    second_pair = jnp.dot(enc_all, second_all, preferred_element_type=F32).astype(BF)
    key_cache, value_cache = pl.pallas_call(
        second_kernel,
        grid=(1,),
        in_specs=[
            pl.BlockSpec(second_pair.shape, lambda i: (0, 0)),
            pl.BlockSpec(memory_space=pl.ANY),
            pl.BlockSpec(memory_space=pl.ANY),
        ],
        out_specs=[pl.BlockSpec((1, tokens, head), lambda i: (1, 0, 0))] * 2,
        out_shape=[cache_shape, cache_shape],
        input_output_aliases={1: 0, 2: 1},
        compiler_params=pltpu.CompilerParams(vmem_limit_bytes=8 * 1024 * 1024),
        name="store_second",
    )(second_pair, key_cache, value_cache)
    mixed, key_cache, value_cache = lax.optimization_barrier((mixed, key_cache, value_cache))
    mixed = pl.pallas_call(
        functools.partial(rows_kernel, tiles, groups),
        grid=(1,),
        in_specs=[whole(mixed.shape), whole(place.shape)],
        out_specs=whole((dec_rows, model_width)),
        out_shape=jax.ShapeDtypeStruct((dec_rows, model_width), BF),
        compiler_params=pltpu.CompilerParams(vmem_limit_bytes=8 * 1024 * 1024),
        name="place_rows",
    )(mixed, place)[None]
    return key_cache[:, None], value_cache[:, None], mixed


def solution(mesh):
    fine = Mesh(mesh.devices.reshape(4, 4, 2, 4, 4), SEQ + EXP)
    return jax.shard_map(
        per_device,
        mesh=fine,
        in_specs=(
            P(EXP, SEQ, None),
            P(None, EXP, SEQ),
            P(None, EXP, SEQ),
            P(EXP, None, SEQ),
            P(EXP, None, None),
            P(SEQ, None),
            P(),
            P(),
            P(EXP, None, None),
            P(EXP, None, SEQ),
            P(EXP, None, SEQ),
            P(EXP, SEQ, None),
        ),
        out_specs=(P(None, EXP, None, SEQ), P(None, EXP, None, SEQ), P(EXP, None, None)),
        check_vma=False,
    )
```

```python
import functools
import math

import jax
import jax.numpy as jnp
from jax import lax
from jax.experimental import pallas as pl
from jax.experimental.pallas import tpu as pltpu
from jax.sharding import Mesh
from jax.sharding import PartitionSpec as P

EPS = 1e-06
SEQ = ("x", "y", "c")
EXP = ("e", "g")
OWNERS = ("g", "e")
LANES = 128
BF = jnp.bfloat16
F32 = jnp.float32
WIDE = 384
CHUNKS = 10
CAP = 6
TOP = 2
PAIRS = 3
EACH = CAP // PAIRS


def shifted(x, count, by):
    return lax.ppermute(x, EXP, [(i, (i + by) % count) for i in range(count)])


def exchanged(x, axes):
    return lax.all_to_all(x, axes, split_axis=0, concat_axis=0, tiled=True)


def spread(x, axes):
    count = lax.axis_size(axes)
    return exchanged(jnp.broadcast_to(x[None], (count,) + x.shape), axes)


def order_kernel(pieces, groups, experts, group_ref, *refs):
    blocks, weight_ref = refs[:-1], refs[-1]
    rows = weight_ref.shape[0] // (groups * experts)
    for block, (offset, first, last) in zip(blocks, pieces):
        group = lax.rem(group_ref[0] + (groups + offset), groups)
        for e in range(first, last):
            at = pl.multiple_of((e * groups + group) * rows, 64)
            weight_ref[pl.ds(at, rows), :] = block[(e - first) * rows : (e - first + 1) * rows, :]


def attention_kernel(
    tiles,
    groups,
    query_ref,
    pick_ref,
    out_ref,
    weight_ref,
    enc_ref,
    pair_ref,
    term_ref,
    held,
    acc_ref,
    sems,
):
    head = query_ref.shape[-1]
    step = held.shape[1] // CHUNKS
    copies = [
        pltpu.make_async_copy(
            enc_ref.at[:, k * step : (k + 1) * step], held.at[:, k * step : (k + 1) * step], sems.at[k]
        )
        for k in range(CHUNKS)
    ]
    for copy in copies:
        copy.start()
    part = held.shape[0] // 2
    for k, copy in enumerate(copies):
        copy.wait()
        for m in (0, part):
            term = jnp.dot(
                held[m : m + part, k * step : (k + 1) * step],
                weight_ref[k * step : (k + 1) * step, :],
                preferred_element_type=F32,
            )
            if k == 0:
                acc_ref[m : m + part] = term
            else:
                acc_ref[m : m + part] += term
    pair_ref[...] = acc_ref[...].astype(BF)
    scores = lax.dot_general(
        query_ref[...], pair_ref[:, :head], (((1,), (1,)), ((), ())), preferred_element_type=F32
    ) / math.sqrt(head)
    raised = jnp.exp(scores - jnp.max(scores, axis=-1, keepdims=True))
    attn = (raised / jnp.sum(raised, axis=-1, keepdims=True)).astype(BF)
    context = jnp.dot(attn, pair_ref[:, head:], preferred_element_type=F32).astype(BF)
    context = jnp.dot(pick_ref[...], context, preferred_element_type=F32).astype(BF)
    rows = context.shape[0] // PAIRS
    for t in range(tiles):
        parts = [
            jnp.dot(
                context,
                out_ref[:, (g * tiles + t) * LANES : (g * tiles + t + 1) * LANES],
                preferred_element_type=F32,
            )
            for g in range(groups)
        ]
        for k in range(PAIRS):
            term_ref[PAIRS * t + k] = jnp.concatenate(
                [p[k * rows : (k + 1) * rows] for p in parts], axis=0
            ).astype(BF)
    for s in range(PAIRS * tiles, term_ref.shape[0]):
        term_ref[s] = jnp.zeros(term_ref.shape[1:], BF)


def store_kernel(first_ref, second_ref, key_ref, value_ref):
    head = key_ref.shape[-1]
    for layer, pair_ref in enumerate((first_ref, second_ref)):
        key_ref[layer] = pair_ref[:, :head]
        value_ref[layer] = pair_ref[:, head:]


def expert_input_kernel(
    hidden, rows_ref, gain_ref, router_ref, gate_ref, up_ref, part_ref, x_ref, gate_all, up_all
):
    tiles = x_ref.shape[1] // LANES
    wide = gate_all.shape[0]
    squares = None
    for t in range(tiles):
        x = jnp.concatenate([rows_ref[PAIRS * t + k] for k in range(PAIRS)], axis=0).astype(F32)
        term = jnp.sum(x * x, axis=1, keepdims=True)
        squares = term if squares is None else squares + term
        gain = gain_ref[:, t * LANES : (t + 1) * LANES]
        x_ref[:, t * LANES : (t + 1) * LANES] = (x * gain).astype(BF)
    gate_all[:hidden] = gate_ref[...]
    gate_all[hidden:] = router_ref[...]
    up_all[:hidden] = up_ref[...]
    up_all[hidden:] = jnp.zeros((wide - hidden, up_all.shape[1]), BF)
    contract = (((1,), (1,)), ((), ()))
    gate = lax.dot_general(x_ref[...], gate_all[...], contract, preferred_element_type=F32)
    lane = lax.broadcasted_iota(jnp.int32, gate.shape, 1)
    gate = jnp.where((lane == hidden + 4) | (lane == hidden + 12), squares, gate)
    high = gate.astype(BF)
    low = (gate - high.astype(F32)).astype(BF)
    part_ref[:, :wide] = jnp.where(lane >= hidden + 8, low.astype(F32), high.astype(F32)).astype(BF)
    up = lax.dot_general(x_ref[...], up_all[...], contract, preferred_element_type=F32)
    part_ref[:, wide:] = up.astype(BF)


def expert_output_kernel(hidden, width, expert_ref, part_ref, down_ref, out_ref):
    total = part_ref[0].astype(F32)
    for k in range(1, part_ref.shape[0]):
        total = total + part_ref[k].astype(F32)
    wide = total.shape[1] // 2
    gate, lifted = total[:, :wide], total[:, wide:]

    def column(j):
        return gate[:, hidden + j : hidden + j + 1] + gate[:, hidden + 8 + j : hidden + 9 + j]

    scale = lax.rsqrt(column(4) / width + EPS)
    logits = [column(j) * scale for j in range(4)]
    top = functools.reduce(jnp.maximum, logits)
    raised = [jnp.exp(logit - top) for logit in logits]
    mine = [jnp.where(expert_ref[0] == j, raised[j], 0.0) for j in range(4)]
    share = sum(mine) / sum(raised)
    gate = gate * scale
    active = 0.5 * gate * (1.0 + jnp.tanh(math.sqrt(2 / math.pi) * (gate + 0.044715 * gate**3)))
    units = (active * (lifted * scale) * share)[:, :hidden].astype(BF)
    out = jnp.dot(units, down_ref[...], preferred_element_type=F32).astype(BF)
    tiles = out.shape[1] // LANES
    rows = out_ref.shape[1]
    for t in range(tiles):
        for k in range(PAIRS):
            out_ref[PAIRS * t + k] = out[k * rows : (k + 1) * rows, t * LANES : (t + 1) * LANES]
    for s in range(PAIRS * tiles, out_ref.shape[0]):
        out_ref[s] = jnp.zeros(out_ref.shape[1:], BF)


def rows_kernel(tiles, groups, parts_ref, place_ref, out_ref):
    rows = out_ref.shape[0]
    for t in range(tiles):
        parts = jnp.concatenate([parts_ref[PAIRS * t + k] for k in range(PAIRS)], axis=0)
        placed = jnp.dot(place_ref[...], parts, preferred_element_type=F32)
        for g in range(groups):
            at = (g * tiles + t) * LANES
            out_ref[:, at : at + LANES] = placed[g * rows : (g + 1) * rows].astype(BF)


def per_device(
    encoded,
    key_weight,
    value_weight,
    queries,
    state,
    out_weight,
    norm_gain,
    router,
    expert_ids,
    gate_weight,
    up_weight,
    down_weight,
):
    seq_count = lax.axis_size(SEQ)
    exp_count = lax.axis_size(EXP)
    groups = lax.axis_size("g")
    experts = lax.axis_size("e")
    dec_rows = state.shape[1]
    model_width = state.shape[2]
    block_width = model_width // groups
    tiles = block_width // LANES
    head = key_weight.shape[2]
    hidden_here = gate_weight.shape[2]
    tokens = encoded.shape[1] * seq_count
    my_seq = lax.axis_index(SEQ)
    my_expert = lax.axis_index("e")
    my_group = lax.axis_index("g")

    enc_all = lax.all_gather(encoded[0], SEQ, axis=0, tiled=True)
    first = jnp.concatenate([key_weight[0], value_weight[0]], axis=1)
    second = jnp.concatenate([key_weight[1], value_weight[1]], axis=1)
    own = lax.all_gather(first, "e", axis=0, tiled=True)
    second, own = lax.optimization_barrier((second, own))
    middle = own.shape[0] // 2
    left = shifted(own, exp_count, 1)
    right = shifted(own, exp_count, -1)
    far_left = shifted(left[:middle], exp_count, 1)
    far_right = shifted(right[middle:], exp_count, -1)
    blocks = [own, left, right, far_left, far_right]
    pieces = [
        (0, 0, experts),
        (-1, 0, experts),
        (1, 0, experts),
        (-2, 0, experts // 2),
        (2, experts // 2, experts),
    ]
    second_all = lax.all_gather(second, EXP, axis=0, tiled=True)

    whole = lambda shape: pl.BlockSpec(shape, lambda i, *_: (0,) * len(shape))
    cache_shape = jax.ShapeDtypeStruct((2, tokens, head), BF)
    ordered = pl.pallas_call(
        functools.partial(order_kernel, pieces, groups, experts),
        grid_spec=pltpu.PrefetchScalarGridSpec(
            num_scalar_prefetch=1,
            grid=(1,),
            in_specs=[whole(block.shape) for block in blocks],
            out_specs=whole((model_width, 2 * head)),
        ),
        out_shape=jax.ShapeDtypeStruct((model_width, 2 * head), BF),
        compiler_params=pltpu.CompilerParams(vmem_limit_bytes=24 * 1024 * 1024),
        name="order_weights",
    )(my_group.reshape(1), *blocks)
    flags = jnp.any(
        expert_ids[0][:, :, None] == jnp.arange(experts, dtype=jnp.int32), axis=1
    ).astype(F32).T
    before = jnp.triu(jnp.ones((dec_rows, dec_rows), F32), 1)
    slot = jnp.where(flags > 0.5, jnp.dot(flags, before), -1.0)
    slots = jnp.arange(CAP, dtype=F32).reshape(PAIRS, 1, EACH, 1)
    pick = jnp.where(slot[None, :, None, :] == slots, 1.0, 0.0).astype(BF)
    piece_rows = experts * EACH
    same = jnp.eye(groups, dtype=BF)
    place = pick.reshape(PAIRS, piece_rows, dec_rows).transpose(2, 0, 1)
    place = (same[:, None, None, :, None] * place[None, :, :, None, :]).reshape(
        groups * dec_rows, PAIRS * groups * piece_rows
    )
    pick = pick.reshape(PAIRS * piece_rows, dec_rows)
    pair_shape = (tokens, 2 * head)
    pair, terms = pl.pallas_call(
        functools.partial(attention_kernel, tiles, groups),
        grid=(1,),
        in_specs=[
            whole((dec_rows, head)),
            whole(pick.shape),
            whole(out_weight.shape),
            whole(ordered.shape),
            pl.BlockSpec(memory_space=pltpu.HBM),
        ],
        out_specs=[whole(pair_shape), whole((seq_count, groups * piece_rows, LANES))],
        out_shape=[
            jax.ShapeDtypeStruct(pair_shape, BF),
            jax.ShapeDtypeStruct((seq_count, groups * piece_rows, LANES), BF),
        ],
        scratch_shapes=[
            pltpu.VMEM((tokens, model_width), BF),
            pltpu.VMEM(pair_shape, F32),
            pltpu.SemaphoreType.DMA((CHUNKS,)),
        ],
        compiler_params=pltpu.CompilerParams(vmem_limit_bytes=32 * 1024 * 1024),
        name="attend",
    )(queries[0], pick, out_weight, ordered, enc_all)

    state_parts = jnp.dot(pick, state[0], preferred_element_type=F32)
    state_parts = state_parts.reshape(PAIRS, piece_rows, groups, tiles, LANES)
    state_here = lax.dynamic_index_in_dim(state_parts, my_seq % PAIRS, 0, keepdims=False)
    my_tile = jnp.minimum(my_seq // PAIRS, tiles - 1)
    state_here = lax.dynamic_index_in_dim(state_here, my_tile, 2, keepdims=False).transpose(1, 0, 2)
    got = exchanged(terms, SEQ)
    attended = jnp.sum(got.astype(F32), axis=0).reshape(groups, piece_rows, LANES) + state_here
    routed = exchanged(attended.astype(BF).reshape(exp_count, EACH, LANES), OWNERS)
    rows_all = spread(routed.reshape(exp_count * EACH, LANES), SEQ)
    slot_count = exp_count * CAP
    gain = lax.dynamic_slice_in_dim(norm_gain, my_group * block_width, block_width, 0)
    routes = lax.dynamic_slice_in_dim(router.T, my_group * block_width, block_width, 1)
    gap = jnp.zeros((8 - experts, block_width), BF)
    routes = jnp.concatenate([routes, gap, routes, gap], axis=0)
    routes = jnp.pad(routes, ((0, WIDE - hidden_here - routes.shape[0]), (0, 0)))
    partial = pl.pallas_call(
        functools.partial(expert_input_kernel, hidden_here),
        grid=(1,),
        in_specs=[
            whole(rows_all.shape),
            whole((1, block_width)),
            whole(routes.shape),
            whole((hidden_here, block_width)),
            whole((hidden_here, block_width)),
        ],
        out_specs=whole((slot_count, 2 * WIDE)),
        out_shape=jax.ShapeDtypeStruct((slot_count, 2 * WIDE), BF),
        scratch_shapes=[
            pltpu.VMEM((slot_count, block_width), BF),
            pltpu.VMEM((WIDE, block_width), BF),
            pltpu.VMEM((WIDE, block_width), BF),
        ],
        compiler_params=pltpu.CompilerParams(vmem_limit_bytes=24 * 1024 * 1024),
        name="expert_input",
    )(
        rows_all,
        gain[None],
        routes,
        gate_weight[0].T,
        up_weight[0].T,
    )
    parts = lax.all_gather(partial, "g", axis=0)
    out = pl.pallas_call(
        functools.partial(expert_output_kernel, hidden_here, model_width),
        grid_spec=pltpu.PrefetchScalarGridSpec(
            num_scalar_prefetch=1,
            grid=(1,),
            in_specs=[
                whole(parts.shape),
                whole((hidden_here, block_width)),
            ],
            out_specs=whole(rows_all.shape),
        ),
        out_shape=jax.ShapeDtypeStruct(rows_all.shape, BF),
        compiler_params=pltpu.CompilerParams(vmem_limit_bytes=24 * 1024 * 1024),
        name="expert_output",
    )(my_expert.reshape(1), parts, down_weight[0])
    back = exchanged(out, SEQ)
    back = jnp.sum(back.astype(F32), axis=0).astype(BF)
    back = exchanged(back.reshape(exp_count, EACH, LANES), OWNERS)
    mixed = attended / TOP + back.reshape(groups, piece_rows, LANES).astype(F32)
    mixed = mixed.astype(BF).reshape(groups * piece_rows, LANES)
    mixed, second_all = lax.optimization_barrier((mixed, second_all))
    mixed = spread(mixed, SEQ)
    second_pair = jnp.dot(enc_all, second_all, preferred_element_type=F32).astype(BF)
    key_cache, value_cache = pl.pallas_call(
        store_kernel,
        grid=(1,),
        in_specs=[whole(pair_shape), whole(pair_shape)],
        out_specs=[whole(cache_shape.shape)] * 2,
        out_shape=[cache_shape, cache_shape],
        compiler_params=pltpu.CompilerParams(vmem_limit_bytes=12 * 1024 * 1024),
        name="store_caches",
    )(pair, second_pair)
    mixed, key_cache, value_cache = lax.optimization_barrier((mixed, key_cache, value_cache))
    mixed = pl.pallas_call(
        functools.partial(rows_kernel, tiles, groups),
        grid=(1,),
        in_specs=[whole(mixed.shape), whole(place.shape)],
        out_specs=whole((dec_rows, model_width)),
        out_shape=jax.ShapeDtypeStruct((dec_rows, model_width), BF),
        compiler_params=pltpu.CompilerParams(vmem_limit_bytes=8 * 1024 * 1024),
        name="place_rows",
    )(mixed, place)[None]
    return key_cache[:, None], value_cache[:, None], mixed


def solution(mesh):
    fine = Mesh(mesh.devices.reshape(4, 4, 2, 4, 4), SEQ + EXP)
    return jax.shard_map(
        per_device,
        mesh=fine,
        in_specs=(
            P(EXP, SEQ, None),
            P(None, EXP, SEQ),
            P(None, EXP, SEQ),
            P(EXP, None, SEQ),
            P(EXP, None, None),
            P(SEQ, None),
            P(),
            P(),
            P(EXP, None, None),
            P(EXP, None, SEQ),
            P(EXP, None, SEQ),
            P(EXP, SEQ, None),
        ),
        out_specs=(P(None, EXP, None, SEQ), P(None, EXP, None, SEQ), P(EXP, None, None)),
        check_vma=False,
    )
```

```python
import functools
import math

import jax
import jax.numpy as jnp
from jax import lax
from jax.experimental import pallas as pl
from jax.experimental.pallas import tpu as pltpu
from jax.sharding import Mesh
from jax.sharding import PartitionSpec as P

EPS = 1e-06
SEQ = ("x", "y", "c")
EXP = ("e", "g")
OWNERS = ("g", "e")
LANES = 128
BF = jnp.bfloat16
F32 = jnp.float32
WIDE = 384
CAP = 6
TOP = 2
PAIRS = 3
EACH = CAP // PAIRS


def shifted(x, count, by):
    return lax.ppermute(x, EXP, [(i, (i + by) % count) for i in range(count)])


def exchanged(x, axes):
    return lax.all_to_all(x, axes, split_axis=0, concat_axis=0, tiled=True)


def spread(x, axes):
    count = lax.axis_size(axes)
    return exchanged(jnp.broadcast_to(x[None], (count,) + x.shape), axes)


def order_kernel(pieces, groups, experts, group_ref, *refs):
    blocks, weight_ref = refs[:-1], refs[-1]
    rows = weight_ref.shape[0] // (groups * experts)
    for block, (offset, first, last) in zip(blocks, pieces):
        group = lax.rem(group_ref[0] + (groups + offset), groups)
        for e in range(first, last):
            at = pl.multiple_of((e * groups + group) * rows, 64)
            weight_ref[pl.ds(at, rows), :] = block[(e - first) * rows : (e - first + 1) * rows, :]


def attention_kernel(
    tiles, groups, query_ref, pair_ref, pick_ref, out_ref, key_ref, value_ref, term_ref
):
    head = key_ref.shape[-1]
    key_ref[0] = pair_ref[:, :head]
    value_ref[0] = pair_ref[:, head:]
    scores = lax.dot_general(
        query_ref[...], key_ref[0], (((1,), (1,)), ((), ())), preferred_element_type=F32
    ) / math.sqrt(head)
    raised = jnp.exp(scores - jnp.max(scores, axis=-1, keepdims=True))
    attn = (raised / jnp.sum(raised, axis=-1, keepdims=True)).astype(BF)
    context = jnp.dot(attn, value_ref[0], preferred_element_type=F32).astype(BF)
    context = jnp.dot(pick_ref[...], context, preferred_element_type=F32).astype(BF)
    rows = context.shape[0] // PAIRS
    for t in range(tiles):
        parts = [
            jnp.dot(
                context,
                out_ref[:, (g * tiles + t) * LANES : (g * tiles + t + 1) * LANES],
                preferred_element_type=F32,
            )
            for g in range(groups)
        ]
        for k in range(PAIRS):
            term_ref[PAIRS * t + k] = jnp.concatenate(
                [p[k * rows : (k + 1) * rows] for p in parts], axis=0
            ).astype(BF)
    for s in range(PAIRS * tiles, term_ref.shape[0]):
        term_ref[s] = jnp.zeros(term_ref.shape[1:], BF)


def second_kernel(pair_ref, key_in, value_in, key_ref, value_ref):
    head = key_ref.shape[-1]
    key_ref[0] = pair_ref[:, :head]
    value_ref[0] = pair_ref[:, head:]


def expert_input_kernel(
    hidden, rows_ref, gain_ref, router_ref, gate_ref, up_ref, part_ref, x_ref, gate_all, up_all
):
    tiles = x_ref.shape[1] // LANES
    wide = gate_all.shape[0]
    squares = None
    for t in range(tiles):
        x = jnp.concatenate([rows_ref[PAIRS * t + k] for k in range(PAIRS)], axis=0).astype(F32)
        term = jnp.sum(x * x, axis=1, keepdims=True)
        squares = term if squares is None else squares + term
        gain = gain_ref[:, t * LANES : (t + 1) * LANES]
        x_ref[:, t * LANES : (t + 1) * LANES] = (x * gain).astype(BF)
    gate_all[:hidden] = gate_ref[...]
    gate_all[hidden:] = router_ref[...]
    up_all[:hidden] = up_ref[...]
    up_all[hidden:] = jnp.zeros((wide - hidden, up_all.shape[1]), BF)
    contract = (((1,), (1,)), ((), ()))
    gate = lax.dot_general(x_ref[...], gate_all[...], contract, preferred_element_type=F32)
    lane = lax.broadcasted_iota(jnp.int32, gate.shape, 1)
    gate = jnp.where((lane == hidden + 4) | (lane == hidden + 12), squares, gate)
    high = gate.astype(BF)
    low = (gate - high.astype(F32)).astype(BF)
    part_ref[:, :wide] = jnp.where(lane >= hidden + 8, low.astype(F32), high.astype(F32)).astype(BF)
    up = lax.dot_general(x_ref[...], up_all[...], contract, preferred_element_type=F32)
    part_ref[:, wide:] = up.astype(BF)


def expert_output_kernel(hidden, width, expert_ref, part_ref, down_ref, out_ref):
    total = part_ref[0].astype(F32)
    for k in range(1, part_ref.shape[0]):
        total = total + part_ref[k].astype(F32)
    wide = total.shape[1] // 2
    gate, lifted = total[:, :wide], total[:, wide:]

    def column(j):
        return gate[:, hidden + j : hidden + j + 1] + gate[:, hidden + 8 + j : hidden + 9 + j]

    scale = lax.rsqrt(column(4) / width + EPS)
    logits = [column(j) * scale for j in range(4)]
    top = functools.reduce(jnp.maximum, logits)
    raised = [jnp.exp(logit - top) for logit in logits]
    mine = [jnp.where(expert_ref[0] == j, raised[j], 0.0) for j in range(4)]
    share = sum(mine) / sum(raised)
    gate = gate * scale
    active = 0.5 * gate * (1.0 + jnp.tanh(math.sqrt(2 / math.pi) * (gate + 0.044715 * gate**3)))
    units = (active * (lifted * scale) * share)[:, :hidden].astype(BF)
    out = jnp.dot(units, down_ref[...], preferred_element_type=F32).astype(BF)
    tiles = out.shape[1] // LANES
    rows = out_ref.shape[1]
    for t in range(tiles):
        for k in range(PAIRS):
            out_ref[PAIRS * t + k] = out[k * rows : (k + 1) * rows, t * LANES : (t + 1) * LANES]
    for s in range(PAIRS * tiles, out_ref.shape[0]):
        out_ref[s] = jnp.zeros(out_ref.shape[1:], BF)


def rows_kernel(tiles, groups, parts_ref, place_ref, out_ref):
    rows = out_ref.shape[0]
    for t in range(tiles):
        parts = jnp.concatenate([parts_ref[PAIRS * t + k] for k in range(PAIRS)], axis=0)
        placed = jnp.dot(place_ref[...], parts, preferred_element_type=F32)
        for g in range(groups):
            at = (g * tiles + t) * LANES
            out_ref[:, at : at + LANES] = placed[g * rows : (g + 1) * rows].astype(BF)


def per_device(
    encoded,
    key_weight,
    value_weight,
    queries,
    state,
    out_weight,
    norm_gain,
    router,
    expert_ids,
    gate_weight,
    up_weight,
    down_weight,
):
    seq_count = lax.axis_size(SEQ)
    exp_count = lax.axis_size(EXP)
    groups = lax.axis_size("g")
    experts = lax.axis_size("e")
    dec_rows = state.shape[1]
    model_width = state.shape[2]
    block_width = model_width // groups
    tiles = block_width // LANES
    head = key_weight.shape[2]
    hidden_here = gate_weight.shape[2]
    tokens = encoded.shape[1] * seq_count
    my_seq = lax.axis_index(SEQ)
    my_expert = lax.axis_index("e")
    my_group = lax.axis_index("g")

    enc_all = lax.all_gather(encoded[0], SEQ, axis=0, tiled=True)
    first = jnp.concatenate([key_weight[0], value_weight[0]], axis=1)
    second = jnp.concatenate([key_weight[1], value_weight[1]], axis=1)
    own = lax.all_gather(first, "e", axis=0, tiled=True)
    middle = own.shape[0] // 2
    left = shifted(own, exp_count, 1)
    right = shifted(own, exp_count, -1)
    far_left = shifted(left[:middle], exp_count, 1)
    far_right = shifted(right[middle:], exp_count, -1)
    blocks = [own, left, right, far_left, far_right]
    pieces = [
        (0, 0, experts),
        (-1, 0, experts),
        (1, 0, experts),
        (-2, 0, experts // 2),
        (2, experts // 2, experts),
    ]

    whole = lambda shape: pl.BlockSpec(shape, lambda i, *_: (0,) * len(shape))
    cache_shape = jax.ShapeDtypeStruct((2, tokens, head), BF)
    ordered = pl.pallas_call(
        functools.partial(order_kernel, pieces, groups, experts),
        grid_spec=pltpu.PrefetchScalarGridSpec(
            num_scalar_prefetch=1,
            grid=(1,),
            in_specs=[whole(block.shape) for block in blocks],
            out_specs=whole((model_width, 2 * head)),
        ),
        out_shape=jax.ShapeDtypeStruct((model_width, 2 * head), BF),
        compiler_params=pltpu.CompilerParams(vmem_limit_bytes=24 * 1024 * 1024),
        name="order_weights",
    )(my_group.reshape(1), *blocks)
    pair = jnp.dot(enc_all, ordered, preferred_element_type=F32).astype(BF)
    second, pair = lax.optimization_barrier((second, pair))
    second_all = lax.all_gather(second, EXP, axis=0, tiled=True)
    flags = jnp.any(
        expert_ids[0][:, :, None] == jnp.arange(experts, dtype=jnp.int32), axis=1
    ).astype(F32).T
    before = jnp.triu(jnp.ones((dec_rows, dec_rows), F32), 1)
    slot = jnp.where(flags > 0.5, jnp.dot(flags, before), -1.0)
    slots = jnp.arange(CAP, dtype=F32).reshape(PAIRS, 1, EACH, 1)
    pick = jnp.where(slot[None, :, None, :] == slots, 1.0, 0.0).astype(BF)
    piece_rows = experts * EACH
    same = jnp.eye(groups, dtype=BF)
    place = pick.reshape(PAIRS, piece_rows, dec_rows).transpose(2, 0, 1)
    place = (same[:, None, None, :, None] * place[None, :, :, None, :]).reshape(
        groups * dec_rows, PAIRS * groups * piece_rows
    )
    pick = pick.reshape(PAIRS * piece_rows, dec_rows)
    key_cache, value_cache, terms = pl.pallas_call(
        functools.partial(attention_kernel, tiles, groups),
        grid=(1,),
        in_specs=[
            whole((dec_rows, head)),
            whole(pair.shape),
            whole(pick.shape),
            whole(out_weight.shape),
        ],
        out_specs=[
            pl.BlockSpec((1, tokens, head), lambda i: (0, 0, 0)),
            pl.BlockSpec((1, tokens, head), lambda i: (0, 0, 0)),
            whole((seq_count, groups * piece_rows, LANES)),
        ],
        out_shape=[
            cache_shape,
            cache_shape,
            jax.ShapeDtypeStruct((seq_count, groups * piece_rows, LANES), BF),
        ],
        compiler_params=pltpu.CompilerParams(vmem_limit_bytes=16 * 1024 * 1024),
        name="attend",
    )(queries[0], pair, pick, out_weight)

    state_parts = jnp.dot(pick, state[0], preferred_element_type=F32)
    state_parts = state_parts.reshape(PAIRS, piece_rows, groups, tiles, LANES)
    state_here = lax.dynamic_index_in_dim(state_parts, my_seq % PAIRS, 0, keepdims=False)
    my_tile = jnp.minimum(my_seq // PAIRS, tiles - 1)
    state_here = lax.dynamic_index_in_dim(state_here, my_tile, 2, keepdims=False).transpose(1, 0, 2)
    got = exchanged(terms, SEQ)
    attended = jnp.sum(got.astype(F32), axis=0).reshape(groups, piece_rows, LANES) + state_here
    routed = exchanged(attended.astype(BF).reshape(exp_count, EACH, LANES), OWNERS)
    rows_all = spread(routed.reshape(exp_count * EACH, LANES), SEQ)
    slot_count = exp_count * CAP
    gain = lax.dynamic_slice_in_dim(norm_gain, my_group * block_width, block_width, 0)
    routes = lax.dynamic_slice_in_dim(router.T, my_group * block_width, block_width, 1)
    gap = jnp.zeros((8 - experts, block_width), BF)
    routes = jnp.concatenate([routes, gap, routes, gap], axis=0)
    routes = jnp.pad(routes, ((0, WIDE - hidden_here - routes.shape[0]), (0, 0)))
    partial = pl.pallas_call(
        functools.partial(expert_input_kernel, hidden_here),
        grid=(1,),
        in_specs=[
            whole(rows_all.shape),
            whole((1, block_width)),
            whole(routes.shape),
            whole((hidden_here, block_width)),
            whole((hidden_here, block_width)),
        ],
        out_specs=whole((slot_count, 2 * WIDE)),
        out_shape=jax.ShapeDtypeStruct((slot_count, 2 * WIDE), BF),
        scratch_shapes=[
            pltpu.VMEM((slot_count, block_width), BF),
            pltpu.VMEM((WIDE, block_width), BF),
            pltpu.VMEM((WIDE, block_width), BF),
        ],
        compiler_params=pltpu.CompilerParams(vmem_limit_bytes=24 * 1024 * 1024),
        name="expert_input",
    )(
        rows_all,
        gain[None],
        routes,
        gate_weight[0].T,
        up_weight[0].T,
    )
    parts = lax.all_gather(partial, "g", axis=0)
    out = pl.pallas_call(
        functools.partial(expert_output_kernel, hidden_here, model_width),
        grid_spec=pltpu.PrefetchScalarGridSpec(
            num_scalar_prefetch=1,
            grid=(1,),
            in_specs=[
                whole(parts.shape),
                whole((hidden_here, block_width)),
            ],
            out_specs=whole(rows_all.shape),
        ),
        out_shape=jax.ShapeDtypeStruct(rows_all.shape, BF),
        compiler_params=pltpu.CompilerParams(vmem_limit_bytes=24 * 1024 * 1024),
        name="expert_output",
    )(my_expert.reshape(1), parts, down_weight[0])
    back = exchanged(out, SEQ)
    back = jnp.sum(back.astype(F32), axis=0).astype(BF)
    back = exchanged(back.reshape(exp_count, EACH, LANES), OWNERS)
    mixed = attended / TOP + back.reshape(groups, piece_rows, LANES).astype(F32)
    mixed = mixed.astype(BF).reshape(groups * piece_rows, LANES)
    mixed, second_all = lax.optimization_barrier((mixed, second_all))
    mixed = spread(mixed, SEQ)
    second_pair = jnp.dot(enc_all, second_all, preferred_element_type=F32).astype(BF)
    key_cache, value_cache = pl.pallas_call(
        second_kernel,
        grid=(1,),
        in_specs=[
            pl.BlockSpec(second_pair.shape, lambda i: (0, 0)),
            pl.BlockSpec(memory_space=pl.ANY),
            pl.BlockSpec(memory_space=pl.ANY),
        ],
        out_specs=[pl.BlockSpec((1, tokens, head), lambda i: (1, 0, 0))] * 2,
        out_shape=[cache_shape, cache_shape],
        input_output_aliases={1: 0, 2: 1},
        compiler_params=pltpu.CompilerParams(vmem_limit_bytes=8 * 1024 * 1024),
        name="store_second",
    )(second_pair, key_cache, value_cache)
    mixed, key_cache, value_cache = lax.optimization_barrier((mixed, key_cache, value_cache))
    mixed = pl.pallas_call(
        functools.partial(rows_kernel, tiles, groups),
        grid=(1,),
        in_specs=[whole(mixed.shape), whole(place.shape)],
        out_specs=whole((dec_rows, model_width)),
        out_shape=jax.ShapeDtypeStruct((dec_rows, model_width), BF),
        compiler_params=pltpu.CompilerParams(vmem_limit_bytes=8 * 1024 * 1024),
        name="place_rows",
    )(mixed, place)[None]
    return key_cache[:, None], value_cache[:, None], mixed


def solution(mesh):
    fine = Mesh(mesh.devices.reshape(4, 4, 2, 4, 4), SEQ + EXP)
    return jax.shard_map(
        per_device,
        mesh=fine,
        in_specs=(
            P(EXP, SEQ, None),
            P(None, EXP, SEQ),
            P(None, EXP, SEQ),
            P(EXP, None, SEQ),
            P(EXP, None, None),
            P(SEQ, None),
            P(),
            P(),
            P(EXP, None, None),
            P(EXP, None, SEQ),
            P(EXP, None, SEQ),
            P(EXP, SEQ, None),
        ),
        out_specs=(P(None, EXP, None, SEQ), P(None, EXP, None, SEQ), P(EXP, None, None)),
        check_vma=False,
    )
```

```python
import functools
import math

import jax
import jax.numpy as jnp
from jax import lax
from jax.experimental import pallas as pl
from jax.experimental.pallas import tpu as pltpu
from jax.sharding import Mesh
from jax.sharding import PartitionSpec as P

EPS = 1e-06
SEQ = ("x", "y", "c")
EXP = ("e", "g")
OWNERS = ("g", "e")
LANES = 128
BF = jnp.bfloat16
F32 = jnp.float32
WIDE = 384
CAP = 6
TOP = 2
PAIRS = 3
EACH = CAP // PAIRS


def shifted(x, count, by):
    return lax.ppermute(x, EXP, [(i, (i + by) % count) for i in range(count)])


def exchanged(x, axes):
    return lax.all_to_all(x, axes, split_axis=0, concat_axis=0, tiled=True)


def spread(x, axes):
    count = lax.axis_size(axes)
    return exchanged(jnp.broadcast_to(x[None], (count,) + x.shape), axes)


def order_kernel(pieces, groups, experts, group_ref, *refs):
    blocks, weight_ref = refs[:-1], refs[-1]
    rows = weight_ref.shape[0] // (groups * experts)
    for block, (offset, first, last) in zip(blocks, pieces):
        group = lax.rem(group_ref[0] + (groups + offset), groups)
        for e in range(first, last):
            at = pl.multiple_of((e * groups + group) * rows, 64)
            weight_ref[pl.ds(at, rows), :] = block[(e - first) * rows : (e - first + 1) * rows, :]


def attention_kernel(
    tiles, groups, query_ref, pair_ref, pick_ref, out_ref, key_ref, value_ref, term_ref
):
    head = key_ref.shape[-1]
    key_ref[0] = pair_ref[:, :head]
    value_ref[0] = pair_ref[:, head:]
    scores = lax.dot_general(
        query_ref[...], key_ref[0], (((1,), (1,)), ((), ())), preferred_element_type=F32
    ) / math.sqrt(head)
    raised = jnp.exp(scores - jnp.max(scores, axis=-1, keepdims=True))
    attn = (raised / jnp.sum(raised, axis=-1, keepdims=True)).astype(BF)
    context = jnp.dot(attn, value_ref[0], preferred_element_type=F32).astype(BF)
    context = jnp.dot(pick_ref[...], context, preferred_element_type=F32).astype(BF)
    rows = context.shape[0] // PAIRS
    for t in range(tiles):
        parts = [
            jnp.dot(
                context,
                out_ref[:, (g * tiles + t) * LANES : (g * tiles + t + 1) * LANES],
                preferred_element_type=F32,
            )
            for g in range(groups)
        ]
        for k in range(PAIRS):
            term_ref[PAIRS * t + k] = jnp.concatenate(
                [p[k * rows : (k + 1) * rows] for p in parts], axis=0
            ).astype(BF)
    for s in range(PAIRS * tiles, term_ref.shape[0]):
        term_ref[s] = jnp.zeros(term_ref.shape[1:], BF)


def second_kernel(pair_ref, key_in, value_in, key_ref, value_ref):
    head = key_ref.shape[-1]
    key_ref[0] = pair_ref[:, :head]
    value_ref[0] = pair_ref[:, head:]


def expert_input_kernel(
    hidden, rows_ref, gain_ref, router_ref, gate_ref, up_ref, part_ref, x_ref, gate_all, up_all
):
    tiles = x_ref.shape[1] // LANES
    wide = gate_all.shape[0]
    squares = None
    for t in range(tiles):
        x = jnp.concatenate([rows_ref[PAIRS * t + k] for k in range(PAIRS)], axis=0).astype(F32)
        term = jnp.sum(x * x, axis=1, keepdims=True)
        squares = term if squares is None else squares + term
        gain = gain_ref[:, t * LANES : (t + 1) * LANES]
        x_ref[:, t * LANES : (t + 1) * LANES] = (x * gain).astype(BF)
    gate_all[:hidden] = gate_ref[...]
    gate_all[hidden:] = router_ref[...]
    up_all[:hidden] = up_ref[...]
    up_all[hidden:] = jnp.zeros((wide - hidden, up_all.shape[1]), BF)
    contract = (((1,), (1,)), ((), ()))
    gate = lax.dot_general(x_ref[...], gate_all[...], contract, preferred_element_type=F32)
    lane = lax.broadcasted_iota(jnp.int32, gate.shape, 1)
    gate = jnp.where((lane == hidden + 4) | (lane == hidden + 12), squares, gate)
    high = gate.astype(BF)
    low = (gate - high.astype(F32)).astype(BF)
    part_ref[:, :wide] = jnp.where(lane >= hidden + 8, low.astype(F32), high.astype(F32)).astype(BF)
    up = lax.dot_general(x_ref[...], up_all[...], contract, preferred_element_type=F32)
    part_ref[:, wide:] = up.astype(BF)


def expert_output_kernel(hidden, width, expert_ref, part_ref, down_ref, out_ref):
    total = part_ref[0].astype(F32)
    for k in range(1, part_ref.shape[0]):
        total = total + part_ref[k].astype(F32)
    wide = total.shape[1] // 2
    gate, lifted = total[:, :wide], total[:, wide:]

    def column(j):
        return gate[:, hidden + j : hidden + j + 1] + gate[:, hidden + 8 + j : hidden + 9 + j]

    scale = lax.rsqrt(column(4) / width + EPS)
    logits = [column(j) * scale for j in range(4)]
    top = functools.reduce(jnp.maximum, logits)
    raised = [jnp.exp(logit - top) for logit in logits]
    mine = [jnp.where(expert_ref[0] == j, raised[j], 0.0) for j in range(4)]
    share = sum(mine) / sum(raised)
    gate = gate * scale
    active = 0.5 * gate * (1.0 + jnp.tanh(math.sqrt(2 / math.pi) * (gate + 0.044715 * gate**3)))
    units = (active * (lifted * scale) * share)[:, :hidden].astype(BF)
    out = jnp.dot(units, down_ref[...], preferred_element_type=F32).astype(BF)
    tiles = out.shape[1] // LANES
    rows = out_ref.shape[1]
    for t in range(tiles):
        for k in range(PAIRS):
            out_ref[PAIRS * t + k] = out[k * rows : (k + 1) * rows, t * LANES : (t + 1) * LANES]
    for s in range(PAIRS * tiles, out_ref.shape[0]):
        out_ref[s] = jnp.zeros(out_ref.shape[1:], BF)


def rows_kernel(tiles, groups, parts_ref, place_ref, out_ref):
    rows = out_ref.shape[0]
    for t in range(tiles):
        parts = jnp.concatenate([parts_ref[PAIRS * t + k] for k in range(PAIRS)], axis=0)
        placed = jnp.dot(place_ref[...], parts, preferred_element_type=F32)
        for g in range(groups):
            at = (g * tiles + t) * LANES
            out_ref[:, at : at + LANES] = placed[g * rows : (g + 1) * rows].astype(BF)


def per_device(
    encoded,
    key_weight,
    value_weight,
    queries,
    state,
    out_weight,
    norm_gain,
    router,
    expert_ids,
    gate_weight,
    up_weight,
    down_weight,
):
    seq_count = lax.axis_size(SEQ)
    exp_count = lax.axis_size(EXP)
    groups = lax.axis_size("g")
    experts = lax.axis_size("e")
    dec_rows = state.shape[1]
    model_width = state.shape[2]
    block_width = model_width // groups
    tiles = block_width // LANES
    head = key_weight.shape[2]
    hidden_here = gate_weight.shape[2]
    tokens = encoded.shape[1] * seq_count
    my_seq = lax.axis_index(SEQ)
    my_expert = lax.axis_index("e")
    my_group = lax.axis_index("g")

    enc_all = lax.all_gather(encoded[0], SEQ, axis=0, tiled=True)
    first = jnp.concatenate([key_weight[0], value_weight[0]], axis=1)
    own = lax.all_gather(first, "e", axis=0, tiled=True)
    later_key, later_value, own = lax.optimization_barrier((key_weight[1], value_weight[1], own))
    second = jnp.concatenate([later_key, later_value], axis=1)
    middle = own.shape[0] // 2
    left = shifted(own, exp_count, 1)
    right = shifted(own, exp_count, -1)
    far_left = shifted(left[:middle], exp_count, 1)
    far_right = shifted(right[middle:], exp_count, -1)
    blocks = [own, left, right, far_left, far_right]
    pieces = [
        (0, 0, experts),
        (-1, 0, experts),
        (1, 0, experts),
        (-2, 0, experts // 2),
        (2, experts // 2, experts),
    ]
    second_all = lax.all_gather(second, EXP, axis=0, tiled=True)

    whole = lambda shape: pl.BlockSpec(shape, lambda i, *_: (0,) * len(shape))
    cache_shape = jax.ShapeDtypeStruct((2, tokens, head), BF)
    ordered = pl.pallas_call(
        functools.partial(order_kernel, pieces, groups, experts),
        grid_spec=pltpu.PrefetchScalarGridSpec(
            num_scalar_prefetch=1,
            grid=(1,),
            in_specs=[whole(block.shape) for block in blocks],
            out_specs=whole((model_width, 2 * head)),
        ),
        out_shape=jax.ShapeDtypeStruct((model_width, 2 * head), BF),
        compiler_params=pltpu.CompilerParams(vmem_limit_bytes=24 * 1024 * 1024),
        name="order_weights",
    )(my_group.reshape(1), *blocks)
    pair = jnp.dot(enc_all, ordered, preferred_element_type=F32).astype(BF)
    flags = jnp.any(
        expert_ids[0][:, :, None] == jnp.arange(experts, dtype=jnp.int32), axis=1
    ).astype(F32).T
    before = jnp.triu(jnp.ones((dec_rows, dec_rows), F32), 1)
    slot = jnp.where(flags > 0.5, jnp.dot(flags, before), -1.0)
    slots = jnp.arange(CAP, dtype=F32).reshape(PAIRS, 1, EACH, 1)
    pick = jnp.where(slot[None, :, None, :] == slots, 1.0, 0.0).astype(BF)
    piece_rows = experts * EACH
    same = jnp.eye(groups, dtype=BF)
    place = pick.reshape(PAIRS, piece_rows, dec_rows).transpose(2, 0, 1)
    place = (same[:, None, None, :, None] * place[None, :, :, None, :]).reshape(
        groups * dec_rows, PAIRS * groups * piece_rows
    )
    pick = pick.reshape(PAIRS * piece_rows, dec_rows)
    key_cache, value_cache, terms = pl.pallas_call(
        functools.partial(attention_kernel, tiles, groups),
        grid=(1,),
        in_specs=[
            whole((dec_rows, head)),
            whole(pair.shape),
            whole(pick.shape),
            whole(out_weight.shape),
        ],
        out_specs=[
            pl.BlockSpec((1, tokens, head), lambda i: (0, 0, 0)),
            pl.BlockSpec((1, tokens, head), lambda i: (0, 0, 0)),
            whole((seq_count, groups * piece_rows, LANES)),
        ],
        out_shape=[
            cache_shape,
            cache_shape,
            jax.ShapeDtypeStruct((seq_count, groups * piece_rows, LANES), BF),
        ],
        compiler_params=pltpu.CompilerParams(vmem_limit_bytes=16 * 1024 * 1024),
        name="attend",
    )(queries[0], pair, pick, out_weight)

    state_parts = jnp.dot(pick, state[0], preferred_element_type=F32)
    state_parts = state_parts.reshape(PAIRS, piece_rows, groups, tiles, LANES)
    state_here = lax.dynamic_index_in_dim(state_parts, my_seq % PAIRS, 0, keepdims=False)
    my_tile = jnp.minimum(my_seq // PAIRS, tiles - 1)
    state_here = lax.dynamic_index_in_dim(state_here, my_tile, 2, keepdims=False).transpose(1, 0, 2)
    got = exchanged(terms, SEQ)
    attended = jnp.sum(got.astype(F32), axis=0).reshape(groups, piece_rows, LANES) + state_here
    routed = exchanged(attended.astype(BF).reshape(exp_count, EACH, LANES), OWNERS)
    rows_all = spread(routed.reshape(exp_count * EACH, LANES), SEQ)
    slot_count = exp_count * CAP
    gain = lax.dynamic_slice_in_dim(norm_gain, my_group * block_width, block_width, 0)
    routes = lax.dynamic_slice_in_dim(router.T, my_group * block_width, block_width, 1)
    gap = jnp.zeros((8 - experts, block_width), BF)
    routes = jnp.concatenate([routes, gap, routes, gap], axis=0)
    routes = jnp.pad(routes, ((0, WIDE - hidden_here - routes.shape[0]), (0, 0)))
    partial = pl.pallas_call(
        functools.partial(expert_input_kernel, hidden_here),
        grid=(1,),
        in_specs=[
            whole(rows_all.shape),
            whole((1, block_width)),
            whole(routes.shape),
            whole((hidden_here, block_width)),
            whole((hidden_here, block_width)),
        ],
        out_specs=whole((slot_count, 2 * WIDE)),
        out_shape=jax.ShapeDtypeStruct((slot_count, 2 * WIDE), BF),
        scratch_shapes=[
            pltpu.VMEM((slot_count, block_width), BF),
            pltpu.VMEM((WIDE, block_width), BF),
            pltpu.VMEM((WIDE, block_width), BF),
        ],
        compiler_params=pltpu.CompilerParams(vmem_limit_bytes=24 * 1024 * 1024),
        name="expert_input",
    )(
        rows_all,
        gain[None],
        routes,
        gate_weight[0].T,
        up_weight[0].T,
    )
    parts = lax.all_gather(partial, "g", axis=0)
    out = pl.pallas_call(
        functools.partial(expert_output_kernel, hidden_here, model_width),
        grid_spec=pltpu.PrefetchScalarGridSpec(
            num_scalar_prefetch=1,
            grid=(1,),
            in_specs=[
                whole(parts.shape),
                whole((hidden_here, block_width)),
            ],
            out_specs=whole(rows_all.shape),
        ),
        out_shape=jax.ShapeDtypeStruct(rows_all.shape, BF),
        compiler_params=pltpu.CompilerParams(vmem_limit_bytes=24 * 1024 * 1024),
        name="expert_output",
    )(my_expert.reshape(1), parts, down_weight[0])
    back = exchanged(out, SEQ)
    back = jnp.sum(back.astype(F32), axis=0).astype(BF)
    back = exchanged(back.reshape(exp_count, EACH, LANES), OWNERS)
    mixed = attended / TOP + back.reshape(groups, piece_rows, LANES).astype(F32)
    mixed = mixed.astype(BF).reshape(groups * piece_rows, LANES)
    mixed, second_all = lax.optimization_barrier((mixed, second_all))
    mixed = spread(mixed, SEQ)
    second_pair = jnp.dot(enc_all, second_all, preferred_element_type=F32).astype(BF)
    key_cache, value_cache = pl.pallas_call(
        second_kernel,
        grid=(1,),
        in_specs=[
            pl.BlockSpec(second_pair.shape, lambda i: (0, 0)),
            pl.BlockSpec(memory_space=pl.ANY),
            pl.BlockSpec(memory_space=pl.ANY),
        ],
        out_specs=[pl.BlockSpec((1, tokens, head), lambda i: (1, 0, 0))] * 2,
        out_shape=[cache_shape, cache_shape],
        input_output_aliases={1: 0, 2: 1},
        compiler_params=pltpu.CompilerParams(vmem_limit_bytes=8 * 1024 * 1024),
        name="store_second",
    )(second_pair, key_cache, value_cache)
    mixed, key_cache, value_cache = lax.optimization_barrier((mixed, key_cache, value_cache))
    mixed = pl.pallas_call(
        functools.partial(rows_kernel, tiles, groups),
        grid=(1,),
        in_specs=[whole(mixed.shape), whole(place.shape)],
        out_specs=whole((dec_rows, model_width)),
        out_shape=jax.ShapeDtypeStruct((dec_rows, model_width), BF),
        compiler_params=pltpu.CompilerParams(vmem_limit_bytes=8 * 1024 * 1024),
        name="place_rows",
    )(mixed, place)[None]
    return key_cache[:, None], value_cache[:, None], mixed


def solution(mesh):
    fine = Mesh(mesh.devices.reshape(4, 4, 2, 4, 4), SEQ + EXP)
    return jax.shard_map(
        per_device,
        mesh=fine,
        in_specs=(
            P(EXP, SEQ, None),
            P(None, EXP, SEQ),
            P(None, EXP, SEQ),
            P(EXP, None, SEQ),
            P(EXP, None, None),
            P(SEQ, None),
            P(),
            P(),
            P(EXP, None, None),
            P(EXP, None, SEQ),
            P(EXP, None, SEQ),
            P(EXP, SEQ, None),
        ),
        out_specs=(P(None, EXP, None, SEQ), P(None, EXP, None, SEQ), P(EXP, None, None)),
        check_vma=False,
    )
```
